32 devices in a mesh: dp: 8 (over y, x, core), rep: 4 (over z).
Axes of the slice: x: 2, y: 2, z: 4, core: 2. Of those that a mesh axis runs over, the one named last changes fastest.
Arguments:
- tokens: bfloat16 [32, 1024, 768], P(('dp', 'rep')), may hold values from -6 to 6
- seg_lens: int32 [32, 5], P(('dp', 'rep')), may hold values from 1 to 512, 1024 in all within a row
- cotangent: float32 [32, 1024, 768], P(('dp', 'rep')), may hold values from -6 to 6
- qkv_w: float32 [3, 768, 768], P(None, 'dp'), may hold values from -0.21875 to 0.21875
- out_w: float32 [768, 768], P('dp'), may hold values from -1.25 to 1.25
- gu_w: float32 [2, 768, 2048], P(None, 'dp'), may hold values from -0.21875 to 0.21875
- down_w: float32 [2048, 768], P('dp'), may hold values from -0.25 to 0.25
- gains: float32 [2, 768], P(None, 'dp'), may hold values from 0.5 to 1.5
- qkv_m: float32 [3, 768, 768], P(None, 'dp'), may hold values from -128 to 128
- qkv_v: float32 [3, 768, 768], P(None, 'dp'), may hold values from 851.968 to 6881.28
- out_m: float32 [768, 768], P('dp'), may hold values from -32 to 32
- out_v: float32 [768, 768], P('dp'), may hold values from 75.3664 to 622.592
- gu_m: float32 [2, 768, 2048], P(None, 'dp'), may hold values from -96 to 96
- gu_v: float32 [2, 768, 2048], P(None, 'dp'), may hold values from 557.056 to 4259.84
- down_m: float32 [2048, 768], P('dp'), may hold values from -96 to 96
- down_v: float32 [2048, 768], P('dp'), may hold values from 557.056 to 4259.84
- gain_m: float32 [2, 768], P(None, 'dp'), may hold values from -256 to 256
- gain_v: float32 [2, 768], P(None, 'dp'), may hold values from 3276.8 to 27525.12
Outputs:
- output: float32 [32, 1024, 768], P(('dp', 'rep'))
- input_grad: float32 [32, 1024, 768], P(('dp', 'rep'))
- qkv_moment: float32 [3, 768, 768], P(None, 'dp')
- qkv_second: float32 [3, 768, 768], P(None, 'dp')
- qkv_new: float32 [3, 768, 768], P(None, 'dp')
- out_moment: float32 [768, 768], P('dp')
- out_second: float32 [768, 768], P('dp')
- out_new: float32 [768, 768], P('dp')
- gu_moment: float32 [2, 768, 2048], P(None, 'dp')
- gu_second: float32 [2, 768, 2048], P(None, 'dp')
- gu_new: float32 [2, 768, 2048], P(None, 'dp')
- down_moment: float32 [2048, 768], P('dp')
- down_second: float32 [2048, 768], P('dp')
- down_new: float32 [2048, 768], P('dp')
- gain_moment: float32 [2, 768], P(None, 'dp')
- gain_second: float32 [2, 768], P(None, 'dp')
- gain_new: float32 [2, 768], P(None, 'dp')
The draws below stay inside these ranges and needn't reach their ends.
Inputs may be any that keep to these rules, and one draw needn't show every extreme that they name: `seg_lens`: each row's 5 lengths are consecutive segments that fill its 1024 slots; the last one is padding; in every draw some segment has exactly 512 slots.
All inputs are finite; a program needn't handle non-finite values.
Results may differ from the reference program's by a relative error of at most 0.014.
The reference program's roundings to bfloat16 on the way count: a program that leaves them out, or rounds other values in their place, can miss the bound.
Values may be sent and summed in bfloat16 or wider, within the bound.
A program may use at most 320 MiB of HBM per device.

```python
import math
import jax
import jax.numpy as jnp
import numpy as np
from jax import lax

D = 768
HEADS = 12
HD = 64
FF = 2048
SEQ = 1024
NSEG = 5
STEP = 10
MOST = 512
ROWS = 32
TOKENS = 32768


def level_of(rng, extent, cuts, low, high):
    def one(position, blocks):
        steps = jax.random.uniform(jax.random.fold_in(jax.random.fold_in(rng, 6), position), (blocks,), jnp.float32, low / len(cuts), high / len(cuts))
        return jnp.repeat(jnp.exp(steps), extent[position] // blocks).reshape((-1,) + (1,) * (len(extent) - position - 1))

    factor_of = one(*cuts[0])
    for cut in cuts[1:]:
        factor_of = factor_of * one(*cut)
    return factor_of


def length_profile(count, total, limit, slope):
    loads = [(1 << 20) // math.isqrt(grade ** slope) + 1 for grade in range(2, count + 1)]
    surplus, counts = total - limit - (count - 1), [1] * (count - 1)
    while surplus > 0:
        candidates = [i for i in range(count - 1) if counts[i] < limit]
        pool, budget = sum([loads[i] for i in candidates]), surplus
        for i in candidates:
            addition = min(limit - counts[i], max(1, budget * loads[i] // pool), surplus)
            counts[i] = counts[i] + addition
            surplus = surplus - addition
    return np.array([limit] + counts)


def uneven_parts(key, number_of, total, limit, lean):
    if number_of == 2:
        one = jax.random.randint(key, (), max(1, total - limit), min(limit, total - 1) + 1)
        return jnp.stack([one, total - one])
    sizes = jnp.asarray(length_profile(number_of, total, limit, lean), jnp.int32)
    twos = (number_of - 1) // 2
    source_of, receiver = sizes[1:1 + 2 * twos:2], sizes[2:2 + 2 * twos:2]
    room = jnp.minimum(source_of - 1, limit - receiver)
    passed = jax.random.randint(jax.random.fold_in(key, 1), (twos,), 0, 1 << 20) % (room + 1)
    sizes = sizes.at[1:1 + 2 * twos:2].set(source_of - passed).at[2:2 + 2 * twos:2].set(receiver + passed)
    return sizes[jax.random.permutation(jax.random.fold_in(key, 2), number_of)]


def noise(key, dims, width, most, shards=(), kind=jnp.bfloat16):
    gain = level_of(key, dims, shards, -0.22, 0.18) if shards else 1.0
    drawn = jax.random.normal(key, dims, jnp.float32) * width * gain
    return jnp.minimum(jnp.maximum(drawn, -most), most).astype(kind)


def setup_inputs(seed: int = 0) -> dict:
    arg_keys = jax.random.split(jax.random.key(seed), 19)
    tokens = noise(arg_keys[0], (ROWS, SEQ, D), 1.0, 6.0, ((0, 32),))
    seg_lens = jax.vmap(lambda own: uneven_parts(own, NSEG, SEQ, MOST, 2))(jax.random.split(arg_keys[1], ROWS)).reshape((ROWS, NSEG)).astype(jnp.int32)
    cotangent = noise(arg_keys[2], (ROWS, SEQ, D), 1.0, 6.0, ((0, 32),), jnp.float32)
    qkv_w = noise(arg_keys[3], (3, D, D), D ** -0.5, 0.21875, ((1, 8),), jnp.float32)
    out_w = noise(arg_keys[4], (D, D), (D // 32) ** -0.5, 1.25, ((0, 8),), jnp.float32)
    gu_w = noise(arg_keys[5], (2, D, FF), D ** -0.5, 0.21875, ((1, 8),), jnp.float32)
    down_w = noise(arg_keys[6], (FF, D), (FF // 4) ** -0.5, 0.25, ((0, 8),), jnp.float32)
    gains = jnp.clip(1.0 + 0.1 * jax.random.normal(arg_keys[7], (2, D), jnp.float32), 0.5, 1.5)
    qkv_m = noise(arg_keys[8], (3, D, D), (0.11 * TOKENS ** 0.5), 128.0, ((1, 8),), jnp.float32)
    qkv_v = jnp.clip(jnp.exp(math.log(6881.28) - 2.089011 * jax.random.uniform(arg_keys[9], (3, D, D), jnp.float32) ** level_of(arg_keys[9], (3, D, D), ((1, 8),), -0.2, 0.2)), 851.968, 6881.28)
    out_m = noise(arg_keys[10], (D, D), (0.033 * TOKENS ** 0.5), 32.0, ((0, 8),), jnp.float32)
    out_v = jnp.clip(jnp.exp(math.log(622.592) - 2.1115298 * jax.random.uniform(arg_keys[11], (D, D), jnp.float32) ** level_of(arg_keys[11], (D, D), ((0, 8),), -0.2, 0.2)), 75.3664, 622.592)
    gu_m = noise(arg_keys[12], (2, D, FF), (0.09 * TOKENS ** 0.5), 96.0, ((1, 8),), jnp.float32)
    gu_v = jnp.clip(jnp.exp(math.log(4259.84) - 2.034321 * jax.random.uniform(arg_keys[13], (2, D, FF), jnp.float32) ** level_of(arg_keys[13], (2, D, FF), ((1, 8),), -0.2, 0.2)), 557.056, 4259.84)
    down_m = noise(arg_keys[14], (FF, D), (0.09 * TOKENS ** 0.5), 96.0, ((0, 8),), jnp.float32)
    down_v = jnp.clip(jnp.exp(math.log(4259.84) - 2.034321 * jax.random.uniform(arg_keys[15], (FF, D), jnp.float32) ** level_of(arg_keys[15], (FF, D), ((0, 8),), -0.2, 0.2)), 557.056, 4259.84)
    gain_m = noise(arg_keys[16], (2, D), (0.22 * TOKENS ** 0.5), 256.0, ((1, 8),), jnp.float32)
    gain_v = jnp.clip(jnp.exp(math.log(27525.12) - 2.1282317 * jax.random.uniform(arg_keys[17], (2, D), jnp.float32) ** level_of(arg_keys[17], (2, D), ((1, 8),), -0.2, 0.2)), 3276.8, 27525.12)
    return dict(tokens=tokens, seg_lens=seg_lens, cotangent=cotangent, qkv_w=qkv_w, out_w=out_w, gu_w=gu_w, down_w=down_w, gains=gains, qkv_m=qkv_m, qkv_v=qkv_v, out_m=out_m, out_v=out_v, gu_m=gu_m, gu_v=gu_v, down_m=down_m, down_v=down_v, gain_m=gain_m, gain_v=gain_v)


@jax.custom_vjp
def low(v):
    return lax.optimization_barrier(v.astype(jnp.bfloat16)).astype(jnp.float32)

@jax.custom_vjp
def low_back(v):
    return v

def low_keep(v):
    return (low(v), None)

def low_pass(kept, grad):
    return (grad,)

def back_keep(v):
    return (v, None)

def back_low(kept, grad):
    return (low(grad),)
low.defvjp(low_keep, low_pass)
low_back.defvjp(back_keep, back_low)
norm_eps = 1e-05
beta_one = 0.9
beta_two = 0.95
adam_eps = 1e-08
weight_decay = 0.05
matrix_rate = 0.1
gain_rate = 0.3
masked_score = -1e+30
highest = lax.Precision.HIGHEST

def segment_layout(seg_lens):
    seg_ends = jnp.cumsum(seg_lens, axis=1).astype(jnp.int32)
    seg_starts = seg_ends - seg_lens
    slot_ids = jnp.arange(SEQ, dtype=jnp.int32)
    inside = ((slot_ids[None, None, :] >= seg_starts[:, :, None]) & (slot_ids[None, None, :] < seg_ends[:, :, None])).astype(jnp.int32)
    seg_ids = lax.optimization_barrier(jnp.sum(inside * jnp.arange(NSEG, dtype=jnp.int32)[None, :, None], axis=1))
    offsets = lax.optimization_barrier(jnp.sum(inside * seg_starts[:, :, None], axis=1))
    return (seg_ids, slot_ids[None, :] - offsets)

def rope_tables(places):
    half_len = HD // 2
    freqs = 10000.0 ** (-jnp.arange(half_len, dtype=jnp.float32) / half_len)
    angles = places.astype(jnp.float32)[:, :, None, None] * freqs
    return (jnp.cos(angles), jnp.sin(angles))

def rotate(tensor, cos_tab, sin_tab):
    half_len = tensor.shape[-1] // 2
    first_half = tensor[..., :half_len]
    second_half = tensor[..., half_len:]
    return jnp.concatenate([first_half * cos_tab - second_half * sin_tab, second_half * cos_tab + first_half * sin_tab], axis=-1)

def rms_norm(values, gain_vec):
    inv_scale = lax.rsqrt(lax.optimization_barrier(jnp.mean(values * values, axis=-1, keepdims=True)) + norm_eps)
    return values * inv_scale * gain_vec

def attend_row(pieces):
    queries, keys_row, values_row, seg_row = pieces
    slot_ids = jnp.arange(SEQ, dtype=jnp.int32)
    allowed = (seg_row[:, None] == seg_row[None, :]) & (slot_ids[None, :] <= slot_ids[:, None])
    scores = low_back(jnp.einsum('qhd,khd->hqk', queries, keys_row, precision=highest) * 0.125)
    scores = jnp.where(allowed[None], scores, masked_score)
    largest = lax.optimization_barrier(jnp.max(scores, axis=-1, keepdims=True))
    exp_vals = jnp.exp(scores - largest)
    prob_low = low(exp_vals / lax.optimization_barrier(jnp.sum(exp_vals, axis=-1, keepdims=True)))
    return jnp.einsum('hqk,khd->qhd', prob_low, values_row, precision=highest)

def layer(tokens, qkv_w, out_w, gu_w, down_w, gains, seg_ids, cos_tab, sin_tab):
    row_count = tokens.shape[0]
    shape_four = (row_count, SEQ, HEADS, HD)
    qkv_low = low(qkv_w)
    out_low = low(out_w)
    gu_low = low(gu_w)
    down_low = low(down_w)
    gain_low = low(gains)
    normed_one = low(rms_norm(tokens, gain_low[0])).reshape(-1, D)
    queries = low_back(jnp.dot(normed_one, qkv_low[0], precision=highest)).reshape(shape_four)
    keys_all = low_back(jnp.dot(normed_one, qkv_low[1], precision=highest)).reshape(shape_four)
    values_all = low(low_back(jnp.dot(normed_one, qkv_low[2], precision=highest))).reshape(shape_four)
    queries = low(rotate(queries, cos_tab, sin_tab))
    keys_all = low(rotate(keys_all, cos_tab, sin_tab))
    mixed = lax.map(jax.checkpoint(attend_row), (queries, keys_all, values_all, seg_ids))
    mixed = low(low_back(mixed.reshape(-1, D)))
    middle = tokens + low_back(jnp.dot(mixed, out_low, precision=highest)).reshape(tokens.shape)
    normed_two = low(rms_norm(middle, gain_low[1])).reshape(-1, D)
    gate = low_back(jnp.dot(normed_two, gu_low[0], precision=highest))
    upward = low_back(jnp.dot(normed_two, gu_low[1], precision=highest))
    hidden = low(jax.nn.silu(gate) * upward)
    return middle + low_back(jnp.dot(hidden, down_low, precision=highest)).reshape(tokens.shape)

def adam_step(weight, grad_sum, moment, second, rate, decay):
    moment_new = beta_one * moment + (1.0 - beta_one) * grad_sum
    second_new = beta_two * second + (1.0 - beta_two) * grad_sum * grad_sum
    moment_hat = moment_new / (1.0 - beta_one ** STEP)
    second_hat = second_new / (1.0 - beta_two ** STEP)
    weight_new = weight - rate * (moment_hat / (jnp.sqrt(second_hat) + adam_eps) + decay * weight)
    return (moment_new, second_new, weight_new)

def reference(tokens, seg_lens, cotangent, qkv_w, out_w, gu_w, down_w, gains, qkv_m, qkv_v, out_m, out_v, gu_m, gu_v, down_m, down_v, gain_m, gain_v):
    seg_ids, places = segment_layout(seg_lens)
    cos_tab, sin_tab = rope_tables(places)

    def forward_fn(tok_in, qkv_in, out_in, gu_in, down_in, gain_in):
        return layer(tok_in, qkv_in, out_in, gu_in, down_in, gain_in, seg_ids, cos_tab, sin_tab)
    output, pullback = jax.vjp(forward_fn, tokens.astype(jnp.float32), qkv_w, out_w, gu_w, down_w, gains)
    input_grad, grad_qkv, grad_out, grad_gu, grad_down, grad_gain = pullback(cotangent)
    qkv_res = adam_step(qkv_w, grad_qkv, qkv_m, qkv_v, matrix_rate, weight_decay)
    out_res = adam_step(out_w, grad_out, out_m, out_v, matrix_rate, weight_decay)
    gu_res = adam_step(gu_w, grad_gu, gu_m, gu_v, matrix_rate, weight_decay)
    down_res = adam_step(down_w, grad_down, down_m, down_v, matrix_rate, weight_decay)
    gain_res = adam_step(gains, grad_gain, gain_m, gain_v, gain_rate, 0.0)
    return (output, input_grad, qkv_res[0], qkv_res[1], qkv_res[2], out_res[0], out_res[1], out_res[2], gu_res[0], gu_res[1], gu_res[2], down_res[0], down_res[1], down_res[2], gain_res[0], gain_res[1], gain_res[2])
```

```python
import functools

import jax
import jax.numpy as jnp
from jax import lax
from jax.experimental import pallas as pl
from jax.experimental.pallas import tpu as pltpu
from jax.sharding import PartitionSpec as P

bf16, f32 = jnp.bfloat16, jnp.float32
STEP = 10
beta_one, beta_two, adam_eps = 0.9, 0.95, 1e-08
weight_decay, matrix_rate, gain_rate = 0.05, 0.1, 0.3
EPS = 1e-5
def nn(a,b): return lax.dot_general(a,b,(((1,),(0,)),((),())),preferred_element_type=f32)
def nt(a,b): return lax.dot_general(a,b,(((1,),(1,)),((),())),preferred_element_type=f32)
def tn(a,b): return lax.dot_general(a,b,(((0,),(0,)),((),())),preferred_element_type=f32)

def mlp_kernel(T, x_ref, ob_ref, obT_ref, cot_ref, wo_ref, wgu_ref, wd_ref, gain_ref,
               out_ref, dmid_ref, dob_ref, dobT_ref, dwo_ref, dwgu_ref, dwd_ref,
               h2_s, h2T_s, dfb_s, dh2_s, r_s, hid_s, dg_s, du_s):
    f = pl.program_id(0); nf = pl.num_programs(0)
    S = x_ref.shape[0]; nt_ = S // T
    gain = gain_ref[1:2, :]
    @pl.when(f == 0)
    def _():
        @pl.loop(0, nt_)
        def _(i):
            t = pl.ds(pl.multiple_of(i*T, T), T)
            mid = x_ref[t, :].astype(f32) + nn(ob_ref[t, :], wo_ref[...])
            out_ref[t, :] = mid
            dmid_ref[t, :] = mid
            r = lax.rsqrt(jnp.mean(mid*mid, axis=-1, keepdims=True) + EPS)
            r_s[t, :] = jnp.broadcast_to(r, (T, 128))
            h2 = ((mid*r)*gain).astype(bf16)
            h2_s[t, :] = h2
            h2T_s[:, t] = h2.T
            dfb_s[t, :] = cot_ref[t, :].astype(bf16)
            dh2_s[t, :] = jnp.zeros_like(mid)
    @pl.loop(0, nt_)
    def _(i):
        t = pl.ds(pl.multiple_of(i*T, T), T)
        h2 = h2_s[t, :]; dfb = dfb_s[t, :]
        g = nn(h2, wgu_ref[0]); u = nn(h2, wgu_ref[1])
        dh = nt(dfb, wd_ref[...])
        sig = 0.5*jnp.tanh(0.5*g)+0.5
        silu = g*sig
        hid = (silu*u).astype(bf16)
        dg = (dh*u*(sig*(1.0+g*(1.0-sig)))).astype(bf16)
        du = (dh*silu).astype(bf16)
        hid_s[t, :] = hid; dg_s[t, :] = dg; du_s[t, :] = du
        out_ref[t, :] += nn(hid, wd_ref[...])
        dh2_s[t, :] += nt(dg, wgu_ref[0]) + nt(du, wgu_ref[1])
    dwd_ref[...] = tn(hid_s[...], dfb_s[...]).astype(bf16)
    dwgu_ref[0] = nn(h2T_s[...], dg_s[...]).astype(bf16)
    dwgu_ref[1] = nn(h2T_s[...], du_s[...]).astype(bf16)
    @pl.when(f == nf-1)
    def _():
        @pl.loop(0, nt_)
        def _(i):
            t = pl.ds(pl.multiple_of(i*T, T), T)
            mid = dmid_ref[t, :]; r = r_s[t, 0:1]
            xh = mid*r; dh = dh2_s[t, :]; w = dh*gain
            back = r*(w - xh*jnp.mean(w*xh, axis=-1, keepdims=True))
            dmid = cot_ref[t, :] + back
            dmid_ref[t, :] = dmid
            dab = dmid.astype(bf16)
            h2_s[t, :] = dab
            dob_ref[t, :] = nt(dab, wo_ref[...]).astype(bf16)
            dobT_ref[:, t] = nt(wo_ref[...], dab).astype(bf16)
        dwo_ref[...] = nn(obT_ref[...], h2_s[...]).astype(bf16)

def mlp(x, ob, obT, cot, wo, wgu, wd, gains, FC=512, T=256):
    S, D = x.shape; FF = wd.shape[0]
    full = lambda *s: pl.BlockSpec(s, lambda f: (0,)*len(s), pipeline_mode=pl.Buffered(1))
    return pl.pallas_call(
        functools.partial(mlp_kernel, T), grid=(FF//FC,),
        in_specs=[full(S,D), full(S,D), full(D,S), full(S,D), full(D,D),
                  pl.BlockSpec((2,D,FC), lambda f:(0,0,f)), pl.BlockSpec((FC,D), lambda f:(f,0)), full(8,D)],
        out_specs=[full(S,D), full(S,D), full(S,D), full(D,S), full(D,D),
                  pl.BlockSpec((2,D,FC), lambda f:(0,0,f)), pl.BlockSpec((FC,D), lambda f:(f,0))],
        out_shape=[jax.ShapeDtypeStruct((S,D),f32), jax.ShapeDtypeStruct((S,D),f32), jax.ShapeDtypeStruct((S,D),bf16),
                   jax.ShapeDtypeStruct((D,S),bf16), jax.ShapeDtypeStruct((D,D),bf16),
                   jax.ShapeDtypeStruct((2,D,FF),bf16), jax.ShapeDtypeStruct((FF,D),bf16)],
        scratch_shapes=[pltpu.VMEM((S,D),bf16), pltpu.VMEM((D,S),bf16), pltpu.VMEM((S,D),bf16), pltpu.VMEM((S,D),f32),
                        pltpu.VMEM((S,128),f32), pltpu.VMEM((S,FC),bf16), pltpu.VMEM((S,FC),bf16), pltpu.VMEM((S,FC),bf16)],
        compiler_params=pltpu.CompilerParams(vmem_limit_bytes=62*2**20),
        name="mlp",
    )(x, ob, obT, cot, wo, wgu, wd, gains)
H, HD = 12, 64
NEG = -1e30
VM = pl.BlockSpec(memory_space=pltpu.VMEM)
def tnt(a,b): return lax.dot_general(a,b,(((0,),(1,)),((),())),preferred_element_type=f32)

def seg_rows(lens_ref, S):
    slot = lax.broadcasted_iota(jnp.int32, (8, S), 1)
    seg = jnp.zeros((8, S), jnp.int32); start = jnp.zeros((8, S), jnp.int32)
    end = jnp.int32(0)
    for s in range(lens_ref.shape[1]-1):
        end = end + lens_ref[0, s]
        past = (slot >= end).astype(jnp.int32)
        seg += past
        start += past * lens_ref[0, s]
    return seg, slot - start

def attn_fwd_body(lens_ref, x_ref, gain_ref, freq_ref, wqkv_ref, qT_ref, kT_ref, vT_ref, ob_ref, oT_ref, lse_ref, cos_ref, sin_ref, segc_ref, segr_ref,
                 bias_s, B=256):
    S, D = x_ref.shape
    n = S // B
    seg, place = seg_rows(lens_ref, S)
    ang = jnp.broadcast_to(place[0:1, :].astype(f32), (HD//2, S)) * freq_ref[:, 0:1]
    cos_ref[...] = jnp.cos(ang); sin_ref[...] = jnp.sin(ang)
    segf = jnp.broadcast_to(seg[0:1, :].astype(f32), (128, S))
    segr_ref[...] = segf[0:8]
    segc_ref[...] = segf.T
    @pl.loop(0, n)
    def _(i):
        t = pl.ds(pl.multiple_of(i*B, B), B)
        xf = x_ref[t, :].astype(f32)
        r = lax.rsqrt(jnp.mean(xf*xf, axis=-1, keepdims=True) + EPS)
        h1 = ((xf*r)*gain_ref[0:1, :]).astype(bf16)
        c = cos_ref[:, t]; s = sin_ref[:, t]
        for w, dst, sc in ((0, qT_ref, 0.125), (1, kT_ref, 1.0)):
            y = tnt(wqkv_ref[w], h1)
            for h in range(H):
                a = y[h*HD:h*HD+32]; b = y[h*HD+32:h*HD+64]
                dst[h*HD:h*HD+32, t] = ((a*c - b*s)*sc).astype(bf16)
                dst[h*HD+32:h*HD+64, t] = ((b*c + a*s)*sc).astype(bf16)
        vT_ref[:, t] = tnt(wqkv_ref[2], h1).astype(bf16)
    for i in range(n):
        k0 = max(0, i-2)*B; nk = i*B + B - k0
        q0 = i*B
        kid = lax.broadcasted_iota(jnp.int32, (nk, B), 0) + k0
        qid = lax.broadcasted_iota(jnp.int32, (nk, B), 1) + q0
        ok = (segc_ref[k0:k0+nk, 0:1] == segr_ref[0:1, q0:q0+B]) & (kid <= qid)
        bias_s[0:nk, :] = jnp.where(ok, 0.0, NEG)
        @pl.loop(0, H//2)
        def _(p):
            for e in range(2):
                rows = pl.ds(pl.multiple_of(p*128 + e*64, 64), 64)
                s = tn(kT_ref[rows, k0:k0+nk], qT_ref[rows, q0:q0+B]) + bias_s[0:nk, :]
                m = jnp.max(s, axis=0, keepdims=True)
                ex = jnp.exp(s - m)
                l = jnp.sum(ex, axis=0, keepdims=True)
                o = nn(vT_ref[rows, k0:k0+nk], ex.astype(bf16)) * (1.0/l)
                oT_ref[rows, q0:q0+B] = o.astype(bf16)
                lse_ref[pl.ds(p*2+e, 1), q0:q0+B] = m + jnp.log(l)
        ob_ref[q0:q0+B, :] = oT_ref[:, q0:q0+B].T

def attn_fwd(lens, x, gains, freq, wqkv):
    S, D = x.shape
    sh = lambda s, d: jax.ShapeDtypeStruct(s, d)
    return pl.pallas_call(attn_fwd_body,
        in_specs=[pl.BlockSpec(memory_space=pltpu.SMEM)]+[VM]*4, out_specs=[VM]*10,
        out_shape=[sh((D,S),bf16), sh((D,S),bf16), sh((D,S),bf16), sh((S,D),bf16), sh((D,S),bf16), sh((16,S),f32),
                   sh((32,S),f32), sh((32,S),f32), sh((S,128),f32), sh((8,S),f32)],
        scratch_shapes=[pltpu.VMEM((768,256),f32)],
        compiler_params=pltpu.CompilerParams(vmem_limit_bytes=62*2**20), name="attn_fwd")(lens, x, gains, freq, wqkv)

def attn_bwd_body(x_ref, gain_ref, wqkv_ref, dmid_ref, qT_ref, kT_ref, vT_ref, dob_ref, dobT_ref, oT_ref, lse_ref, cos_ref, sin_ref, segc_ref, segr_ref,
                  ig_ref, dw_ref, bias_s, k_s, v_s, q_s, dqT_s, dk_s, dv_s, dkT_s, h1T_s, B=256):
    S, D = x_ref.shape
    n = S // B
    k_s[...] = kT_ref[...].T; v_s[...] = vT_ref[...].T; q_s[...] = qT_ref[...].T
    dk_s[...] = jnp.zeros_like(dk_s); dv_s[...] = jnp.zeros_like(dv_s)
    lane = lax.broadcasted_iota(jnp.int32, (B, 128), 1)
    for i in range(n):
        k0 = max(0, i-2)*B; nk = i*B + B - k0
        q0 = i*B
        kid = lax.broadcasted_iota(jnp.int32, (nk, B), 0) + k0
        qid = lax.broadcasted_iota(jnp.int32, (nk, B), 1) + q0
        ok = (segc_ref[k0:k0+nk, 0:1] == segr_ref[0:1, q0:q0+B]) & (kid <= qid)
        bias_s[0:nk, :] = jnp.where(ok, 0.0, NEG)
        @pl.loop(0, H//2)
        def _(p):
            cols = pl.ds(pl.multiple_of(p*128, 128), 128)
            dv = None
            for e in range(2):
                rows = pl.ds(pl.multiple_of(p*128 + e*64, 64), 64)
                mine = (lane < 64) if e == 0 else (lane >= 64)
                dobz = jnp.where(mine, dob_ref[q0:q0+B, cols], 0).astype(bf16)
                qz = jnp.where(mine, q_s[q0:q0+B, cols], 0).astype(bf16)
                s = tn(kT_ref[rows, k0:k0+nk], qT_ref[rows, q0:q0+B]) + bias_s[0:nk, :]
                pr = jnp.exp(s - lse_ref[pl.ds(p*2+e, 1), q0:q0+B])
                dp = tn(vT_ref[rows, k0:k0+nk], dobT_ref[rows, q0:q0+B])
                inner = jnp.sum(pr*dp, axis=0, keepdims=True)
                ds = (pr*(dp - inner)).astype(bf16)
                dve = nn(pr.astype(bf16), dobz)
                dke = nn(ds, qz)
                dqT_s[rows, q0:q0+B] = nn(kT_ref[rows, k0:k0+nk], ds) * 0.125
                dv = dve if dv is None else dv + dve
                dk = dke if e == 0 else dk + dke
            dv_s[k0:k0+nk, cols] += dv
            dk_s[k0:k0+nk, cols] += dk
    @pl.loop(0, n)
    def _(i):
        t = pl.ds(pl.multiple_of(i*B, B), B)
        c = cos_ref[:, t]; s = sin_ref[:, t]
        dkT = dk_s[t, :].T
        for src, dst in ((dqT_s[:, t], qT_ref), (dkT, kT_ref)):
            for h in range(H):
                a = src[h*HD:h*HD+32]; b = src[h*HD+32:h*HD+64]
                dqT_s[h*HD:h*HD+32, t] = a*c + b*s
                dqT_s[h*HD+32:h*HD+64, t] = b*c - a*s
            if dst is qT_ref:
                q_s[t, :] = dqT_s[:, t].astype(bf16).T
            else:
                k_s[t, :] = dqT_s[:, t].astype(bf16).T
        dvb = dv_s[t, :].astype(bf16)
        v_s[t, :] = dvb
        gain = gain_ref[0:1, :]
        xf = x_ref[t, :].astype(f32)
        r = lax.rsqrt(jnp.mean(xf*xf, axis=-1, keepdims=True) + EPS)
        xh = xf*r
        h1T_s[:, t] = (xh*gain).astype(bf16).T
        dh = nt(q_s[t, :], wqkv_ref[0]) + nt(k_s[t, :], wqkv_ref[1]) + nt(dvb, wqkv_ref[2])
        w = dh*gain
        ig_ref[t, :] = dmid_ref[t, :] + r*(w - xh*jnp.mean(w*xh, axis=-1, keepdims=True))
    dw_ref[0] = nn(h1T_s[...], q_s[...]).astype(bf16)
    dw_ref[1] = nn(h1T_s[...], k_s[...]).astype(bf16)
    dw_ref[2] = nn(h1T_s[...], v_s[...]).astype(bf16)

def attn_bwd(x, gains, wqkv, dmid, qT, kT, vT, dob, dobT, oT, lse, cos, sin, segc, segr):
    S, D = x.shape
    sh = lambda s, d: jax.ShapeDtypeStruct(s, d)
    return pl.pallas_call(attn_bwd_body,
        in_specs=[VM]*15, out_specs=[VM]*2,
        out_shape=[sh((S,D),f32), sh((3,D,D),bf16)],
        scratch_shapes=[pltpu.VMEM((768,256),f32), pltpu.VMEM((S,D),bf16), pltpu.VMEM((S,D),bf16), pltpu.VMEM((S,D),bf16),
                        pltpu.VMEM((D,S),f32), pltpu.VMEM((S,D),f32), pltpu.VMEM((S,D),f32), pltpu.VMEM((8,128),f32), pltpu.VMEM((D,S),bf16)],
        compiler_params=pltpu.CompilerParams(vmem_limit_bytes=62*2**20), name="attn_bwd")(x, gains, wqkv, dmid, qT, kT, vT, dob, dobT, oT, lse, cos, sin, segc, segr)


def adam_step(weight, grad_sum, moment, second, rate, decay):
    moment_new = beta_one * moment + (1.0 - beta_one) * grad_sum
    second_new = beta_two * second + (1.0 - beta_two) * grad_sum * grad_sum
    moment_hat = moment_new / (1.0 - beta_one**STEP)
    second_hat = second_new / (1.0 - beta_two**STEP)
    weight_new = weight - rate * (moment_hat / (jnp.sqrt(second_hat) + adam_eps) + decay * weight)
    return (moment_new, second_new, weight_new)


def per_device(tokens, seg_lens, cotangent, qkv_w, out_w, gu_w, down_w, gains,
               qkv_m, qkv_v, out_m, out_v, gu_m, gu_v, down_m, down_v, gain_m, gain_v):
    _, S, D = tokens.shape
    x = tokens.reshape(S, D)
    cot = cotangent.reshape(S, D)
    gain_low = gains.astype(bf16)
    wqkv = lax.all_gather(qkv_w.astype(bf16), "dp", axis=1, tiled=True)
    gain_full = lax.all_gather(gain_low, "dp", axis=1, tiled=True).astype(f32)
    wo = lax.all_gather(out_w.astype(bf16), "dp", axis=0, tiled=True)
    wgu = lax.all_gather(gu_w.astype(bf16), "dp", axis=1, tiled=True)
    wd = lax.all_gather(down_w.astype(bf16), "dp", axis=0, tiled=True)
    gain8 = jnp.pad(gain_full, ((0, 6), (0, 0)))
    freq = 10000.0 ** (-jnp.arange(HD // 2, dtype=f32) / (HD // 2))
    freq = jnp.broadcast_to(freq[:, None], (HD // 2, 128))
    qT, kT, vT, ob, oT, lse, cos, sin, segc, segr = attn_fwd(seg_lens, x, gain8, freq, wqkv)
    output, dmid, dob, dobT, dwo, dwgu, dwd = mlp(x, ob, oT, cot, wo, wgu, wd, gain8)
    input_grad, dwqkv = attn_bwd(x, gain8, wqkv, dmid, qT, kT, vT, dob, dobT, oT, lse, cos, sin, segc, segr)

    def owned(grad, axis):
        part = lax.psum_scatter(grad, "dp", scatter_dimension=axis, tiled=True)
        return lax.psum(part.astype(f32), "rep")

    g_down = owned(dwd, 0)
    g_gu = owned(dwgu, 1)
    g_out = owned(dwo, 0)
    g_qkv = owned(dwqkv, 1)
    gain_f = gain_low.astype(f32)
    g_gain = jnp.stack([
        jnp.sum(g_qkv * qkv_w.astype(bf16).astype(f32), axis=(0, 2)) / gain_f[0],
        jnp.sum(g_gu * gu_w.astype(bf16).astype(f32), axis=(0, 2)) / gain_f[1],
    ])
    qkv_res = adam_step(qkv_w, g_qkv, qkv_m, qkv_v, matrix_rate, weight_decay)
    out_res = adam_step(out_w, g_out, out_m, out_v, matrix_rate, weight_decay)
    gu_res = adam_step(gu_w, g_gu, gu_m, gu_v, matrix_rate, weight_decay)
    down_res = adam_step(down_w, g_down, down_m, down_v, matrix_rate, weight_decay)
    gain_res = adam_step(gains, g_gain, gain_m, gain_v, gain_rate, 0.0)
    return (output.reshape(tokens.shape), input_grad.reshape(tokens.shape)) + qkv_res + out_res + gu_res + down_res + gain_res


def solution(mesh):
    rows, cols, vec = P(("dp", "rep"), None, None), P(None, "dp", None), P("dp", None)
    small = P(None, "dp")
    return jax.shard_map(
        per_device,
        mesh=mesh,
        in_specs=(rows, P(("dp", "rep"), None), rows, cols, vec, cols, vec, small,
                  cols, cols, vec, vec, cols, cols, vec, vec, small, small),
        out_specs=(rows, rows) + (cols,) * 3 + (vec,) * 3 + (cols,) * 3 + (vec,) * 3 + (small,) * 3,
        check_vma=False,
    )
```

```python
import functools

import jax
import jax.numpy as jnp
from jax import lax
from jax.experimental import pallas as pl
from jax.experimental.pallas import tpu as pltpu
from jax.sharding import PartitionSpec as P

bf16, f32 = jnp.bfloat16, jnp.float32
STEP = 10
beta_one, beta_two, adam_eps = 0.9, 0.95, 1e-08
weight_decay, matrix_rate, gain_rate = 0.05, 0.1, 0.3
EPS = 1e-5
def nn(a,b): return lax.dot_general(a,b,(((1,),(0,)),((),())),preferred_element_type=f32)
def nt(a,b): return lax.dot_general(a,b,(((1,),(1,)),((),())),preferred_element_type=f32)
def tn(a,b): return lax.dot_general(a,b,(((0,),(0,)),((),())),preferred_element_type=f32)

def mlp_kernel(T, x_ref, ob_ref, obT_ref, cot_ref, wo_ref, wgu_ref, wd_ref, gain_ref,
               out_ref, dmid_ref, dob_ref, dobT_ref, dwo_ref, dwgu_ref, dwd_ref,
               h2_s, h2T_s, dfb_s, dh2_s, r_s, hid_s, dg_s, du_s):
    f = pl.program_id(0); nf = pl.num_programs(0)
    S = x_ref.shape[0]; nt_ = S // T
    gain = gain_ref[1:2, :]
    @pl.when(f == 0)
    def _():
        @pl.loop(0, nt_)
        def _(i):
            t = pl.ds(pl.multiple_of(i*T, T), T)
            mid = x_ref[t, :].astype(f32) + nn(ob_ref[t, :], wo_ref[...])
            out_ref[t, :] = mid
            dmid_ref[t, :] = mid
            r = lax.rsqrt(jnp.mean(mid*mid, axis=-1, keepdims=True) + EPS)
            r_s[t, :] = jnp.broadcast_to(r, (T, 128))
            h2 = ((mid*r)*gain).astype(bf16)
            h2_s[t, :] = h2
            h2T_s[:, t] = h2.T
            dfb_s[t, :] = cot_ref[t, :].astype(bf16)
            dh2_s[t, :] = jnp.zeros_like(mid)
    @pl.loop(0, nt_)
    def _(i):
        t = pl.ds(pl.multiple_of(i*T, T), T)
        h2 = h2_s[t, :]; dfb = dfb_s[t, :]
        g = nn(h2, wgu_ref[0]); u = nn(h2, wgu_ref[1])
        dh = nt(dfb, wd_ref[...])
        sig = 0.5*jnp.tanh(0.5*g)+0.5
        silu = g*sig
        hid = (silu*u).astype(bf16)
        dg = (dh*u*(sig*(1.0+g*(1.0-sig)))).astype(bf16)
        du = (dh*silu).astype(bf16)
        hid_s[t, :] = hid; dg_s[t, :] = dg; du_s[t, :] = du
        out_ref[t, :] += nn(hid, wd_ref[...])
        dh2_s[t, :] += nt(dg, wgu_ref[0]) + nt(du, wgu_ref[1])
    dwd_ref[...] = tn(hid_s[...], dfb_s[...]).astype(bf16)
    dwgu_ref[0] = nn(h2T_s[...], dg_s[...]).astype(bf16)
    dwgu_ref[1] = nn(h2T_s[...], du_s[...]).astype(bf16)
    @pl.when(f == nf-1)
    def _():
        @pl.loop(0, nt_)
        def _(i):
            t = pl.ds(pl.multiple_of(i*T, T), T)
            mid = dmid_ref[t, :]; r = r_s[t, 0:1]
            xh = mid*r; dh = dh2_s[t, :]; w = dh*gain
            back = r*(w - xh*jnp.mean(w*xh, axis=-1, keepdims=True))
            dmid = cot_ref[t, :] + back
            dmid_ref[t, :] = dmid
            dab = dmid.astype(bf16)
            h2_s[t, :] = dab
            dob_ref[t, :] = nt(dab, wo_ref[...]).astype(bf16)
            dobT_ref[:, t] = nt(wo_ref[...], dab).astype(bf16)
        dwo_ref[...] = nn(obT_ref[...], h2_s[...]).astype(bf16)

def mlp(x, ob, obT, cot, wo, wgu, wd, gains, FC=512, T=256):
    S, D = x.shape; FF = wd.shape[0]
    full = lambda *s: pl.BlockSpec(s, lambda f: (0,)*len(s), pipeline_mode=pl.Buffered(1))
    return pl.pallas_call(
        functools.partial(mlp_kernel, T), grid=(FF//FC,),
        in_specs=[full(S,D), full(S,D), full(D,S), full(S,D), full(D,D),
                  pl.BlockSpec((2,D,FC), lambda f:(0,0,f)), pl.BlockSpec((FC,D), lambda f:(f,0)), full(8,D)],
        out_specs=[full(S,D), full(S,D), full(S,D), full(D,S), full(D,D),
                  pl.BlockSpec((2,D,FC), lambda f:(0,0,f)), pl.BlockSpec((FC,D), lambda f:(f,0))],
        out_shape=[jax.ShapeDtypeStruct((S,D),f32), jax.ShapeDtypeStruct((S,D),f32), jax.ShapeDtypeStruct((S,D),bf16),
                   jax.ShapeDtypeStruct((D,S),bf16), jax.ShapeDtypeStruct((D,D),bf16),
                   jax.ShapeDtypeStruct((2,D,FF),bf16), jax.ShapeDtypeStruct((FF,D),bf16)],
        scratch_shapes=[pltpu.VMEM((S,D),bf16), pltpu.VMEM((D,S),bf16), pltpu.VMEM((S,D),bf16), pltpu.VMEM((S,D),f32),
                        pltpu.VMEM((S,128),f32), pltpu.VMEM((S,FC),bf16), pltpu.VMEM((S,FC),bf16), pltpu.VMEM((S,FC),bf16)],
        compiler_params=pltpu.CompilerParams(vmem_limit_bytes=62*2**20),
        name="mlp",
    )(x, ob, obT, cot, wo, wgu, wd, gains)

H, HD = 12, 64
NEG = -1e30
VM = pl.BlockSpec(memory_space=pltpu.VMEM)
def tnt(a,b): return lax.dot_general(a,b,(((0,),(1,)),((),())),preferred_element_type=f32)

def seg_rows(lens_ref, S):
    slot = lax.broadcasted_iota(jnp.int32, (8, S), 1)
    seg = jnp.zeros((8, S), jnp.int32); start = jnp.zeros((8, S), jnp.int32)
    end = jnp.int32(0)
    for s in range(lens_ref.shape[1]-1):
        end = end + lens_ref[0, s]
        past = (slot >= end).astype(jnp.int32)
        seg += past
        start += past * lens_ref[0, s]
    return seg, slot - start

def attn_bwd_body(x_ref, gain_ref, wqkv_ref, dmid_ref, qT_ref, kT_ref, vT_ref, dob_ref, dobT_ref, oT_ref, lse_ref, cos_ref, sin_ref, segc_ref, segr_ref,
                  ig_ref, dw_ref, bias_s, k_s, v_s, q_s, dqT_s, dk_s, dv_s, dkT_s, h1T_s, B=256):
    S, D = x_ref.shape
    n = S // B
    k_s[...] = kT_ref[...].T; v_s[...] = vT_ref[...].T; q_s[...] = qT_ref[...].T
    dk_s[...] = jnp.zeros_like(dk_s); dv_s[...] = jnp.zeros_like(dv_s)
    lane = lax.broadcasted_iota(jnp.int32, (B, 128), 1)
    for i in range(n):
        k0 = max(0, i-2)*B; nk = i*B + B - k0
        q0 = i*B
        kid = lax.broadcasted_iota(jnp.int32, (nk, B), 0) + k0
        qid = lax.broadcasted_iota(jnp.int32, (nk, B), 1) + q0
        ok = (segc_ref[k0:k0+nk, 0:1] == segr_ref[0:1, q0:q0+B]) & (kid <= qid)
        bias_s[0:nk, :] = jnp.where(ok, 0.0, NEG)
        @pl.loop(0, H//2)
        def _(p):
            cols = pl.ds(pl.multiple_of(p*128, 128), 128)
            dv = None
            for e in range(2):
                rows = pl.ds(pl.multiple_of(p*128 + e*64, 64), 64)
                mine = (lane < 64) if e == 0 else (lane >= 64)
                dobz = jnp.where(mine, dob_ref[q0:q0+B, cols], 0).astype(bf16)
                qz = jnp.where(mine, q_s[q0:q0+B, cols], 0).astype(bf16)
                s = tn(kT_ref[rows, k0:k0+nk], qT_ref[rows, q0:q0+B]) + bias_s[0:nk, :]
                pr = jnp.exp(s - lse_ref[pl.ds(p*2+e, 1), q0:q0+B])
                dp = tn(vT_ref[rows, k0:k0+nk], dobT_ref[rows, q0:q0+B])
                inner = jnp.sum(pr*dp, axis=0, keepdims=True)
                ds = (pr*(dp - inner)).astype(bf16)
                dve = nn(pr.astype(bf16), dobz)
                dke = nn(ds, qz)
                dqT_s[rows, q0:q0+B] = nn(kT_ref[rows, k0:k0+nk], ds) * 0.125
                dv = dve if dv is None else dv + dve
                dk = dke if e == 0 else dk + dke
            dv_s[k0:k0+nk, cols] += dv
            dk_s[k0:k0+nk, cols] += dk
    @pl.loop(0, n)
    def _(i):
        t = pl.ds(pl.multiple_of(i*B, B), B)
        c = cos_ref[:, t]; s = sin_ref[:, t]
        dkT = dk_s[t, :].T
        for src, dst in ((dqT_s[:, t], qT_ref), (dkT, kT_ref)):
            for h in range(H):
                a = src[h*HD:h*HD+32]; b = src[h*HD+32:h*HD+64]
                dqT_s[h*HD:h*HD+32, t] = a*c + b*s
                dqT_s[h*HD+32:h*HD+64, t] = b*c - a*s
            if dst is qT_ref:
                q_s[t, :] = dqT_s[:, t].astype(bf16).T
            else:
                k_s[t, :] = dqT_s[:, t].astype(bf16).T
        dvb = dv_s[t, :].astype(bf16)
        v_s[t, :] = dvb
        gain = gain_ref[0:1, :]
        xf = x_ref[t, :].astype(f32)
        r = lax.rsqrt(jnp.mean(xf*xf, axis=-1, keepdims=True) + EPS)
        xh = xf*r
        h1T_s[:, t] = (xh*gain).astype(bf16).T
        dh = nt(q_s[t, :], wqkv_ref[0]) + nt(k_s[t, :], wqkv_ref[1]) + nt(dvb, wqkv_ref[2])
        w = dh*gain
        ig_ref[t, :] = dmid_ref[t, :] + r*(w - xh*jnp.mean(w*xh, axis=-1, keepdims=True))
    dw_ref[0] = nn(h1T_s[...], q_s[...]).astype(bf16)
    dw_ref[1] = nn(h1T_s[...], k_s[...]).astype(bf16)
    dw_ref[2] = nn(h1T_s[...], v_s[...]).astype(bf16)

def attn_bwd(x, gains, wqkv, dmid, qT, kT, vT, dob, dobT, oT, lse, cos, sin, segc, segr):
    S, D = x.shape
    sh = lambda s, d: jax.ShapeDtypeStruct(s, d)
    return pl.pallas_call(attn_bwd_body,
        in_specs=[VM]*15, out_specs=[VM]*2,
        out_shape=[sh((S,D),f32), sh((3,D,D),bf16)],
        scratch_shapes=[pltpu.VMEM((768,256),f32), pltpu.VMEM((S,D),bf16), pltpu.VMEM((S,D),bf16), pltpu.VMEM((S,D),bf16),
                        pltpu.VMEM((D,S),f32), pltpu.VMEM((S,D),f32), pltpu.VMEM((S,D),f32), pltpu.VMEM((8,128),f32), pltpu.VMEM((D,S),bf16)],
        compiler_params=pltpu.CompilerParams(vmem_limit_bytes=62*2**20), name="attn_bwd")(x, gains, wqkv, dmid, qT, kT, vT, dob, dobT, oT, lse, cos, sin, segc, segr)

MESH = pl.DeviceIdType.MESH

def flip(v, b):
    return v + b - 2*b*lax.rem(lax.div(v, b), 2)

def places():
    d = lax.axis_index("dp"); z = lax.axis_index("rep")
    sib, xn, yn = flip(d, 1), flip(d, 2), flip(d, 4)
    xy = flip(xn, 4)
    return d, z, sib, xn, yn, xy

def greet(devs):
    bar = pltpu.get_barrier_semaphore()
    for dev in devs:
        pl.semaphore_signal(bar, inc=1, device_id=dev, device_id_type=MESH)
    pl.semaphore_wait(bar, len(devs))

class Gather:
    N = 15
    def __init__(self, ref, view, send, recv, g):
        self.ref, self.view, self.send, self.recv, self.g = ref, view, send, recv, g
        d, z, sib, xn, yn, xy = places()
        zn = flip(z, 1)
        S, X, Y, Z = (sib, z), (xn, z), (yn, z), (d, zn)
        self.moves = [(d, "all", S), (d, "zb", X), (d, "zb", Y),
                      (xn, "zb", S), (xn, "z", Y), (xn, "z", Z),
                      (yn, "zb", S), (yn, "b", X), (yn, "z", Z),
                      (xy, "z", S), (xy, "z", Z), (xy, "b", S),
                      (xn, "o", S), (yn, "o", S), (xy, "o", S)]
        self.after = {1: (3, 4, 5), 2: (6, 7, 8), 4: (9, 10), 7: (11,), 5: (12,), 8: (13,), 10: (14,)}
    def copy(self, k):
        d, part, dev = self.moves[k]
        v = self.view(self.ref, d, part)
        return pltpu.make_async_remote_copy(src_ref=v, dst_ref=v, send_sem=self.send.at[self.g, k], recv_sem=self.recv.at[self.g, k],
                                            device_id=dev, device_id_type=MESH)
    def begin(self):
        for k in (1, 2, 0): self.copy(k).start()
    def got(self, *ks):
        for k in ks:
            self.copy(k).wait_recv()
            for j in self.after.get(k, ()): self.copy(j).start()
    def first(self): self.got(1, 2)
    def second(self): self.got(4, 7, 5, 8)
    def third(self): self.got(10)
    def sibling(self): self.got(0, 3, 6, 9, 11, 12, 13, 14)
    def sent(self):
        for k in range(self.N): self.copy(k).wait_send()

def row_view(rows, a, lead):
    z = lax.axis_index("rep"); p = lax.rem(z, 2)
    def view(ref, d, part):
        off, n = {"all": (0, rows), "zb": (p*a, rows - a), "z": (p*(rows - a), a), "b": (a, rows - 2*a), "o": ((1 - p)*(rows - a), a)}[part]
        s = pl.ds(pl.multiple_of(d*rows + off, 16), n)
        return ref.at[:, s, :] if lead else ref.at[s, :]
    return view

def cut(rows):
    return rows // 3 // 16 * 16

def can_gather(mesh_dp, mesh_rep, *rows):
    return mesh_dp == 8 and mesh_rep % 2 == 0 and all(r % 16 == 0 and cut(r) > 0 for r in rows)

ANY = pl.BlockSpec(memory_space=pl.ANY)
SM = pl.BlockSpec(memory_space=pltpu.SMEM)
B = 256

def spread_gain(pieces, D):
    n, wide = pieces.shape[0], D // pieces.shape[0]
    r = lax.broadcasted_iota(jnp.int32, (n*128, D), 0); c = lax.broadcasted_iota(jnp.int32, (n*128, D), 1)
    pick = (c == lax.div(r, 128)*wide + lax.rem(r, 128)) & (lax.rem(r, 128) < wide)
    flat = jnp.concatenate([pieces[i] for i in range(n)], axis=1).astype(bf16)
    return nn(flat, jnp.where(pick, 1.0, 0.0).astype(bf16))

def forward_attention(lens_ref, x_ref, freq_ref, gain_of, weights_in, w_ref, qT_s, kT_s, vT_s, oT_s, lse_s, cos_s, sin_s, segc_s, segr_s, bias_s, hook):
    S, D = x_ref.shape
    n = S // B
    seg, place = seg_rows(lens_ref, S)
    ang = jnp.broadcast_to(place[0:1, :].astype(f32), (HD//2, S)) * freq_ref[:, 0:1]
    cos_s[...] = jnp.cos(ang); sin_s[...] = jnp.sin(ang)
    segf = jnp.broadcast_to(seg[0:1, :].astype(f32), (128, S))
    segr_s[...] = segf[0:8]
    segc_s[...] = segf.T
    weights_in()
    gain = gain_of()
    @pl.loop(0, n)
    def _(i):
        t = pl.ds(pl.multiple_of(i*B, B), B)
        xf = x_ref[t, :].astype(f32)
        r = lax.rsqrt(jnp.mean(xf*xf, axis=-1, keepdims=True) + EPS)
        h1 = ((xf*r)*gain).astype(bf16)
        c = cos_s[:, t]; s = sin_s[:, t]
        for w, dst, sc in ((0, qT_s, 0.125), (1, kT_s, 1.0)):
            y = tnt(w_ref[w], h1)
            for h in range(H):
                a = y[h*HD:h*HD+32]; b = y[h*HD+32:h*HD+64]
                dst[h*HD:h*HD+32, t] = ((a*c - b*s)*sc).astype(bf16)
                dst[h*HD+32:h*HD+64, t] = ((b*c + a*s)*sc).astype(bf16)
        vT_s[:, t] = tnt(w_ref[2], h1).astype(bf16)
    hook("proj")
    for i in range(n):
        k0 = max(0, i-2)*B; nk = i*B + B - k0
        q0 = i*B
        kid = lax.broadcasted_iota(jnp.int32, (nk, B), 0) + k0
        qid = lax.broadcasted_iota(jnp.int32, (nk, B), 1) + q0
        ok = (segc_s[k0:k0+nk, 0:1] == segr_s[0:1, q0:q0+B]) & (kid <= qid)
        bias_s[0:nk, :] = jnp.where(ok, 0.0, NEG)
        @pl.loop(0, H//2)
        def _(p):
            for e in range(2):
                rows = pl.ds(pl.multiple_of(p*128 + e*64, 64), 64)
                s = tn(kT_s[rows, k0:k0+nk], qT_s[rows, q0:q0+B]) + bias_s[0:nk, :]
                m = jnp.max(s, axis=0, keepdims=True)
                ex = jnp.exp(s - m)
                l = jnp.sum(ex, axis=0, keepdims=True)
                o = nn(vT_s[rows, k0:k0+nk], ex.astype(bf16)) * (1.0/l)
                oT_s[rows, q0:q0+B] = o.astype(bf16)
                lse_s[pl.ds(p*2+e, 1), q0:q0+B] = m + jnp.log(l)
        hook(i)

def ka_body(sizes, lens_ref, x_ref, freq_ref, gain_ref, qw_ref, ow_ref, gw_ref, dw_ref,
            qT_o, kT_o, vT_o, oT_o, lse_ref, cos_ref, sin_ref, segc_ref, segr_ref, gain8_ref, wq_o, wo_o, wgu_o, wd_o,
            qT_s, kT_s, vT_s, oT_s, bias_s, wq_s, ost_s, gst_s, dst_s, of_s, gf_s, df_s, gp_s, send, recv, gsend, grecv, loc):
    n_dp, n_rep = sizes
    D = x_ref.shape[1]
    d, z, sib, xn, yn, xy = places()
    others = [lax.rem(d + j, n_dp) for j in range(1, n_dp)]
    loads = [pltpu.make_async_copy(a, b, loc.at[i]) for i, (a, b) in enumerate(((ow_ref, of_s), (gw_ref, gf_s), (dw_ref, df_s)))]
    for c in loads: c.start()
    gp_s[pl.ds(d, 1)] = gain_ref[...].reshape(1, 8, 128)
    rq, ro, rg, rd = qw_ref.shape[1], ow_ref.shape[0], gw_ref.shape[1], dw_ref.shape[0]
    G = [Gather(full, row_view(r, cut(r), ld), send, recv, g)
         for g, (full, r, ld) in enumerate(((wq_s, rq, True), (wo_o, ro, False), (wgu_o, rg, True), (wd_o, rd, False)))]
    wq_s[:, pl.ds(pl.multiple_of(d*rq, 16), rq), :] = qw_ref[...].astype(bf16)
    greet([(o, z) for o in others] + [(d, flip(z, 1))])
    gains = [pltpu.make_async_remote_copy(src_ref=gp_s.at[d], dst_ref=gp_s.at[d], send_sem=gsend.at[j], recv_sem=grecv.at[j],
                                          device_id=(o, z), device_id_type=MESH) for j, o in enumerate(others)]
    for c in gains: c.start()
    G[0].begin()
    stage = []
    for i, (f_s, b_s) in enumerate(((of_s, ost_s), (gf_s, gst_s), (df_s, dst_s))):
        loads[i].wait()
        b_s[...] = f_s[...].astype(bf16)
        g = G[i+1]
        c = pltpu.make_async_copy(b_s, g.view(g.ref, d, "all"), loc.at[3+i]); c.start()
        stage.append(c)
    outs = []
    def out(src, dst):
        c = pltpu.make_async_copy(src, dst, loc.at[6 + len(outs)]); c.start(); outs.append(c)
    def weights_in():
        G[0].first()
        for i in range(3):
            stage[i].wait(); G[1+i].begin()
        G[0].second(); G[0].third(); G[0].sibling()
        out(wq_s, wq_o)
    def gain_of():
        for c in gains: c.wait_recv()
        full = spread_gain(gp_s[...], D)
        gain8_ref[...] = full
        return full[0:1, :]
    def hook(at):
        if at == "proj":
            out(qT_s, qT_o); out(kT_s, kT_o); out(vT_s, vT_o)
        elif at == 1:
            G[1].first(); G[2].first()
        elif at == 2:
            G[3].first(); G[1].second(); G[1].third(); G[2].second()
        elif at == 3:
            out(oT_s, oT_o)
            G[2].third(); G[3].second(); G[3].third()
            for g in G[1:]: g.sibling()
    forward_attention(lens_ref, x_ref, freq_ref, gain_of, weights_in, wq_s, qT_s, kT_s, vT_s, oT_s, lse_ref, cos_ref, sin_ref, segc_ref, segr_ref, bias_s, hook)
    for c in gains: c.wait_send()
    for g in G: g.sent()
    for c in outs: c.wait()

def ka(n_dp, n_rep, lens, x, freq, gain_piece, qw, ow, gw, dw):
    S, D = x.shape
    FF = gw.shape[2]
    sh = lambda s, d: jax.ShapeDtypeStruct(s, d)
    return pl.pallas_call(functools.partial(ka_body, (n_dp, n_rep)),
        in_specs=[SM, VM, VM, VM, VM, ANY, ANY, ANY], out_specs=[ANY]*4+[VM]*6+[ANY]*4,
        out_shape=[sh((D,S),bf16)]*4 + [sh((16,S),f32), sh((32,S),f32), sh((32,S),f32), sh((S,128),f32), sh((8,S),f32), sh((8,D),f32),
                   sh((3,D,D),bf16), sh((D,D),bf16), sh((2,D,FF),bf16), sh((FF,D),bf16)],
        scratch_shapes=[pltpu.VMEM((D,S),bf16)]*4 + [pltpu.VMEM((768,256),f32), pltpu.VMEM((3,D,D),bf16),
                        pltpu.VMEM(ow.shape,bf16), pltpu.VMEM(gw.shape,bf16), pltpu.VMEM(dw.shape,bf16),
                        pltpu.VMEM(ow.shape,f32), pltpu.VMEM(gw.shape,f32), pltpu.VMEM(dw.shape,f32), pltpu.VMEM((n_dp,8,128),f32),
                        pltpu.SemaphoreType.DMA((4,15)), pltpu.SemaphoreType.DMA((4,15)), pltpu.SemaphoreType.DMA((n_dp-1,)), pltpu.SemaphoreType.DMA((n_dp-1,)),
                        pltpu.SemaphoreType.DMA((16,))],
        compiler_params=pltpu.CompilerParams(collective_id=0, has_side_effects=True, vmem_limit_bytes=62*2**20),
        cost_estimate=pl.CostEstimate(flops=12*10**9, bytes_accessed=30*10**6, transcendentals=7*10**6),
        name="gather_attend")(lens, x, freq, gain_piece, qw, ow, gw, dw)

def local_body(lens_ref, x_ref, freq_ref, gain_ref, w_ref, qT_ref, kT_ref, vT_ref, oT_ref, lse_ref, cos_ref, sin_ref, segc_ref, segr_ref, bias_s):
    forward_attention(lens_ref, x_ref, freq_ref, lambda: gain_ref[0:1, :], lambda: None, w_ref, qT_ref, kT_ref, vT_ref, oT_ref,
                      lse_ref, cos_ref, sin_ref, segc_ref, segr_ref, bias_s, lambda at: None)

def attn_fwd(lens, x, gains, freq, wqkv):
    S, D = x.shape
    sh = lambda s, d: jax.ShapeDtypeStruct(s, d)
    return pl.pallas_call(local_body,
        in_specs=[SM]+[VM]*4, out_specs=[VM]*9,
        out_shape=[sh((D,S),bf16)]*4 + [sh((16,S),f32), sh((32,S),f32), sh((32,S),f32), sh((S,128),f32), sh((8,S),f32)],
        scratch_shapes=[pltpu.VMEM((768,256),f32)],
        compiler_params=pltpu.CompilerParams(vmem_limit_bytes=62*2**20), name="attend")(lens, x, freq, gains, wqkv)

def adam_step(weight, grad_sum, moment, second, rate, decay):
    moment_new = beta_one * moment + (1.0 - beta_one) * grad_sum
    second_new = beta_two * second + (1.0 - beta_two) * grad_sum * grad_sum
    moment_hat = moment_new / (1.0 - beta_one**STEP)
    second_hat = second_new / (1.0 - beta_two**STEP)
    weight_new = weight - rate * (moment_hat / (jnp.sqrt(second_hat) + adam_eps) + decay * weight)
    return (moment_new, second_new, weight_new)


def per_device(tokens, seg_lens, cotangent, qkv_w, out_w, gu_w, down_w, gains,
               qkv_m, qkv_v, out_m, out_v, gu_m, gu_v, down_m, down_v, gain_m, gain_v):
    _, S, D = tokens.shape
    x = tokens.reshape(S, D)
    cot = cotangent.reshape(S, D)
    gain_low = gains.astype(bf16)
    freq = 10000.0 ** (-jnp.arange(HD // 2, dtype=f32) / (HD // 2))
    freq = jnp.broadcast_to(freq[:, None], (HD // 2, 128))
    n_dp, n_rep = lax.axis_size("dp"), lax.axis_size("rep")
    if can_gather(n_dp, n_rep, qkv_w.shape[1], out_w.shape[0], gu_w.shape[1], down_w.shape[0]):
        piece = jnp.pad(gain_low.astype(f32), ((0, 6), (0, 128 - gains.shape[1])))
        qT, kT, vT, oT, lse, cos, sin, segc, segr, gain8, wqkv, wo, wgu, wd = ka(
            n_dp, n_rep, seg_lens, x, freq, piece, qkv_w, out_w, gu_w, down_w)
    else:
        wqkv = lax.all_gather(qkv_w.astype(bf16), "dp", axis=1, tiled=True)
        gain_full = lax.all_gather(gain_low, "dp", axis=1, tiled=True).astype(f32)
        wo = lax.all_gather(out_w.astype(bf16), "dp", axis=0, tiled=True)
        wgu = lax.all_gather(gu_w.astype(bf16), "dp", axis=1, tiled=True)
        wd = lax.all_gather(down_w.astype(bf16), "dp", axis=0, tiled=True)
        gain8 = jnp.pad(gain_full, ((0, 6), (0, 0)))
        qT, kT, vT, oT, lse, cos, sin, segc, segr = attn_fwd(seg_lens, x, gain8, freq, wqkv)
    ob = oT.T
    output, dmid, dob, dobT, dwo, dwgu, dwd = mlp(x, ob, oT, cot, wo, wgu, wd, gain8)
    input_grad, dwqkv = attn_bwd(x, gain8, wqkv, dmid, qT, kT, vT, dob, dobT, oT, lse, cos, sin, segc, segr)

    def owned(grad, axis):
        part = lax.psum_scatter(grad, "dp", scatter_dimension=axis, tiled=True)
        return lax.psum(part.astype(f32), "rep")

    g_down = owned(dwd, 0)
    g_gu = owned(dwgu, 1)
    g_out = owned(dwo, 0)
    g_qkv = owned(dwqkv, 1)
    gain_f = gain_low.astype(f32)
    g_gain = jnp.stack([
        jnp.sum(g_qkv * qkv_w.astype(bf16).astype(f32), axis=(0, 2)) / gain_f[0],
        jnp.sum(g_gu * gu_w.astype(bf16).astype(f32), axis=(0, 2)) / gain_f[1],
    ])
    qkv_res = adam_step(qkv_w, g_qkv, qkv_m, qkv_v, matrix_rate, weight_decay)
    out_res = adam_step(out_w, g_out, out_m, out_v, matrix_rate, weight_decay)
    gu_res = adam_step(gu_w, g_gu, gu_m, gu_v, matrix_rate, weight_decay)
    down_res = adam_step(down_w, g_down, down_m, down_v, matrix_rate, weight_decay)
    gain_res = adam_step(gains, g_gain, gain_m, gain_v, gain_rate, 0.0)
    return (output.reshape(tokens.shape), input_grad.reshape(tokens.shape)) + qkv_res + out_res + gu_res + down_res + gain_res


def solution(mesh):
    rows, cols, vec = P(("dp", "rep"), None, None), P(None, "dp", None), P("dp", None)
    small = P(None, "dp")
    return jax.shard_map(
        per_device,
        mesh=mesh,
        in_specs=(rows, P(("dp", "rep"), None), rows, cols, vec, cols, vec, small,
                  cols, cols, vec, vec, cols, cols, vec, vec, small, small),
        out_specs=(rows, rows) + (cols,) * 3 + (vec,) * 3 + (cols,) * 3 + (vec,) * 3 + (small,) * 3,
        check_vma=False,
    )
```

```python
import functools

import jax
import jax.numpy as jnp
from jax import lax
from jax.experimental import pallas as pl
from jax.experimental.pallas import tpu as pltpu
from jax.sharding import PartitionSpec as P

bf16, f32 = jnp.bfloat16, jnp.float32
STEP = 10
beta_one, beta_two, adam_eps = 0.9, 0.95, 1e-08
weight_decay, matrix_rate, gain_rate = 0.05, 0.1, 0.3
EPS = 1e-5
def nn(a,b): return lax.dot_general(a,b,(((1,),(0,)),((),())),preferred_element_type=f32)
def nt(a,b): return lax.dot_general(a,b,(((1,),(1,)),((),())),preferred_element_type=f32)
def tn(a,b): return lax.dot_general(a,b,(((0,),(0,)),((),())),preferred_element_type=f32)

def mlp_kernel(T, x_ref, ob_ref, obT_ref, cot_ref, wo_ref, wgu_ref, wd_ref, gain_ref,
               out_ref, dmid_ref, dob_ref, dobT_ref, dwo_ref, dwgu_ref, dwd_ref,
               h2_s, h2T_s, dfb_s, dh2_s, r_s, hid_s, dg_s, du_s):
    f = pl.program_id(0); nf = pl.num_programs(0)
    S = x_ref.shape[0]; nt_ = S // T
    gain = gain_ref[1:2, :]
    @pl.when(f == 0)
    def _():
        @pl.loop(0, nt_)
        def _(i):
            t = pl.ds(pl.multiple_of(i*T, T), T)
            mid = x_ref[t, :].astype(f32) + nn(ob_ref[t, :], wo_ref[...])
            out_ref[t, :] = mid
            dmid_ref[t, :] = mid
            r = lax.rsqrt(jnp.mean(mid*mid, axis=-1, keepdims=True) + EPS)
            r_s[t, :] = jnp.broadcast_to(r, (T, 128))
            h2 = ((mid*r)*gain).astype(bf16)
            h2_s[t, :] = h2
            h2T_s[:, t] = h2.T
            dfb_s[t, :] = cot_ref[t, :].astype(bf16)
            dh2_s[t, :] = jnp.zeros_like(mid)
    @pl.loop(0, nt_)
    def _(i):
        t = pl.ds(pl.multiple_of(i*T, T), T)
        h2 = h2_s[t, :]; dfb = dfb_s[t, :]
        g = nn(h2, wgu_ref[0]); u = nn(h2, wgu_ref[1])
        dh = nt(dfb, wd_ref[...])
        sig = 0.5*jnp.tanh(0.5*g)+0.5
        silu = g*sig
        hid = (silu*u).astype(bf16)
        dg = (dh*u*(sig*(1.0+g*(1.0-sig)))).astype(bf16)
        du = (dh*silu).astype(bf16)
        hid_s[t, :] = hid; dg_s[t, :] = dg; du_s[t, :] = du
        out_ref[t, :] += nn(hid, wd_ref[...])
        dh2_s[t, :] += nt(dg, wgu_ref[0]) + nt(du, wgu_ref[1])
    dwd_ref[...] = tn(hid_s[...], dfb_s[...]).astype(bf16)
    dwgu_ref[0] = nn(h2T_s[...], dg_s[...]).astype(bf16)
    dwgu_ref[1] = nn(h2T_s[...], du_s[...]).astype(bf16)
    @pl.when(f == nf-1)
    def _():
        @pl.loop(0, nt_)
        def _(i):
            t = pl.ds(pl.multiple_of(i*T, T), T)
            mid = dmid_ref[t, :]; r = r_s[t, 0:1]
            xh = mid*r; dh = dh2_s[t, :]; w = dh*gain
            back = r*(w - xh*jnp.mean(w*xh, axis=-1, keepdims=True))
            dmid = cot_ref[t, :] + back
            dmid_ref[t, :] = dmid
            dab = dmid.astype(bf16)
            h2_s[t, :] = dab
            dob_ref[t, :] = nt(dab, wo_ref[...]).astype(bf16)
            dobT_ref[:, t] = nt(wo_ref[...], dab).astype(bf16)
        dwo_ref[...] = nn(obT_ref[...], h2_s[...]).astype(bf16)

def mlp(x, ob, obT, cot, wo, wgu, wd, gains, FC=512, T=256):
    S, D = x.shape; FF = wd.shape[0]
    full = lambda *s: pl.BlockSpec(s, lambda f: (0,)*len(s), pipeline_mode=pl.Buffered(1))
    return pl.pallas_call(
        functools.partial(mlp_kernel, T), grid=(FF//FC,),
        in_specs=[full(S,D), full(S,D), full(D,S), full(S,D), full(D,D),
                  pl.BlockSpec((2,D,FC), lambda f:(0,0,f)), pl.BlockSpec((FC,D), lambda f:(f,0)), full(8,D)],
        out_specs=[full(S,D), full(S,D), full(S,D), full(D,S), full(D,D),
                  pl.BlockSpec((2,D,FC), lambda f:(0,0,f)), pl.BlockSpec((FC,D), lambda f:(f,0))],
        out_shape=[jax.ShapeDtypeStruct((S,D),f32), jax.ShapeDtypeStruct((S,D),f32), jax.ShapeDtypeStruct((S,D),bf16),
                   jax.ShapeDtypeStruct((D,S),bf16), jax.ShapeDtypeStruct((D,D),bf16),
                   jax.ShapeDtypeStruct((2,D,FF),bf16), jax.ShapeDtypeStruct((FF,D),bf16)],
        scratch_shapes=[pltpu.VMEM((S,D),bf16), pltpu.VMEM((D,S),bf16), pltpu.VMEM((S,D),bf16), pltpu.VMEM((S,D),f32),
                        pltpu.VMEM((S,128),f32), pltpu.VMEM((S,FC),bf16), pltpu.VMEM((S,FC),bf16), pltpu.VMEM((S,FC),bf16)],
        compiler_params=pltpu.CompilerParams(vmem_limit_bytes=62*2**20),
        name="mlp",
    )(x, ob, obT, cot, wo, wgu, wd, gains)

H, HD = 12, 64
NEG = -1e30
VM = pl.BlockSpec(memory_space=pltpu.VMEM)
def tnt(a,b): return lax.dot_general(a,b,(((0,),(1,)),((),())),preferred_element_type=f32)

def seg_rows(lens_ref, S):
    slot = lax.broadcasted_iota(jnp.int32, (8, S), 1)
    seg = jnp.zeros((8, S), jnp.int32); start = jnp.zeros((8, S), jnp.int32)
    end = jnp.int32(0)
    for s in range(lens_ref.shape[1]-1):
        end = end + lens_ref[0, s]
        past = (slot >= end).astype(jnp.int32)
        seg += past
        start += past * lens_ref[0, s]
    return seg, slot - start


MESH = pl.DeviceIdType.MESH

def flip(v, b):
    return v + b - 2*b*lax.rem(lax.div(v, b), 2)

def places():
    d = lax.axis_index("dp"); z = lax.axis_index("rep")
    sib, xn, yn = flip(d, 1), flip(d, 2), flip(d, 4)
    xy = flip(xn, 4)
    return d, z, sib, xn, yn, xy

def greet(devs):
    bar = pltpu.get_barrier_semaphore()
    for dev in devs:
        pl.semaphore_signal(bar, inc=1, device_id=dev, device_id_type=MESH)
    pl.semaphore_wait(bar, len(devs))

class Gather:
    N = 15
    def __init__(self, ref, view, send, recv, g):
        self.ref, self.view, self.send, self.recv, self.g = ref, view, send, recv, g
        d, z, sib, xn, yn, xy = places()
        zn = flip(z, 1)
        S, X, Y, Z = (sib, z), (xn, z), (yn, z), (d, zn)
        self.moves = [(d, "all", S), (d, "zb", X), (d, "zb", Y),
                      (xn, "zb", S), (xn, "z", Y), (xn, "z", Z),
                      (yn, "zb", S), (yn, "b", X), (yn, "z", Z),
                      (xy, "z", S), (xy, "z", Z), (xy, "b", S),
                      (xn, "o", S), (yn, "o", S), (xy, "o", S)]
        self.after = {1: (3, 4, 5), 2: (6, 7, 8), 4: (9, 10), 7: (11,), 5: (12,), 8: (13,), 10: (14,)}
    def copy(self, k):
        d, part, dev = self.moves[k]
        v = self.view(self.ref, d, part)
        return pltpu.make_async_remote_copy(src_ref=v, dst_ref=v, send_sem=self.send.at[self.g, k], recv_sem=self.recv.at[self.g, k],
                                            device_id=dev, device_id_type=MESH)
    def begin(self):
        for k in (1, 2, 0): self.copy(k).start()
    def got(self, *ks):
        for k in ks:
            self.copy(k).wait_recv()
            for j in self.after.get(k, ()): self.copy(j).start()
    def first(self): self.got(1, 2)
    def second(self): self.got(4, 7, 5, 8)
    def third(self): self.got(10)
    def sibling(self): self.got(0, 3, 6, 9, 11, 12, 13, 14)
    def sent(self):
        for k in range(self.N): self.copy(k).wait_send()

def row_view(rows, a, lead):
    z = lax.axis_index("rep"); p = lax.rem(z, 2)
    def view(ref, d, part):
        off, n = {"all": (0, rows), "zb": (p*a, rows - a), "z": (p*(rows - a), a), "b": (a, rows - 2*a), "o": ((1 - p)*(rows - a), a)}[part]
        s = pl.ds(pl.multiple_of(d*rows + off, 16), n)
        return ref.at[:, s, :] if lead else ref.at[s, :]
    return view

def cut(rows):
    return rows // 3 // 16 * 16

def can_gather(mesh_dp, mesh_rep, *rows):
    return mesh_dp == 8 and mesh_rep % 2 == 0 and all(r % 16 == 0 and cut(r) > 0 for r in rows)

ANY = pl.BlockSpec(memory_space=pl.ANY)
SM = pl.BlockSpec(memory_space=pltpu.SMEM)
B = 256

def spread_gain(pieces, D):
    n, wide = pieces.shape[0], D // pieces.shape[0]
    r = lax.broadcasted_iota(jnp.int32, (n*128, D), 0); c = lax.broadcasted_iota(jnp.int32, (n*128, D), 1)
    pick = (c == lax.div(r, 128)*wide + lax.rem(r, 128)) & (lax.rem(r, 128) < wide)
    flat = jnp.concatenate([pieces[i] for i in range(n)], axis=1).astype(bf16)
    return nn(flat, jnp.where(pick, 1.0, 0.0).astype(bf16))

def forward_attention(lens_ref, x_ref, freq_ref, gain_of, weights_in, w_ref, qT_s, kT_s, vT_s, oT_s, lse_s, cos_s, sin_s, segc_s, segr_s, bias_s, hook):
    S, D = x_ref.shape
    n = S // B
    seg, place = seg_rows(lens_ref, S)
    ang = jnp.broadcast_to(place[0:1, :].astype(f32), (HD//2, S)) * freq_ref[:, 0:1]
    cos_s[...] = jnp.cos(ang); sin_s[...] = jnp.sin(ang)
    segf = jnp.broadcast_to(seg[0:1, :].astype(f32), (128, S))
    segr_s[...] = segf[0:8]
    segc_s[...] = segf.T
    weights_in()
    gain = gain_of()
    @pl.loop(0, n)
    def _(i):
        t = pl.ds(pl.multiple_of(i*B, B), B)
        xf = x_ref[t, :].astype(f32)
        r = lax.rsqrt(jnp.mean(xf*xf, axis=-1, keepdims=True) + EPS)
        h1 = ((xf*r)*gain).astype(bf16)
        c = cos_s[:, t]; s = sin_s[:, t]
        for w, dst, sc in ((0, qT_s, 0.125), (1, kT_s, 1.0)):
            y = tnt(w_ref[w], h1)
            for h in range(H):
                a = y[h*HD:h*HD+32]; b = y[h*HD+32:h*HD+64]
                dst[h*HD:h*HD+32, t] = ((a*c - b*s)*sc).astype(bf16)
                dst[h*HD+32:h*HD+64, t] = ((b*c + a*s)*sc).astype(bf16)
        vT_s[:, t] = tnt(w_ref[2], h1).astype(bf16)
    hook("proj")
    for i in range(n):
        k0 = max(0, i-2)*B; nk = i*B + B - k0
        q0 = i*B
        kid = lax.broadcasted_iota(jnp.int32, (nk, B), 0) + k0
        qid = lax.broadcasted_iota(jnp.int32, (nk, B), 1) + q0
        ok = (segc_s[k0:k0+nk, 0:1] == segr_s[0:1, q0:q0+B]) & (kid <= qid)
        bias_s[0:nk, :] = jnp.where(ok, 0.0, NEG)
        @pl.loop(0, H//2)
        def _(p):
            for e in range(2):
                rows = pl.ds(pl.multiple_of(p*128 + e*64, 64), 64)
                s = tn(kT_s[rows, k0:k0+nk], qT_s[rows, q0:q0+B]) + bias_s[0:nk, :]
                m = jnp.max(s, axis=0, keepdims=True)
                ex = jnp.exp(s - m)
                l = jnp.sum(ex, axis=0, keepdims=True)
                o = nn(vT_s[rows, k0:k0+nk], ex.astype(bf16)) * (1.0/l)
                oT_s[rows, q0:q0+B] = o.astype(bf16)
                lse_s[pl.ds(p*2+e, 1), q0:q0+B] = m + jnp.log(l)
        hook(i)

def ka_body(sizes, lens_ref, x_ref, freq_ref, gain_ref, qw_ref, ow_ref, gw_ref, dw_ref,
            qT_o, kT_o, vT_o, oT_o, lse_ref, cos_ref, sin_ref, segc_ref, segr_ref, gain8_ref, wq_o, wo_o, wgu_o, wd_o,
            qT_s, kT_s, vT_s, oT_s, bias_s, wq_s, ost_s, gst_s, dst_s, of_s, gf_s, df_s, gp_s, send, recv, gsend, grecv, loc):
    n_dp, n_rep = sizes
    D = x_ref.shape[1]
    d, z, sib, xn, yn, xy = places()
    others = [lax.rem(d + j, n_dp) for j in range(1, n_dp)]
    loads = [pltpu.make_async_copy(a, b, loc.at[i]) for i, (a, b) in enumerate(((ow_ref, of_s), (gw_ref, gf_s), (dw_ref, df_s)))]
    for c in loads: c.start()
    gp_s[pl.ds(d, 1)] = gain_ref[...].reshape(1, 8, 128)
    rq, ro, rg, rd = qw_ref.shape[1], ow_ref.shape[0], gw_ref.shape[1], dw_ref.shape[0]
    G = [Gather(full, row_view(r, cut(r), ld), send, recv, g)
         for g, (full, r, ld) in enumerate(((wq_s, rq, True), (wo_o, ro, False), (wgu_o, rg, True), (wd_o, rd, False)))]
    wq_s[:, pl.ds(pl.multiple_of(d*rq, 16), rq), :] = qw_ref[...].astype(bf16)
    greet([(o, z) for o in others] + [(d, flip(z, 1))])
    gains = [pltpu.make_async_remote_copy(src_ref=gp_s.at[d], dst_ref=gp_s.at[d], send_sem=gsend.at[j], recv_sem=grecv.at[j],
                                          device_id=(o, z), device_id_type=MESH) for j, o in enumerate(others)]
    for c in gains: c.start()
    G[0].begin()
    stage = []
    for i, (f_s, b_s) in enumerate(((of_s, ost_s), (gf_s, gst_s), (df_s, dst_s))):
        loads[i].wait()
        b_s[...] = f_s[...].astype(bf16)
        g = G[i+1]
        c = pltpu.make_async_copy(b_s, g.view(g.ref, d, "all"), loc.at[3+i]); c.start()
        stage.append(c)
    outs = []
    def out(src, dst):
        c = pltpu.make_async_copy(src, dst, loc.at[6 + len(outs)]); c.start(); outs.append(c)
    def weights_in():
        G[0].first()
        for i in range(3):
            stage[i].wait(); G[1+i].begin()
        G[0].second(); G[0].third(); G[0].sibling()
        out(wq_s, wq_o)
    def gain_of():
        for c in gains: c.wait_recv()
        full = spread_gain(gp_s[...], D)
        gain8_ref[...] = full
        return full[0:1, :]
    def hook(at):
        if at == "proj":
            out(qT_s, qT_o); out(kT_s, kT_o); out(vT_s, vT_o)
        elif at == 1:
            G[1].first(); G[2].first()
        elif at == 2:
            G[3].first(); G[1].second(); G[1].third(); G[2].second()
        elif at == 3:
            out(oT_s, oT_o)
            G[2].third(); G[3].second(); G[3].third()
            for g in G[1:]: g.sibling()
    forward_attention(lens_ref, x_ref, freq_ref, gain_of, weights_in, wq_s, qT_s, kT_s, vT_s, oT_s, lse_ref, cos_ref, sin_ref, segc_ref, segr_ref, bias_s, hook)
    for c in gains: c.wait_send()
    for g in G: g.sent()
    for c in outs: c.wait()

def ka(n_dp, n_rep, lens, x, freq, gain_piece, qw, ow, gw, dw):
    S, D = x.shape
    FF = gw.shape[2]
    sh = lambda s, d: jax.ShapeDtypeStruct(s, d)
    return pl.pallas_call(functools.partial(ka_body, (n_dp, n_rep)),
        in_specs=[SM, VM, VM, VM, VM, ANY, ANY, ANY], out_specs=[ANY]*4+[VM]*6+[ANY]*4,
        out_shape=[sh((D,S),bf16)]*4 + [sh((16,S),f32), sh((32,S),f32), sh((32,S),f32), sh((S,128),f32), sh((8,S),f32), sh((8,D),f32),
                   sh((3,D,D),bf16), sh((D,D),bf16), sh((2,D,FF),bf16), sh((FF,D),bf16)],
        scratch_shapes=[pltpu.VMEM((D,S),bf16)]*4 + [pltpu.VMEM((768,256),f32), pltpu.VMEM((3,D,D),bf16),
                        pltpu.VMEM(ow.shape,bf16), pltpu.VMEM(gw.shape,bf16), pltpu.VMEM(dw.shape,bf16),
                        pltpu.VMEM(ow.shape,f32), pltpu.VMEM(gw.shape,f32), pltpu.VMEM(dw.shape,f32), pltpu.VMEM((n_dp,8,128),f32),
                        pltpu.SemaphoreType.DMA((4,15)), pltpu.SemaphoreType.DMA((4,15)), pltpu.SemaphoreType.DMA((n_dp-1,)), pltpu.SemaphoreType.DMA((n_dp-1,)),
                        pltpu.SemaphoreType.DMA((16,))],
        compiler_params=pltpu.CompilerParams(collective_id=0, has_side_effects=True, vmem_limit_bytes=62*2**20),
        cost_estimate=pl.CostEstimate(flops=12*10**9, bytes_accessed=30*10**6, transcendentals=7*10**6),
        name="gather_attend")(lens, x, freq, gain_piece, qw, ow, gw, dw)

def local_body(lens_ref, x_ref, freq_ref, gain_ref, w_ref, qT_ref, kT_ref, vT_ref, oT_ref, lse_ref, cos_ref, sin_ref, segc_ref, segr_ref, bias_s):
    forward_attention(lens_ref, x_ref, freq_ref, lambda: gain_ref[0:1, :], lambda: None, w_ref, qT_ref, kT_ref, vT_ref, oT_ref,
                      lse_ref, cos_ref, sin_ref, segc_ref, segr_ref, bias_s, lambda at: None)

def attn_fwd(lens, x, gains, freq, wqkv):
    S, D = x.shape
    sh = lambda s, d: jax.ShapeDtypeStruct(s, d)
    return pl.pallas_call(local_body,
        in_specs=[SM]+[VM]*4, out_specs=[VM]*9,
        out_shape=[sh((D,S),bf16)]*4 + [sh((16,S),f32), sh((32,S),f32), sh((32,S),f32), sh((S,128),f32), sh((8,S),f32)],
        scratch_shapes=[pltpu.VMEM((768,256),f32)],
        compiler_params=pltpu.CompilerParams(vmem_limit_bytes=62*2**20), name="attend")(lens, x, freq, gains, wqkv)

GW = 256

def backward_attention(x_ref, gain_ref, w_ref, ig_s, ig_ready, ig_done, qT_ref, kT_ref, vT_ref, dob_ref, dobT_ref, lse_ref, cos_ref, sin_ref, segc_ref, segr_ref,
                       dw_s, bias_s, q_s, dqT_s, dk_s, dv_s, g_s, h1T_s, hook):
    S, D = x_ref.shape
    n = S // B
    gain = gain_ref[0:1, :]
    hook("start")
    blocks = []
    at = 0
    for i in range(n):
        k0 = max(0, i-2)*B; nk = i*B + B - k0
        q0 = i*B
        kid = lax.broadcasted_iota(jnp.int32, (nk, B), 0) + k0
        qid = lax.broadcasted_iota(jnp.int32, (nk, B), 1) + q0
        ok = (segc_ref[k0:k0+nk, 0:1] == segr_ref[0:1, q0:q0+B]) & (kid <= qid)
        bias_s[at:at+nk, :] = jnp.where(ok, 0.0, NEG)
        blocks.append((q0, k0, nk, at)); at += nk
    q_s[...] = qT_ref[...].T
    @pl.loop(0, n)
    def _(i):
        t = pl.ds(pl.multiple_of(i*B, B), B)
        xf = x_ref[t, :].astype(f32)
        r = lax.rsqrt(jnp.mean(xf*xf, axis=-1, keepdims=True) + EPS)
        h1T_s[:, t] = ((xf*r)*gain).astype(bf16).T
    hook("ready")
    lane = lax.broadcasted_iota(jnp.int32, (B, 128), 1)
    @pl.loop(0, H//2)
    def _(p):
        cols = pl.ds(pl.multiple_of(p*128, 128), 128)
        dk_s[...] = jnp.zeros_like(dk_s); dv_s[...] = jnp.zeros_like(dv_s)
        for q0, k0, nk, at in blocks:
            dv = dk = None
            for e in range(2):
                rows = pl.ds(pl.multiple_of(p*128 + e*64, 64), 64)
                mine = (lane < 64) if e == 0 else (lane >= 64)
                dobz = jnp.where(mine, dob_ref[q0:q0+B, cols], 0).astype(bf16)
                qz = jnp.where(mine, q_s[q0:q0+B, cols], 0).astype(bf16)
                s = tn(kT_ref[rows, k0:k0+nk], qT_ref[rows, q0:q0+B]) + bias_s[at:at+nk, :]
                pr = jnp.exp(s - lse_ref[pl.ds(p*2+e, 1), q0:q0+B])
                dp = tn(vT_ref[rows, k0:k0+nk], dobT_ref[rows, q0:q0+B])
                inner = jnp.sum(pr*dp, axis=0, keepdims=True)
                ds = (pr*(dp - inner)).astype(bf16)
                dve = nn(pr.astype(bf16), dobz)
                dke = nn(ds, qz)
                dqT_s[e*64:e*64+64, q0:q0+B] = nn(kT_ref[rows, k0:k0+nk], ds) * 0.125
                dv = dve if dv is None else dv + dve
                dk = dke if dk is None else dk + dke
            dv_s[k0:k0+nk, :] += dv
            dk_s[k0:k0+nk, :] += dk
        c = cos_ref[...]; s = sin_ref[...]
        for j, src in ((0, dqT_s[...]), (1, dk_s[...].T)):
            parts = []
            for e in range(2):
                a = src[e*HD:e*HD+32]; b = src[e*HD+32:e*HD+64]
                parts += [a*c + b*s, b*c - a*s]
            g_s[j, :, cols] = jnp.concatenate(parts, axis=0).astype(bf16).T
        g_s[2, :, cols] = dv_s[...].astype(bf16)
        @pl.when(lax.rem(p, 2) == 1)
        def _():
            g = lax.div(p, 2)
            wide = pl.ds(pl.multiple_of(g*GW, GW), GW)
            for j in range(3):
                dw_s[g, j] = nn(h1T_s[...], g_s[j, :, wide]).astype(bf16)
        for k in range(H//2):
            @pl.when(p == k)
            def _():
                hook(k)
    ig_ready()
    for i in range(n):
        t = pl.ds(i*B, B)
        xf = x_ref[t, :].astype(f32)
        r = lax.rsqrt(jnp.mean(xf*xf, axis=-1, keepdims=True) + EPS)
        xh = xf*r
        dh = nt(g_s[0, t, :], w_ref[0]) + nt(g_s[1, t, :], w_ref[1]) + nt(g_s[2, t, :], w_ref[2])
        w = dh*gain
        ig_s[t, :] += r*(w - xh*jnp.mean(w*xh, axis=-1, keepdims=True))
        ig_done(i, t)
        hook("tile%d" % i)

def scratch_bwd(S, D):
    n = S // B
    area = sum(min(i+1, 3) for i in range(n))*B
    return [pltpu.VMEM((D//GW, 3, D, GW), bf16), pltpu.VMEM((area, B), f32), pltpu.VMEM((S, D), bf16), pltpu.VMEM((128, S), f32),
            pltpu.VMEM((S, 128), f32), pltpu.VMEM((S, 128), f32), pltpu.VMEM((3, S, D), bf16), pltpu.VMEM((D, S), bf16)]

def bwd_local_body(x_ref, gain_ref, w_ref, dmid_ref, qT_ref, kT_ref, vT_ref, dob_ref, dobT_ref, lse_ref, cos_ref, sin_ref, segc_ref, segr_ref,
                   ig_ref, dw_ref, bias_s, q_s, dqT_s, dk_s, dv_s, g_s, h1T_s):
    ig_ref[...] = dmid_ref[...]
    backward_attention(x_ref, gain_ref, w_ref, ig_ref, lambda: None, lambda i, t: None, qT_ref, kT_ref, vT_ref, dob_ref, dobT_ref, lse_ref, cos_ref, sin_ref,
                       segc_ref, segr_ref, dw_ref, bias_s, q_s, dqT_s, dk_s, dv_s, g_s, h1T_s, lambda at: None)

def attn_bwd(x, gains, wqkv, dmid, qT, kT, vT, dob, dobT, lse, cos, sin, segc, segr):
    S, D = x.shape
    sh = lambda s, d: jax.ShapeDtypeStruct(s, d)
    ig, dw = pl.pallas_call(bwd_local_body,
        in_specs=[VM]*14, out_specs=[VM]*2,
        out_shape=[sh((S,D),f32), sh((D//GW,3,D,GW),bf16)],
        scratch_shapes=scratch_bwd(S, D)[1:],
        compiler_params=pltpu.CompilerParams(vmem_limit_bytes=62*2**20), name="attend_back")(x, gains, wqkv, dmid, qT, kT, vT, dob, dobT, lse, cos, sin, segc, segr)
    return ig, jnp.moveaxis(dw, 0, 2).reshape(3, D, D)

class Reduce:
    N = 13
    def __init__(self, u, piece, other, own_load, rs, rx, r2, zr, tot, out, send, recv):
        self.u, self.piece, self.other, self.own_load = u, piece, other, own_load
        self.rs, self.rx, self.r2, self.zr, self.tot, self.out, self.send, self.recv = rs, rx, r2, zr, tot, out, send, recv
        self.d, self.z, self.sib, self.xn, self.yn, self.xy = places()
        self.rows = rs.shape[-2]; self.half = self.rows // 2
        self.inner = (self.z == 1) | (self.z == 2)
    def cut(self, ref, h):
        s = slice(0, self.half) if h == 0 else slice(self.half, self.rows)
        return ref.at[..., s, :]
    def copy(self, k, src, dst, dev):
        return pltpu.make_async_remote_copy(src_ref=src, dst_ref=dst, send_sem=self.send.at[self.u, k], recv_sem=self.recv.at[self.u, k],
                                            device_id=dev, device_id_type=MESH)
    def s_copy(self, j): return self.copy(j, self.other(j), self.rs.at[j], (self.sib, self.z))
    def x_copies(self):
        X, Y = (self.xn, self.z), (self.yn, self.z)
        return [self.copy(4, self.half_of(1, 0), self.cut(self.rx.at[0], 0), X), self.copy(5, self.half_of(3, 0), self.cut(self.rx.at[1], 0), X),
                self.copy(6, self.half_of(2, 1), self.cut(self.rx.at[0], 1), Y), self.copy(7, self.half_of(3, 1), self.cut(self.rx.at[1], 1), Y)]
    def half_of(self, j, h): return self.piece(j, h)
    def y_copies(self):
        return [self.copy(8, self.half_of(2, 0), self.cut(self.r2, 0), (self.yn, self.z)), self.copy(9, self.half_of(1, 1), self.cut(self.r2, 1), (self.xn, self.z))]
    def z_copy(self, k):
        zn = (self.d, flip(self.z, 1))
        if k == 0: return self.copy(10, self.piece(0, None), self.zr.at[0], zn)
        if k == 1: return self.copy(11, self.zr.at[0], self.zr.at[1], (self.d, 3 - self.z))
        return self.copy(12, self.tot, self.tot, zn)
    def add(self, dst, *refs):
        lead = dst.shape[0] if len(dst.shape) == 3 else None
        def one(i):
            g = (lambda r: r[...]) if i is None else (lambda r: r[i])
            v = g(refs[0]).astype(f32)
            for r in refs[1:]: v += g(r).astype(f32)
            if i is None: dst[...] = v.astype(bf16)
            else: dst[i] = v.astype(bf16)
        if lead is None: one(None)
        else:
            for i in range(lead): one(i)
    def start_s(self):
        for j in range(4): self.s_copy(j).start()
        if self.own_load:
            for j in range(4): self.own_load(j).start()
    def s2x(self):
        for j in (3, 1, 2, 0):
            self.s_copy(j).wait_recv()
            if self.own_load: self.own_load(j).wait()
            p = self.piece(j, None)
            self.add(p, p, self.rs.at[j])
        for c in self.x_copies(): c.start()
    def x2y(self):
        cs = self.x_copies()
        for c in cs: c.wait_recv()
        for j, h, r in ((2, 0, 1), (1, 1, 1)):
            p = self.piece(j, h)
            self.add(p, p, self.cut(self.rx.at[r], h))
        for c in self.y_copies(): c.start()
        p = self.piece(0, None)
        self.add(p, p, self.rx.at[0])
    def y2z(self):
        for c in self.y_copies(): c.wait_recv()
        p = self.piece(0, None)
        self.add(p, p, self.r2)
        @pl.when(jnp.logical_not(self.inner))
        def _(): self.z_copy(0).start()
    def z2(self):
        @pl.when(self.inner)
        def _():
            self.z_copy(0).wait_recv()
            self.add(self.zr.at[0], self.zr.at[0], self.piece(0, None))
            self.z_copy(1).start()
    def z3(self):
        @pl.when(self.inner)
        def _():
            self.z_copy(1).wait_recv()
            self.add(self.tot, self.zr.at[0], self.zr.at[1])
            self.z_copy(2).start()
            self.out().start()
    def last(self):
        @pl.when(jnp.logical_not(self.inner))
        def _():
            self.z_copy(2).wait_recv()
            self.out().start()
    def drain(self):
        for j in range(4): self.s_copy(j).wait_send()
        for c in self.x_copies() + self.y_copies(): c.wait_send()
        @pl.when(self.inner)
        def _():
            self.z_copy(1).wait_send(); self.z_copy(2).wait_send()
        @pl.when(jnp.logical_not(self.inner))
        def _(): self.z_copy(0).wait_send()
        self.out().wait()

def kc_body(x_ref, gain_ref, w_ref, qT_ref, kT_ref, vT_ref, dob_ref, dobT_ref, lse_ref, cos_ref, sin_ref, segc_ref, segr_ref, dmid_ref, dgu_ref, ddn_ref, dou_ref,
            ig_o, gq_o, ggu_o, gdn_o, gou_o,
            dw_s, bias_s, q_s, dqT_s, dk_s, dv_s, g_s, h1T_s, ig_s,
            gu_p, gu_rs, gu_rx, gu_r2, gu_z, gu_t, dn_p, dn_rs, dn_rx, dn_r2, dn_z, dn_t, ou_p, ou_rs, ou_rx, ou_r2, ou_z, ou_t, q_rs, q_rx, q_r2, q_z, q_t,
            send, recv, loc):
    S, D = x_ref.shape
    n = S // B
    d, z, sib, xn, yn, xy = places()
    owners = [d, xn, yn, xy]
    load = pltpu.make_async_copy(dmid_ref, ig_s, loc.at[0]); load.start()
    def rows_of(ref, o, r, lead):
        s = pl.ds(pl.multiple_of(o*r, 16), r)
        return ref.at[:, s, :] if lead else ref.at[s, :]
    def halves(r, h): return (0, r) if h is None else (h*(r//2), r//2)
    units = []
    for u, (ref, lead, p, rs, rx, r2, zr, tot, out) in enumerate(((ddn_ref, False, dn_p, dn_rs, dn_rx, dn_r2, dn_z, dn_t, gdn_o), (dgu_ref, True, gu_p, gu_rs, gu_rx, gu_r2, gu_z, gu_t, ggu_o),
                                                                 (dou_ref, False, ou_p, ou_rs, ou_rx, ou_r2, ou_z, ou_t, gou_o))):
        r = rs.shape[-2]
        def piece(j, h, p=p, r=r):
            o, m = halves(r, h)
            return p.at[j, ..., o:o+m, :]
        other = lambda j, ref=ref, r=r, lead=lead: rows_of(ref, flip(owners[j], 1), r, lead)
        own = lambda j, ref=ref, r=r, lead=lead, p=p, u=u: pltpu.make_async_copy(rows_of(ref, owners[j], r, lead), p.at[j], loc.at[1 + u*4 + j])
        fin = lambda tot=tot, out=out, u=u: pltpu.make_async_copy(tot, out, loc.at[16 + u])
        units.append(Reduce(u, piece, other, own, rs, rx, r2, zr, tot, fin, send, recv))
    r = q_rs.shape[-2]
    for g in range(D//GW):
        def piece(j, h, g=g):
            o, m = halves(r, h)
            return dw_s.at[g, :, pl.ds(pl.multiple_of(owners[j]*r + o, 16), m), :]
        other = lambda j, g=g: rows_of(dw_s.at[g], flip(owners[j], 1), r, True)
        fin = lambda g=g: pltpu.make_async_copy(q_t.at[g], gq_o.at[:, :, pl.ds(g*GW, GW)], loc.at[19 + g])
        units.append(Reduce(3+g, piece, other, None, q_rs.at[g], q_rx.at[g], q_r2.at[g], q_z.at[g], q_t.at[g], fin, send, recv))
    U = units
    def hook(at):
        if at == "start":
            greet([(sib, z), (xn, z), (yn, z), (d, flip(z, 1)), (d, 3 - z)])
            U[0].start_s(); U[1].start_s(); U[2].start_s()
        elif at == "ready": U[0].s2x()
        elif at == 0: U[1].s2x(); U[2].s2x()
        elif at == 1: U[3].start_s(); U[0].x2y()
        elif at == 2: U[3].s2x()
        elif at == 3: U[4].start_s(); U[1].x2y(); U[2].x2y()
        elif at == 4: U[4].s2x(); U[0].y2z(); U[3].x2y()
        elif at == 5: U[5].start_s(); U[0].z2(); U[1].y2z(); U[2].y2z(); U[4].x2y()
        elif at == "tile0": U[5].s2x(); U[0].z3(); U[3].y2z()
        elif at == "tile1": U[1].z2(); U[2].z2(); U[3].z2()
        elif at == "tile2": U[4].y2z(); U[0].last()
        elif at == "tile3":
            U[5].x2y(); U[4].z2(); U[1].z3(); U[2].z3(); U[3].z3(); U[5].y2z(); U[4].z3(); U[5].z2(); U[5].z3()
            for k in range(1, 6): U[k].last()
    def ig_out(i): return pltpu.make_async_copy(ig_s.at[pl.ds(i*B, B), :], ig_o.at[pl.ds(i*B, B), :], loc.at[24 + i])
    backward_attention(x_ref, gain_ref, w_ref, ig_s, load.wait, lambda i, t: ig_out(i).start(), qT_ref, kT_ref, vT_ref, dob_ref, dobT_ref, lse_ref, cos_ref, sin_ref,
                       segc_ref, segr_ref, dw_s, bias_s, q_s, dqT_s, dk_s, dv_s, g_s, h1T_s, hook)
    for u in U: u.drain()
    for i in range(n): ig_out(i).wait()

def kc(x, gains, wqkv, qT, kT, vT, dob, dobT, lse, cos, sin, segc, segr, dmid, dgu, ddn, dou, n_dp):
    S, D = x.shape
    FF = ddn.shape[0]
    sh = lambda s, d: jax.ShapeDtypeStruct(s, d)
    V = lambda *s: pltpu.VMEM(s, bf16)
    def bufs(*piece): return [V(4, *piece), V(4, *piece), V(2, *piece), V(*piece), V(2, *piece), V(*piece)]
    rq, rf = D//n_dp, FF//n_dp
    G = D//GW
    return pl.pallas_call(kc_body,
        in_specs=[VM]*13 + [ANY]*4, out_specs=[ANY]*5,
        out_shape=[sh((S,D),f32), sh((3,rq,D),bf16), sh((2,rq,FF),bf16), sh((rf,D),bf16), sh((rq,D),bf16)],
        scratch_shapes=scratch_bwd(S, D) + [pltpu.VMEM((S,D),f32)] + bufs(2,rq,FF) + bufs(rf,D) + bufs(rq,D)
            + [V(G,4,3,rq,GW), V(G,2,3,rq,GW), V(G,3,rq,GW), V(G,2,3,rq,GW), V(G,3,rq,GW)]
            + [pltpu.SemaphoreType.DMA((3+G,13)), pltpu.SemaphoreType.DMA((3+G,13)), pltpu.SemaphoreType.DMA((32,))],
        compiler_params=pltpu.CompilerParams(collective_id=1, has_side_effects=True, vmem_limit_bytes=62*2**20),
        cost_estimate=pl.CostEstimate(flops=20*10**9, bytes_accessed=50*10**6, transcendentals=7*10**6),
        name="attend_back_reduce")(x, gains, wqkv, qT, kT, vT, dob, dobT, lse, cos, sin, segc, segr, dmid, dgu, ddn, dou)

def can_reduce(n_dp, n_rep, *rows):
    return n_dp == 8 and n_rep == 4 and all(r % 32 == 0 for r in rows)

def adam_step(weight, grad_sum, moment, second, rate, decay):
    moment_new = beta_one * moment + (1.0 - beta_one) * grad_sum
    second_new = beta_two * second + (1.0 - beta_two) * grad_sum * grad_sum
    moment_hat = moment_new / (1.0 - beta_one**STEP)
    second_hat = second_new / (1.0 - beta_two**STEP)
    weight_new = weight - rate * (moment_hat / (jnp.sqrt(second_hat) + adam_eps) + decay * weight)
    return (moment_new, second_new, weight_new)


def per_device(tokens, seg_lens, cotangent, qkv_w, out_w, gu_w, down_w, gains,
               qkv_m, qkv_v, out_m, out_v, gu_m, gu_v, down_m, down_v, gain_m, gain_v):
    _, S, D = tokens.shape
    x = tokens.reshape(S, D)
    cot = cotangent.reshape(S, D)
    gain_low = gains.astype(bf16)
    freq = 10000.0 ** (-jnp.arange(HD // 2, dtype=f32) / (HD // 2))
    freq = jnp.broadcast_to(freq[:, None], (HD // 2, 128))
    n_dp, n_rep = lax.axis_size("dp"), lax.axis_size("rep")
    if can_gather(n_dp, n_rep, qkv_w.shape[1], out_w.shape[0], gu_w.shape[1], down_w.shape[0]):
        piece = jnp.pad(gain_low.astype(f32), ((0, 6), (0, 128 - gains.shape[1])))
        qT, kT, vT, oT, lse, cos, sin, segc, segr, gain8, wqkv, wo, wgu, wd = ka(
            n_dp, n_rep, seg_lens, x, freq, piece, qkv_w, out_w, gu_w, down_w)
    else:
        wqkv = lax.all_gather(qkv_w.astype(bf16), "dp", axis=1, tiled=True)
        gain_full = lax.all_gather(gain_low, "dp", axis=1, tiled=True).astype(f32)
        wo = lax.all_gather(out_w.astype(bf16), "dp", axis=0, tiled=True)
        wgu = lax.all_gather(gu_w.astype(bf16), "dp", axis=1, tiled=True)
        wd = lax.all_gather(down_w.astype(bf16), "dp", axis=0, tiled=True)
        gain8 = jnp.pad(gain_full, ((0, 6), (0, 0)))
        qT, kT, vT, oT, lse, cos, sin, segc, segr = attn_fwd(seg_lens, x, gain8, freq, wqkv)
    ob = oT.T
    output, dmid, dob, dobT, dwo, dwgu, dwd = mlp(x, ob, oT, cot, wo, wgu, wd, gain8)
    if can_reduce(n_dp, n_rep, qkv_w.shape[1], out_w.shape[0], gu_w.shape[1], down_w.shape[0]):
        input_grad, g_qkv, g_gu, g_down, g_out = kc(x, gain8, wqkv, qT, kT, vT, dob, dobT, lse, cos, sin, segc, segr, dmid, dwgu, dwd, dwo, n_dp)
        g_qkv, g_gu, g_down, g_out = (g.astype(f32) for g in (g_qkv, g_gu, g_down, g_out))
    else:
        input_grad, dwqkv = attn_bwd(x, gain8, wqkv, dmid, qT, kT, vT, dob, dobT, lse, cos, sin, segc, segr)

        def owned(grad, axis):
            part = lax.psum_scatter(grad, "dp", scatter_dimension=axis, tiled=True)
            return lax.psum(part.astype(f32), "rep")

        g_down = owned(dwd, 0)
        g_gu = owned(dwgu, 1)
        g_out = owned(dwo, 0)
        g_qkv = owned(dwqkv, 1)
    gain_f = gain_low.astype(f32)
    g_gain = jnp.stack([
        jnp.sum(g_qkv * qkv_w.astype(bf16).astype(f32), axis=(0, 2)) / gain_f[0],
        jnp.sum(g_gu * gu_w.astype(bf16).astype(f32), axis=(0, 2)) / gain_f[1],
    ])
    qkv_res = adam_step(qkv_w, g_qkv, qkv_m, qkv_v, matrix_rate, weight_decay)
    out_res = adam_step(out_w, g_out, out_m, out_v, matrix_rate, weight_decay)
    gu_res = adam_step(gu_w, g_gu, gu_m, gu_v, matrix_rate, weight_decay)
    down_res = adam_step(down_w, g_down, down_m, down_v, matrix_rate, weight_decay)
    gain_res = adam_step(gains, g_gain, gain_m, gain_v, gain_rate, 0.0)
    return (output.reshape(tokens.shape), input_grad.reshape(tokens.shape)) + qkv_res + out_res + gu_res + down_res + gain_res


def solution(mesh):
    rows, cols, vec = P(("dp", "rep"), None, None), P(None, "dp", None), P("dp", None)
    small = P(None, "dp")
    return jax.shard_map(
        per_device,
        mesh=mesh,
        in_specs=(rows, P(("dp", "rep"), None), rows, cols, vec, cols, vec, small,
                  cols, cols, vec, vec, cols, cols, vec, vec, small, small),
        out_specs=(rows, rows) + (cols,) * 3 + (vec,) * 3 + (cols,) * 3 + (vec,) * 3 + (small,) * 3,
        check_vma=False,
    )
```

```python
import functools

import jax
import jax.numpy as jnp
from jax import lax
from jax.experimental import pallas as pl
from jax.experimental.pallas import tpu as pltpu
from jax.sharding import PartitionSpec as P

bf16, f32 = jnp.bfloat16, jnp.float32
STEP = 10
beta_one, beta_two, adam_eps = 0.9, 0.95, 1e-08
weight_decay, matrix_rate, gain_rate = 0.05, 0.1, 0.3
EPS = 1e-5
def nn(a,b): return lax.dot_general(a,b,(((1,),(0,)),((),())),preferred_element_type=f32)
def nt(a,b): return lax.dot_general(a,b,(((1,),(1,)),((),())),preferred_element_type=f32)
def tn(a,b): return lax.dot_general(a,b,(((0,),(0,)),((),())),preferred_element_type=f32)

def mlp_kernel(T, x_ref, ob_ref, obT_ref, cot_ref, wo_ref, wgu_ref, wd_ref, gain_ref,
               out_ref, dmid_ref, dob_ref, dobT_ref, dwo_ref, dwgu_ref, dwd_ref,
               h2_s, h2T_s, dfb_s, dh2_s, r_s, hid_s, dg_s, du_s):
    f = pl.program_id(0); nf = pl.num_programs(0)
    S = x_ref.shape[0]; nt_ = S // T
    gain = gain_ref[1:2, :]
    @pl.when(f == 0)
    def _():
        @pl.loop(0, nt_)
        def _(i):
            t = pl.ds(pl.multiple_of(i*T, T), T)
            mid = x_ref[t, :].astype(f32) + nn(ob_ref[t, :], wo_ref[...])
            out_ref[t, :] = mid
            dmid_ref[t, :] = mid
            r = lax.rsqrt(jnp.mean(mid*mid, axis=-1, keepdims=True) + EPS)
            r_s[t, :] = jnp.broadcast_to(r, (T, 128))
            h2 = ((mid*r)*gain).astype(bf16)
            h2_s[t, :] = h2
            h2T_s[:, t] = h2.T
            dfb_s[t, :] = cot_ref[t, :].astype(bf16)
            dh2_s[t, :] = jnp.zeros_like(mid)
    @pl.loop(0, nt_)
    def _(i):
        t = pl.ds(pl.multiple_of(i*T, T), T)
        h2 = h2_s[t, :]; dfb = dfb_s[t, :]
        g = nn(h2, wgu_ref[0]); u = nn(h2, wgu_ref[1])
        dh = nt(dfb, wd_ref[...])
        sig = 0.5*jnp.tanh(0.5*g)+0.5
        silu = g*sig
        hid = (silu*u).astype(bf16)
        dg = (dh*u*(sig*(1.0+g*(1.0-sig)))).astype(bf16)
        du = (dh*silu).astype(bf16)
        hid_s[t, :] = hid; dg_s[t, :] = dg; du_s[t, :] = du
        out_ref[t, :] += nn(hid, wd_ref[...])
        dh2_s[t, :] += nt(dg, wgu_ref[0]) + nt(du, wgu_ref[1])
    dwd_ref[...] = tn(hid_s[...], dfb_s[...]).astype(bf16)
    dwgu_ref[0] = nn(h2T_s[...], dg_s[...]).astype(bf16)
    dwgu_ref[1] = nn(h2T_s[...], du_s[...]).astype(bf16)
    @pl.when(f == nf-1)
    def _():
        @pl.loop(0, nt_)
        def _(i):
            t = pl.ds(pl.multiple_of(i*T, T), T)
            mid = dmid_ref[t, :]; r = r_s[t, 0:1]
            xh = mid*r; dh = dh2_s[t, :]; w = dh*gain
            back = r*(w - xh*jnp.mean(w*xh, axis=-1, keepdims=True))
            dmid = cot_ref[t, :] + back
            dmid_ref[t, :] = dmid
            dab = dmid.astype(bf16)
            h2_s[t, :] = dab
            dob_ref[t, :] = nt(dab, wo_ref[...]).astype(bf16)
            dobT_ref[:, t] = nt(wo_ref[...], dab).astype(bf16)
        dwo_ref[...] = nn(obT_ref[...], h2_s[...]).astype(bf16)

def mlp(x, ob, obT, cot, wo, wgu, wd, gains, FC=512, T=256):
    S, D = x.shape; FF = wd.shape[0]
    full = lambda *s: pl.BlockSpec(s, lambda f: (0,)*len(s), pipeline_mode=pl.Buffered(1))
    return pl.pallas_call(
        functools.partial(mlp_kernel, T), grid=(FF//FC,),
        in_specs=[full(S,D), full(S,D), full(D,S), full(S,D), full(D,D),
                  pl.BlockSpec((2,D,FC), lambda f:(0,0,f)), pl.BlockSpec((FC,D), lambda f:(f,0)), full(8,D)],
        out_specs=[full(S,D), full(S,D), full(S,D), full(D,S), full(D,D),
                  pl.BlockSpec((2,D,FC), lambda f:(0,0,f)), pl.BlockSpec((FC,D), lambda f:(f,0))],
        out_shape=[jax.ShapeDtypeStruct((S,D),f32), jax.ShapeDtypeStruct((S,D),f32), jax.ShapeDtypeStruct((S,D),bf16),
                   jax.ShapeDtypeStruct((D,S),bf16), jax.ShapeDtypeStruct((D,D),bf16),
                   jax.ShapeDtypeStruct((2,D,FF),bf16), jax.ShapeDtypeStruct((FF,D),bf16)],
        scratch_shapes=[pltpu.VMEM((S,D),bf16), pltpu.VMEM((D,S),bf16), pltpu.VMEM((S,D),bf16), pltpu.VMEM((S,D),f32),
                        pltpu.VMEM((S,128),f32), pltpu.VMEM((S,FC),bf16), pltpu.VMEM((S,FC),bf16), pltpu.VMEM((S,FC),bf16)],
        compiler_params=pltpu.CompilerParams(vmem_limit_bytes=62*2**20),
        name="mlp",
    )(x, ob, obT, cot, wo, wgu, wd, gains)

H, HD = 12, 64
NEG = -1e30
VM = pl.BlockSpec(memory_space=pltpu.VMEM)
def tnt(a,b): return lax.dot_general(a,b,(((0,),(1,)),((),())),preferred_element_type=f32)

def seg_rows(lens_ref, S):
    slot = lax.broadcasted_iota(jnp.int32, (8, S), 1)
    seg = jnp.zeros((8, S), jnp.int32); start = jnp.zeros((8, S), jnp.int32)
    end = jnp.int32(0)
    for s in range(lens_ref.shape[1]-1):
        end = end + lens_ref[0, s]
        past = (slot >= end).astype(jnp.int32)
        seg += past
        start += past * lens_ref[0, s]
    return seg, slot - start


MESH = pl.DeviceIdType.MESH

def flip(v, b):
    return v + b - 2*b*lax.rem(lax.div(v, b), 2)

def places():
    d = lax.axis_index("dp"); z = lax.axis_index("rep")
    sib, xn, yn = flip(d, 1), flip(d, 2), flip(d, 4)
    xy = flip(xn, 4)
    return d, z, sib, xn, yn, xy

def greet(devs):
    bar = pltpu.get_barrier_semaphore()
    for dev in devs:
        pl.semaphore_signal(bar, inc=1, device_id=dev, device_id_type=MESH)
    pl.semaphore_wait(bar, len(devs))

class Gather:
    N = 15
    def __init__(self, ref, view, send, recv, g):
        self.ref, self.view, self.send, self.recv, self.g = ref, view, send, recv, g
        d, z, sib, xn, yn, xy = places()
        zn = flip(z, 1)
        S, X, Y, Z = (sib, z), (xn, z), (yn, z), (d, zn)
        self.moves = [(d, "all", S), (d, "zb", X), (d, "zb", Y),
                      (xn, "zb", S), (xn, "z", Y), (xn, "z", Z),
                      (yn, "zb", S), (yn, "b", X), (yn, "z", Z),
                      (xy, "z", S), (xy, "z", Z), (xy, "b", S),
                      (xn, "o", S), (yn, "o", S), (xy, "o", S)]
        self.after = {1: (3, 4, 5), 2: (6, 7, 8), 4: (9, 10), 7: (11,), 5: (12,), 8: (13,), 10: (14,)}
    def copy(self, k):
        d, part, dev = self.moves[k]
        v = self.view(self.ref, d, part)
        return pltpu.make_async_remote_copy(src_ref=v, dst_ref=v, send_sem=self.send.at[self.g, k], recv_sem=self.recv.at[self.g, k],
                                            device_id=dev, device_id_type=MESH)
    def begin(self):
        for k in (1, 2, 0): self.copy(k).start()
    def got(self, *ks):
        for k in ks:
            self.copy(k).wait_recv()
            for j in self.after.get(k, ()): self.copy(j).start()
    def first(self): self.got(1, 2)
    def second(self): self.got(4, 7, 5, 8)
    def third(self): self.got(10)
    def sibling(self): self.got(0, 3, 6, 9, 11, 12, 13, 14)
    def sent(self):
        for k in range(self.N): self.copy(k).wait_send()

def cut(rows):
    return rows // 3 // 16 * 16


ANY = pl.BlockSpec(memory_space=pl.ANY)
SM = pl.BlockSpec(memory_space=pltpu.SMEM)
B = 256

def spread_gain(pieces, D):
    n, wide = pieces.shape[0], D // pieces.shape[0]
    r = lax.broadcasted_iota(jnp.int32, (n*128, D), 0); c = lax.broadcasted_iota(jnp.int32, (n*128, D), 1)
    pick = (c == lax.div(r, 128)*wide + lax.rem(r, 128)) & (lax.rem(r, 128) < wide)
    flat = jnp.concatenate([pieces[i] for i in range(n)], axis=1).astype(bf16)
    return nn(flat, jnp.where(pick, 1.0, 0.0).astype(bf16))

def forward_attention(lens_ref, x_ref, freq_ref, gain_of, weights_in, w_ref, qT_s, kT_s, vT_s, oT_s, lse_s, cos_s, sin_s, segc_s, segr_s, bias_s, hook):
    S, D = x_ref.shape
    n = S // B
    seg, place = seg_rows(lens_ref, S)
    ang = jnp.broadcast_to(place[0:1, :].astype(f32), (HD//2, S)) * freq_ref[:, 0:1]
    cos_s[...] = jnp.cos(ang); sin_s[...] = jnp.sin(ang)
    segf = jnp.broadcast_to(seg[0:1, :].astype(f32), (128, S))
    segr_s[...] = segf[0:8]
    segc_s[...] = segf.T
    weights_in()
    gain = gain_of()
    @pl.loop(0, n)
    def _(i):
        t = pl.ds(pl.multiple_of(i*B, B), B)
        xf = x_ref[t, :].astype(f32)
        r = lax.rsqrt(jnp.mean(xf*xf, axis=-1, keepdims=True) + EPS)
        h1 = ((xf*r)*gain).astype(bf16)
        c = cos_s[:, t]; s = sin_s[:, t]
        for w, dst, sc in ((0, qT_s, 0.125), (1, kT_s, 1.0)):
            y = tnt(w_ref[w], h1)
            for h in range(H):
                a = y[h*HD:h*HD+32]; b = y[h*HD+32:h*HD+64]
                dst[h*HD:h*HD+32, t] = ((a*c - b*s)*sc).astype(bf16)
                dst[h*HD+32:h*HD+64, t] = ((b*c + a*s)*sc).astype(bf16)
        vT_s[:, t] = tnt(w_ref[2], h1).astype(bf16)
    hook("proj")
    for i in range(n):
        k0 = max(0, i-2)*B; nk = i*B + B - k0
        q0 = i*B
        kid = lax.broadcasted_iota(jnp.int32, (nk, B), 0) + k0
        qid = lax.broadcasted_iota(jnp.int32, (nk, B), 1) + q0
        ok = (segc_s[k0:k0+nk, 0:1] == segr_s[0:1, q0:q0+B]) & (kid <= qid)
        bias_s[0:nk, :] = jnp.where(ok, 0.0, NEG)
        @pl.loop(0, H//2)
        def _(p):
            for e in range(2):
                rows = pl.ds(pl.multiple_of(p*128 + e*64, 64), 64)
                s = tn(kT_s[rows, k0:k0+nk], qT_s[rows, q0:q0+B]) + bias_s[0:nk, :]
                m = jnp.max(s, axis=0, keepdims=True)
                ex = jnp.exp(s - m)
                l = jnp.sum(ex, axis=0, keepdims=True)
                o = nn(vT_s[rows, k0:k0+nk], ex.astype(bf16)) * (1.0/l)
                oT_s[rows, q0:q0+B] = o.astype(bf16)
                lse_s[pl.ds(p*2+e, 1), q0:q0+B] = m + jnp.log(l)
        hook(i)

def local_body(lens_ref, x_ref, freq_ref, gain_ref, w_ref, qT_ref, kT_ref, vT_ref, oT_ref, lse_ref, cos_ref, sin_ref, segc_ref, segr_ref, bias_s):
    forward_attention(lens_ref, x_ref, freq_ref, lambda: gain_ref[0:1, :], lambda: None, w_ref, qT_ref, kT_ref, vT_ref, oT_ref,
                      lse_ref, cos_ref, sin_ref, segc_ref, segr_ref, bias_s, lambda at: None)

def attn_fwd(lens, x, gains, freq, wqkv):
    S, D = x.shape
    sh = lambda s, d: jax.ShapeDtypeStruct(s, d)
    return pl.pallas_call(local_body,
        in_specs=[SM]+[VM]*4, out_specs=[VM]*9,
        out_shape=[sh((D,S),bf16)]*4 + [sh((16,S),f32), sh((32,S),f32), sh((32,S),f32), sh((S,128),f32), sh((8,S),f32)],
        scratch_shapes=[pltpu.VMEM((768,256),f32)],
        compiler_params=pltpu.CompilerParams(vmem_limit_bytes=62*2**20), name="attend")(lens, x, freq, gains, wqkv)

GW = 256

def backward_attention(x_ref, gain_ref, w_ref, ig_s, ig_ready, ig_done, qT_ref, kT_ref, vT_ref, dob_ref, dobT_ref, lse_ref, cos_ref, sin_ref, segc_ref, segr_ref,
                       dw_s, bias_s, q_s, dqT_s, dk_s, dv_s, g_s, h1T_s, hook):
    S, D = x_ref.shape
    n = S // B
    gain = gain_ref[0:1, :]
    hook("start")
    blocks = []
    at = 0
    for i in range(n):
        k0 = max(0, i-2)*B; nk = i*B + B - k0
        q0 = i*B
        kid = lax.broadcasted_iota(jnp.int32, (nk, B), 0) + k0
        qid = lax.broadcasted_iota(jnp.int32, (nk, B), 1) + q0
        ok = (segc_ref[k0:k0+nk, 0:1] == segr_ref[0:1, q0:q0+B]) & (kid <= qid)
        bias_s[at:at+nk, :] = jnp.where(ok, 0.0, NEG)
        blocks.append((q0, k0, nk, at)); at += nk
    q_s[...] = qT_ref[...].T
    @pl.loop(0, n)
    def _(i):
        t = pl.ds(pl.multiple_of(i*B, B), B)
        xf = x_ref[t, :].astype(f32)
        r = lax.rsqrt(jnp.mean(xf*xf, axis=-1, keepdims=True) + EPS)
        h1T_s[:, t] = ((xf*r)*gain).astype(bf16).T
    hook("ready")
    lane = lax.broadcasted_iota(jnp.int32, (B, 128), 1)
    @pl.loop(0, H//2)
    def _(p):
        cols = pl.ds(pl.multiple_of(p*128, 128), 128)
        dk_s[...] = jnp.zeros_like(dk_s); dv_s[...] = jnp.zeros_like(dv_s)
        for q0, k0, nk, at in blocks:
            dv = dk = None
            for e in range(2):
                rows = pl.ds(pl.multiple_of(p*128 + e*64, 64), 64)
                mine = (lane < 64) if e == 0 else (lane >= 64)
                dobz = jnp.where(mine, dob_ref[q0:q0+B, cols], 0).astype(bf16)
                qz = jnp.where(mine, q_s[q0:q0+B, cols], 0).astype(bf16)
                s = tn(kT_ref[rows, k0:k0+nk], qT_ref[rows, q0:q0+B]) + bias_s[at:at+nk, :]
                pr = jnp.exp(s - lse_ref[pl.ds(p*2+e, 1), q0:q0+B])
                dp = tn(vT_ref[rows, k0:k0+nk], dobT_ref[rows, q0:q0+B])
                inner = jnp.sum(pr*dp, axis=0, keepdims=True)
                ds = (pr*(dp - inner)).astype(bf16)
                dve = nn(pr.astype(bf16), dobz)
                dke = nn(ds, qz)
                dqT_s[e*64:e*64+64, q0:q0+B] = nn(kT_ref[rows, k0:k0+nk], ds) * 0.125
                dv = dve if dv is None else dv + dve
                dk = dke if dk is None else dk + dke
            dv_s[k0:k0+nk, :] += dv
            dk_s[k0:k0+nk, :] += dk
        c = cos_ref[...]; s = sin_ref[...]
        for j, src in ((0, dqT_s[...]), (1, dk_s[...].T)):
            parts = []
            for e in range(2):
                a = src[e*HD:e*HD+32]; b = src[e*HD+32:e*HD+64]
                parts += [a*c + b*s, b*c - a*s]
            g_s[j, :, cols] = jnp.concatenate(parts, axis=0).astype(bf16).T
        g_s[2, :, cols] = dv_s[...].astype(bf16)
        @pl.when(lax.rem(p, 2) == 1)
        def _():
            g = lax.div(p, 2)
            wide = pl.ds(pl.multiple_of(g*GW, GW), GW)
            for j in range(3):
                dw_s[g, j] = nn(h1T_s[...], g_s[j, :, wide]).astype(bf16)
        for k in range(H//2):
            @pl.when(p == k)
            def _():
                hook(k)
    ig_ready()
    for i in range(n):
        t = pl.ds(i*B, B)
        xf = x_ref[t, :].astype(f32)
        r = lax.rsqrt(jnp.mean(xf*xf, axis=-1, keepdims=True) + EPS)
        xh = xf*r
        dh = nt(g_s[0, t, :], w_ref[0]) + nt(g_s[1, t, :], w_ref[1]) + nt(g_s[2, t, :], w_ref[2])
        w = dh*gain
        ig_s[t, :] += r*(w - xh*jnp.mean(w*xh, axis=-1, keepdims=True))
        ig_done(i, t)
        hook("tile%d" % i)

def scratch_bwd(S, D):
    n = S // B
    area = sum(min(i+1, 3) for i in range(n))*B
    return [pltpu.VMEM((D//GW, 3, D, GW), bf16), pltpu.VMEM((area, B), f32), pltpu.VMEM((S, D), bf16), pltpu.VMEM((128, S), f32),
            pltpu.VMEM((S, 128), f32), pltpu.VMEM((S, 128), f32), pltpu.VMEM((3, S, D), bf16), pltpu.VMEM((D, S), bf16)]

def bwd_local_body(x_ref, gain_ref, w_ref, dmid_ref, qT_ref, kT_ref, vT_ref, dob_ref, dobT_ref, lse_ref, cos_ref, sin_ref, segc_ref, segr_ref,
                   ig_ref, dw_ref, bias_s, q_s, dqT_s, dk_s, dv_s, g_s, h1T_s):
    ig_ref[...] = dmid_ref[...]
    backward_attention(x_ref, gain_ref, w_ref, ig_ref, lambda: None, lambda i, t: None, qT_ref, kT_ref, vT_ref, dob_ref, dobT_ref, lse_ref, cos_ref, sin_ref,
                       segc_ref, segr_ref, dw_ref, bias_s, q_s, dqT_s, dk_s, dv_s, g_s, h1T_s, lambda at: None)

def attn_bwd(x, gains, wqkv, dmid, qT, kT, vT, dob, dobT, lse, cos, sin, segc, segr):
    S, D = x.shape
    sh = lambda s, d: jax.ShapeDtypeStruct(s, d)
    ig, dw = pl.pallas_call(bwd_local_body,
        in_specs=[VM]*14, out_specs=[VM]*2,
        out_shape=[sh((S,D),f32), sh((D//GW,3,D,GW),bf16)],
        scratch_shapes=scratch_bwd(S, D)[1:],
        compiler_params=pltpu.CompilerParams(vmem_limit_bytes=62*2**20), name="attend_back")(x, gains, wqkv, dmid, qT, kT, vT, dob, dobT, lse, cos, sin, segc, segr)
    return ig, jnp.moveaxis(dw, 0, 2).reshape(3, D, D)


FC, MT = 512, 512

def staggered(items, first, middle, last):
    a = first(items[0]); prev = None
    for i, it in enumerate(items):
        nxt = first(items[i+1]) if i + 1 < len(items) else None
        m = middle(it, a)
        if prev is not None: last(items[i-1], prev)
        prev, a = m, nxt
    last(items[-1], prev)

class Sum(object):
    def __init__(self, u, piece, other, rs, rx, r2, zr, out, send, recv, loc):
        self.u, self.piece, self.other, self.rs, self.rx, self.r2, self.zr, self.out = u, piece, other, rs, rx, r2, zr, out
        self.send, self.recv, self.loc = send, recv, loc
        self.d, self.z, self.sib, self.xn, self.yn, self.xy = places()
        self.rows = rs.shape[-2]; self.half = self.rows // 2
        self.inner = (self.z == 1) | (self.z == 2)
    def cut(self, ref, h):
        s = slice(0, self.half) if h == 0 else slice(self.half, self.rows)
        return ref.at[..., s, :]
    def copy(self, k, src, dst, dev):
        return pltpu.make_async_remote_copy(src_ref=src, dst_ref=dst, send_sem=self.send.at[self.u, k], recv_sem=self.recv.at[self.u, k],
                                            device_id=dev, device_id_type=MESH)
    def s_copy(self, j): return self.copy(j, self.other(j), self.rs.at[j], (self.sib, self.z))
    def x_copies(self):
        X, Y = (self.xn, self.z), (self.yn, self.z)
        return [self.copy(4, self.piece(1, 0), self.cut(self.rx.at[0], 0), X), self.copy(5, self.piece(3, 0), self.cut(self.rx.at[1], 0), X),
                self.copy(6, self.piece(2, 1), self.cut(self.rx.at[0], 1), Y), self.copy(7, self.piece(3, 1), self.cut(self.rx.at[1], 1), Y)]
    def y_copies(self):
        return [self.copy(8, self.piece(2, 0), self.cut(self.r2, 0), (self.yn, self.z)), self.copy(9, self.piece(1, 1), self.cut(self.r2, 1), (self.xn, self.z))]
    def z_copy(self, k):
        zn = (self.d, flip(self.z, 1))
        if k == 0: return self.copy(10, self.piece(0, None), self.zr.at[0], zn)
        if k == 1: return self.copy(11, self.zr.at[0], self.zr.at[1], (self.d, 3 - self.z))
        return self.copy(12, self.piece(0, None), self.zr.at[0], zn)
    def fin(self, inner): return pltpu.make_async_copy(self.piece(0, None) if inner else self.zr.at[0], self.out, self.loc)
    def add(self, dst, a, b):
        if len(dst.shape) == 2: dst[...] = (a[...].astype(f32) + b[...].astype(f32)).astype(bf16)
        else:
            for i in range(dst.shape[0]): dst[i] = (a[i].astype(f32) + b[i].astype(f32)).astype(bf16)
    def a(self):
        for j in (3, 1, 2, 0): self.s_copy(j).start()
    def b(self):
        xs = self.x_copies()
        for j in (3, 1, 2, 0):
            self.s_copy(j).wait_recv()
            p = self.piece(j, None)
            self.add(p, p, self.rs.at[j])
            for k in {3: (1, 3), 1: (0,), 2: (2,), 0: ()}[j]: xs[k].start()
    def c(self):
        for k in self.x_copies(): k.wait_recv()
        ys = self.y_copies()
        for j, h, k in ((2, 0, 0), (1, 1, 1)):
            p = self.piece(j, h)
            self.add(p, p, self.cut(self.rx.at[1], h))
            ys[k].start()
        p = self.piece(0, None)
        self.add(p, p, self.rx.at[0])
    def e(self):
        for k in self.y_copies(): k.wait_recv()
        p = self.piece(0, None)
        self.add(p, p, self.r2)
        @pl.when(jnp.logical_not(self.inner))
        def _(): self.z_copy(0).start()
    def f(self):
        @pl.when(self.inner)
        def _():
            self.z_copy(0).wait_recv()
            self.add(self.zr.at[0], self.zr.at[0], self.piece(0, None))
            self.z_copy(1).start()
    def g(self):
        @pl.when(self.inner)
        def _():
            self.z_copy(1).wait_recv()
            self.add(self.piece(0, None), self.zr.at[0], self.zr.at[1])
            self.z_copy(2).start()
            self.fin(True).start()
    def h(self):
        @pl.when(jnp.logical_not(self.inner))
        def _():
            self.z_copy(2).wait_recv()
            self.fin(False).start()
    def drain(self):
        for j in range(4): self.s_copy(j).wait_send()
        for k in self.x_copies() + self.y_copies(): k.wait_send()
        @pl.when(self.inner)
        def _():
            self.z_copy(1).wait_send(); self.z_copy(2).wait_send()
            self.fin(True).wait()
        @pl.when(jnp.logical_not(self.inner))
        def _():
            self.z_copy(0).wait_send()
            self.fin(False).wait()

def layer_body(n_dp, lens_ref, freq_ref, gain_ref, x_hbm, cot_hbm, qw_hbm, ow_hbm, gw_hbm, dw_hbm,
               out_o, ig_o, gq_o, ggu_o, gdn_o, gou_o,
               wq_s, wo_s, wgu_s, wd_s, qT_s, kT_s, vT_s, oT_s, cos_s, sin_s, segc_s, segr_s, lse_s, dlt_s, gain_s, gp_s,
               out_s, dh2_s, mid_s, acc_s, h2T_s, dfb_s, ch_s, dw2_s,
               g_rs, g_rx, g_r2, g_z, n_rs, n_rx, n_r2, n_z, o_rs, o_rx, o_r2, o_z, q_rs, q_rx, q_r2, q_z,
               ag_send, ag_recv, gn_send, gn_recv, rs_send, rs_recv, rs_loc, loc):
    S, D = x_hbm.shape
    x_s, h1T_s, h1T_late = dfb_s, h2T_s, oT_s
    FF = wd_s.shape[0]
    n, nf, ng = S//B, FF//FC, D//GW
    rq, rd = D//n_dp, FF//n_dp
    d, z, sib, xn, yn, xy = places()
    owners = [d, xn, yn, xy]
    others = [lax.rem(d + j, n_dp) for j in range(1, n_dp)]
    bar = pltpu.get_barrier_semaphore()
    met = [(o, z) for o in others] + [(d, flip(z, 1)), (d, 3 - z)]
    for dev in met: pl.semaphore_signal(bar, inc=1, device_id=dev, device_id_type=MESH)

    def rows(o, r): return pl.ds(pl.multiple_of(o*r, 16), r)
    loads = {}
    def load(key, src, dst):
        c = pltpu.make_async_copy(src, dst, loc.at[len(loads)]); c.start(); loads[key] = c
    for c in range(3): load("q%d" % c, qw_hbm.at[c], out_s.at[c*rq:(c+1)*rq, :])
    load("x", x_hbm, x_s)
    load("o", ow_hbm, out_s.at[3*rq:4*rq, :])
    load("d", dw_hbm, out_s.at[4*rq:4*rq+rd, :])
    wides = [(a, min(D, FF - a)) for a in range(0, FF, D)]
    for c in range(2):
        for k, (a, w) in enumerate(wides):
            load("g%d%d" % (c, k), gw_hbm.at[c, :, a:a+w], dh2_s.at[(c*len(wides)+k)*rq:(c*len(wides)+k+1)*rq, 0:w])
    cot_base = len(loads)
    base = cot_base + 4
    HB = B//2
    def cot_copies(i): return [pltpu.make_async_copy(cot_hbm.at[(i % n)*B + k*HB:(i % n)*B + (k+1)*HB, :], acc_s.at[i % 2 * 2 + k, :, 0:D],
                                                     loc.at[cot_base + i % 2 * 2 + k]) for k in range(2)]
    def cot_start(i):
        for c in cot_copies(i): c.start()
    def cot_get(i):
        for c in cot_copies(i): c.wait()
        return jnp.concatenate([acc_s[i % 2 * 2 + k, :, 0:D] for k in range(2)], axis=0)
    cot_start(0); cot_start(1)

    def rv(r, lead, cols=None):
        a = cut(r)
        p = lax.rem(z, 2)
        def view(ref, o, part):
            off, m = {"all": (0, r), "zb": (p*a, r - a), "z": (p*(r - a), a), "b": (a, r - 2*a), "o": ((1 - p)*(r - a), a)}[part]
            s = pl.ds(pl.multiple_of(o*r + off, 16), m)
            if not lead: return ref.at[s, :]
            return ref.at[:, s, :] if cols is None else ref.at[:, s, cols]
        return view
    G = [Gather(wq_s.at[c], rv(rq, False), ag_send, ag_recv, c) for c in range(3)]
    G.append(Gather(wo_s, rv(rq, False), ag_send, ag_recv, 3))
    gu = lambda f, g: Gather(wgu_s, rv(rq, True, slice(f*FC, (f+1)*FC)), ag_send, ag_recv, g)
    G.append(gu(0, 4))
    G.append(Gather(wd_s, rv(rd, False), ag_send, ag_recv, 5))
    for f in range(1, nf): G.append(gu(f, 5 + f))
    def step(s):
        if s < len(G): G[s].first()
        if 0 <= s - 1 < len(G): G[s-1].second()
        if 0 <= s - 2 < len(G): G[s-2].third()
        if 0 <= s - 3 < len(G): G[s-3].sibling()

    def unit(u, ref, r, lead, cols, bufs, out):
        def piece(j, h):
            o, m = (0, r) if h is None else (h*(r//2), r//2)
            s = pl.ds(pl.multiple_of(owners[j]*r + o, 16), m)
            return ref.at[:, s, cols] if lead else ref.at[s, :]
        def other(j):
            s = rows(flip(owners[j], 1), r)
            return ref.at[:, s, cols] if lead else ref.at[s, :]
        return Sum(u, piece, other, *bufs, out, rs_send, rs_recv, rs_loc.at[u])
    R = []
    for f in range(nf):
        cols = slice(f*FC, (f+1)*FC)
        R.append(unit(f, wgu_s, rq, True, cols, [b.at[f] for b in (g_rs, g_rx, g_r2, g_z)], ggu_o.at[:, :, cols]))
    R.append(unit(nf, wd_s, rd, False, None, (n_rs, n_rx, n_r2, n_z), gdn_o))
    R.append(unit(nf+1, wo_s, rq, False, None, (o_rs, o_rx, o_r2, o_z), gou_o))
    def dw_ref(g): return dw2_s if g == ng - 1 else ch_s.at[:, 0:D, g*GW:(g+1)*GW]
    for g in range(ng):
        R.append(unit(nf+2+g, dw_ref(g), rq, True, slice(0, GW), [b.at[g] for b in (q_rs, q_rx, q_r2, q_z)], gq_o.at[:, :, g*GW:(g+1)*GW]))
    plan = PLAN
    def hook(at):
        for what in plan.get(at, "").split():
            k = int(what[1:])
            if what[0] == "S": step(k)
            elif what[0] == "B": G[k].begin()
            else: getattr(R[k], what[0])()

    gp_s[pl.ds(d, 1)] = gain_ref[...].reshape(1, 8, 128)
    for c in range(3):
        loads["q%d" % c].wait()
        wq_s[c, rows(d, rq), :] = out_s[c*rq:(c+1)*rq, :].astype(bf16)
        if c == 0:
            pl.semaphore_wait(bar, len(met))
            gains = [pltpu.make_async_remote_copy(src_ref=gp_s.at[d], dst_ref=gp_s.at[d], send_sem=gn_send.at[j], recv_sem=gn_recv.at[j],
                                                  device_id=(o, z), device_id_type=MESH) for j, o in enumerate(others)]
        G[c].begin()
        if c == 0:
            for k in gains: k.start()
    loads["o"].wait()
    wo_s[rows(d, rq), :] = out_s[3*rq:4*rq, :].astype(bf16)
    for c in range(2):
        for k, (a, w) in enumerate(wides):
            loads["g%d%d" % (c, k)].wait()
            i = c*len(wides) + k
            wgu_s[c, rows(d, rq), a:a+w] = dh2_s[i*rq:(i+1)*rq, 0:w].astype(bf16)
    loads["d"].wait()
    wd_s[rows(d, rd), :] = out_s[4*rq:4*rq+rd, :].astype(bf16)

    seg, place = seg_rows(lens_ref, S)
    ang = jnp.broadcast_to(place[0:1, :].astype(f32), (HD//2, S)) * freq_ref[:, 0:1]
    cos_s[...] = jnp.cos(ang); sin_s[...] = jnp.sin(ang)
    segf = jnp.broadcast_to(seg[0:1, :].astype(f32), (128, S))
    segr_s[...] = segf[0:8]
    segc_s[...] = segf.astype(bf16).T
    blocks = []
    at = {0: (0, 0), 1: (B, 0), 2: (0, B), 3: (0, 2*B)}
    for i in range(n):
        k0 = max(0, i-2)*B
        blocks.append((i*B, k0, i*B + B - k0) + at[i])
    def masks():
        for q0, k0, nk, r0, c0 in blocks:
            kid = lax.broadcasted_iota(jnp.int32, (nk, B), 0) + k0
            qid = lax.broadcasted_iota(jnp.int32, (nk, B), 1) + q0
            ok = (segc_s[k0:k0+nk, 0:1].astype(f32) == segr_s[0:1, q0:q0+B]) & (kid <= qid)
            dh2_s[r0:r0+nk, c0:c0+B] = jnp.where(ok, 0.0, NEG)
    masks()
    loads["x"].wait()
    hook("start")
    for k in gains: k.wait_recv()
    gain_s[...] = spread_gain(gp_s[...], D)
    def normed(dst):
        @pl.loop(0, n)
        def _(i):
            t = pl.ds(pl.multiple_of(i*B, B), B)
            xf = x_s[t, :].astype(f32)
            r = lax.rsqrt(jnp.mean(xf*xf, axis=-1, keepdims=True) + EPS)
            dst[:, t] = ((xf*r)*gain_s[0:1, :]).astype(bf16).T
    normed(h1T_s)
    for w, dst, sc in ((0, qT_s, 0.125), (1, kT_s, 1.0), (2, vT_s, None)):
        hook("proj%d" % w)
        for t0 in range(0, S, MT):
            t = slice(t0, t0+MT)
            y = tn(wq_s[w], h1T_s[:, t])
            if sc is None: dst[:, t] = y.astype(bf16)
            else:
                c = cos_s[:, t]; s = sin_s[:, t]
                for h in range(H):
                    a = y[h*HD:h*HD+32]; b = y[h*HD+32:h*HD+64]
                    dst[h*HD:h*HD+32, t] = ((a*c - b*s)*sc).astype(bf16)
                    dst[h*HD+32:h*HD+64, t] = ((b*c + a*s)*sc).astype(bf16)

    @pl.loop(0, H//2)
    def _(p):
        rs = [pl.ds(pl.multiple_of(p*128 + e*64, 64), 64) for e in range(2)]
        def scores(it):
            (q0, k0, nk, r0, c0), e = it
            return tn(kT_s[rs[e], k0:k0+nk], qT_s[rs[e], q0:q0+B]) + dh2_s[r0:r0+nk, c0:c0+B]
        def soft(it, s):
            m = jnp.max(s, axis=0, keepdims=True)
            ex = jnp.exp(s - m)
            return m, ex.astype(bf16), jnp.sum(ex, axis=0, keepdims=True)
        def mix(it, mel):
            (q0, k0, nk, r0, c0), e = it
            m, ex, l = mel
            oT_s[rs[e], q0:q0+B] = (nn(vT_s[rs[e], k0:k0+nk], ex) * (1.0/l)).astype(bf16)
            lse_s[pl.ds(p*2+e, 1), q0:q0+B] = m + jnp.log(l)
        staggered([(b, e) for b in blocks for e in range(2)], scores, soft, mix)
        for k in range(H//2):
            @pl.when(p == k)
            def _(): hook("a%d" % k)

    hook("mlp")
    gain2 = gain_s[1:2, :]
    for i in range(n):
        t = slice(i*B, (i+1)*B)
        mid = x_s[t, :].astype(f32) + tn(oT_s[:, t], wo_s[...])
        out_s[t, :] = mid; mid_s[t, :] = mid
        r = lax.rsqrt(jnp.mean(mid*mid, axis=-1, keepdims=True) + EPS)
        h2T_s[:, t] = ((mid*r)*gain2).astype(bf16).T
        dfb_s[t, :] = cot_get(i).astype(bf16)
        cot_start(i+2)
        dh2_s[t, :] = jnp.zeros_like(mid)
    @pl.loop(0, nf)
    def _(f):
        cols = pl.ds(pl.multiple_of(f*FC, FC), FC)
        def first(i):
            t = slice(i*MT, (i+1)*MT)
            return tn(h2T_s[:, t], wgu_s[0, :, cols]), tn(h2T_s[:, t], wgu_s[1, :, cols]), nt(dfb_s[t, :], wd_s[cols, :])
        def middle(i, gud):
            g, u, dh = gud
            t = slice(i*MT, (i+1)*MT)
            sig = 0.5*jnp.tanh(0.5*g) + 0.5
            silu = g*sig
            hid = (silu*u).astype(bf16)
            dg = (dh*u*(sig + silu*(1.0 - sig))).astype(bf16)
            du = (dh*silu).astype(bf16)
            ch_s[0, t, :] = hid; ch_s[1, t, :] = dg; ch_s[2, t, :] = du
            if i == 0:
                for k in range(nf):
                    @pl.when(f == k)
                    def _(): hook("f%dmid" % k)
            return hid, dg, du
        def last(i, hdd):
            hid, dg, du = hdd
            t = slice(i*MT, (i+1)*MT)
            out_s[t, :] += nn(hid, wd_s[cols, :])
            dh2_s[t, :] += nt(dg, wgu_s[0, :, cols]) + nt(du, wgu_s[1, :, cols])
        staggered(list(range(S//MT)), first, middle, last)
        for k in range(nf):
            @pl.when(f == k)
            def _():
                for g in ([4, 5] if k == 0 else [5 + k]): G[g].sent()
        wgu_s[0, :, cols] = nn(h2T_s[...], ch_s[1]).astype(bf16)
        wgu_s[1, :, cols] = nn(h2T_s[...], ch_s[2]).astype(bf16)
        wd_s[cols, :] = tn(ch_s[0], dfb_s[...]).astype(bf16)
        for k in range(nf):
            @pl.when(f == k)
            def _(): hook("f%dend" % k)
    out_c = pltpu.make_async_copy(out_s, out_o, loc.at[base]); out_c.start()
    for i in range(n):
        t = slice(i*B, (i+1)*B)
        mid = mid_s[t, :]; dh = dh2_s[t, :]
        r = lax.rsqrt(jnp.mean(mid*mid, axis=-1, keepdims=True) + EPS)
        xh = mid*r; w = dh*gain2
        dmid = cot_get(i) + r*(w - xh*jnp.mean(w*xh, axis=-1, keepdims=True))
        if i + 2 < n: cot_start(i+2)
        mid_s[t, :] = dmid
        dab = dmid.astype(bf16)
        dfb_s[t, :] = dab
        h2T_s[:, t] = nt(wo_s[...], dab).astype(bf16)
        if i == 1: hook("e0")
    G[3].sent()
    wo_s[...] = nn(oT_s[...], dfb_s[...]).astype(bf16)
    x_again = pltpu.make_async_copy(x_hbm, x_s, loc.at[0]); x_again.start()
    for h in range(H):
        r = slice(h*HD, (h+1)*HD)
        dlt_s[h:h+1, :] = jnp.sum(h2T_s[r, :].astype(f32)*oT_s[r, :].astype(f32), axis=0, keepdims=True)
    masks()
    hook("e1")
    x_again.wait()
    normed(h1T_late)

    dq_s, dk_s, dv_s = (acc_s.at[j] for j in range(3))
    @pl.loop(0, H//2)
    def _(p):
        rs = [pl.ds(pl.multiple_of(p*128 + e*64, 64), 64) for e in range(2)]
        dk_s[...] = jnp.zeros_like(dk_s); dv_s[...] = jnp.zeros_like(dv_s)
        def first(it):
            (q0, k0, nk, r0, c0), e = it
            return (tn(kT_s[rs[e], k0:k0+nk], qT_s[rs[e], q0:q0+B]) + dh2_s[r0:r0+nk, c0:c0+B],
                    tn(vT_s[rs[e], k0:k0+nk], h2T_s[rs[e], q0:q0+B]))
        def middle(it, sd):
            (q0, k0, nk, r0, c0), e = it
            s, dp = sd
            pr = jnp.exp(s - lse_s[pl.ds(p*2+e, 1), q0:q0+B])
            return pr.astype(bf16), (pr*(dp - dlt_s[pl.ds(p*2+e, 1), q0:q0+B])).astype(bf16)
        def last(it, pd):
            (q0, k0, nk, r0, c0), e = it
            pr, ds = pd
            r = slice(e*HD, (e+1)*HD)
            dv_s[r, k0:k0+nk] += nt(h2T_s[rs[e], q0:q0+B], pr)
            dk_s[r, k0:k0+nk] += nt(qT_s[rs[e], q0:q0+B], ds)
            dq_s[r, q0:q0+B] = nn(kT_s[rs[e], k0:k0+nk], ds) * 0.125
        staggered([(b, e) for b in blocks for e in range(2)], first, middle, last)
        c = cos_s[...]; s = sin_s[...]
        for src, dst in ((dq_s, qT_s), (dk_s, kT_s)):
            for e in range(2):
                a = src[e*HD:e*HD+32, :]; b = src[e*HD+32:(e+1)*HD, :]
                dst[pl.ds(pl.multiple_of(p*128 + e*64, 32), 32), :] = (a*c + b*s).astype(bf16)
                dst[pl.ds(pl.multiple_of(p*128 + e*64 + 32, 32), 32), :] = (b*c - a*s).astype(bf16)
        vT_s[pl.ds(pl.multiple_of(p*128, 128), 128), :] = dv_s[...].astype(bf16)
        for k in range(H//2):
            @pl.when(p == k)
            def _():
                if k % 2 == 1:
                    g = k//2
                    for j, src in enumerate((qT_s, kT_s, vT_s)):
                        dw_ref(g)[j] = nt(h1T_late[...], src[g*GW:(g+1)*GW, :]).astype(bf16)
                hook("c%d" % k)
    def ig_copy(i): return pltpu.make_async_copy(mid_s.at[i*B:(i+1)*B, :], ig_o.at[i*B:(i+1)*B, :], loc.at[base + 1 + i])
    gain1 = gain_s[0:1, :]
    for i in range(n):
        t = slice(i*B, (i+1)*B)
        xf = x_s[t, :].astype(f32)
        r = lax.rsqrt(jnp.mean(xf*xf, axis=-1, keepdims=True) + EPS)
        xh = xf*r
        dh = tnt(qT_s[:, t], wq_s[0]) + tnt(kT_s[:, t], wq_s[1]) + tnt(vT_s[:, t], wq_s[2])
        w = dh*gain1
        mid_s[t, :] += r*(w - xh*jnp.mean(w*xh, axis=-1, keepdims=True))
        ig_copy(i).start()
        hook("t%d" % i)
    hook("end")
    for g in range(3): G[g].sent()
    for k in gains: k.wait_send()
    for u in R: u.drain()
    out_c.wait()
    for i in range(n): ig_copy(i).wait()

PLAN = {
    "start": "S0 B3 S1 B4 S2 B5",
    "proj0": "S3 B6", "proj1": "S4 B7", "proj2": "S5 B8",
    "a1": "S6", "a3": "S7", "a5": "S8",
    "f0mid": "S9", "f1mid": "S10 b0", "f2mid": "S11 c0 b1", "f3mid": "b2 c1 f0",
    "f0end": "a0", "f1end": "a1", "f2end": "a2 e0", "f3end": "a3 a4 e1",
    "e0": "g0 b3 c2 f1", "e1": "a5 b4 e2",
    "c0": "h0 b5 c3 f2 g1", "c1": "a6 e3 h1 g2", "c2": "b6 c4 c5 f3 h2", "c3": "a7 c6 e4 e5 g3", "c4": "b7 e6 f4 f5 h3", "c5": "a8 c7 f6 g4 g5",
    "t0": "b8 e7 g6 h4 h5", "t1": "f7 h6", "t2": "c8 g7", "t3": "e8 h7",
    "end": "f8 g8 h8",
}

def layer(n_dp, lens, freq, piece, x, cot, qw, ow, gw, dw):
    S, D = x.shape
    FF = gw.shape[2]
    sh = lambda s, d: jax.ShapeDtypeStruct(s, d)
    b = lambda *s: pltpu.VMEM(s, bf16)
    w = lambda *s: pltpu.VMEM(s, f32)
    rq, rd, nf, ng = D//n_dp, FF//n_dp, FF//FC, D//GW
    dma = pltpu.SemaphoreType.DMA
    def bufs(*lead_piece, many=None):
        m = () if many is None else (many,)
        return [b(*m, 4, *lead_piece), b(*m, 2, *lead_piece), b(*m, *lead_piece), b(*m, 2, *lead_piece)]
    return pl.pallas_call(functools.partial(layer_body, n_dp),
        in_specs=[SM, VM, VM] + [ANY]*6, out_specs=[ANY]*6,
        out_shape=[sh((S,D),f32), sh((S,D),f32), sh((3,rq,D),bf16), sh((2,rq,FF),bf16), sh((rd,D),bf16), sh((rq,D),bf16)],
        scratch_shapes=[b(3,D,D), b(D,D), b(2,D,FF), b(FF,D), b(D,S), b(D,S), b(D,S), b(D,S),
                        w(HD//2,S), w(HD//2,S), b(S,128), w(8,S), w(16,S), w(16,S), w(8,D), w(n_dp,8,128),
                        w(S,D), w(S,D), w(S,D), w(4,128,S), b(D,S), b(S,D), b(3,S,FC), b(3,D,GW)]
            + bufs(2,rq,FC,many=nf) + bufs(rd,D) + bufs(rq,D) + bufs(3,rq,GW,many=ng)
            + [dma((5+nf,15)), dma((5+nf,15)), dma((n_dp-1,)), dma((n_dp-1,)), dma((nf+2+ng,13)), dma((nf+2+ng,13)), dma((nf+2+ng,)), dma((24,))],
        compiler_params=pltpu.CompilerParams(collective_id=0, has_side_effects=True, vmem_limit_bytes=63*2**20),
        cost_estimate=pl.CostEstimate(flops=55*10**9, bytes_accessed=40*10**6, transcendentals=20*10**6),
        name="layer")(lens, freq, piece, x, cot, qw, ow, gw, dw)

def can_fuse(n_dp, n_rep, S, D, FF, *rows):
    return n_dp == 8 and n_rep == 4 and S == 4*B and D % GW == 0 and FF == 4*FC and all(r % 32 == 0 for r in rows)

def adam_step(weight, grad_sum, moment, second, rate, decay):
    moment_new = beta_one * moment + (1.0 - beta_one) * grad_sum
    second_new = beta_two * second + (1.0 - beta_two) * grad_sum * grad_sum
    moment_hat = moment_new / (1.0 - beta_one**STEP)
    second_hat = second_new / (1.0 - beta_two**STEP)
    weight_new = weight - rate * (moment_hat / (jnp.sqrt(second_hat) + adam_eps) + decay * weight)
    return (moment_new, second_new, weight_new)


def per_device(tokens, seg_lens, cotangent, qkv_w, out_w, gu_w, down_w, gains,
               qkv_m, qkv_v, out_m, out_v, gu_m, gu_v, down_m, down_v, gain_m, gain_v):
    _, S, D = tokens.shape
    x = tokens.reshape(S, D)
    cot = cotangent.reshape(S, D)
    gain_low = gains.astype(bf16)
    freq = 10000.0 ** (-jnp.arange(HD // 2, dtype=f32) / (HD // 2))
    freq = jnp.broadcast_to(freq[:, None], (HD // 2, 128))
    n_dp, n_rep = lax.axis_size("dp"), lax.axis_size("rep")
    if can_fuse(n_dp, n_rep, S, D, gu_w.shape[2], qkv_w.shape[1], out_w.shape[0], gu_w.shape[1], down_w.shape[0]):
        piece = jnp.pad(gain_low.astype(f32), ((0, 6), (0, 128 - gains.shape[1])))
        output, input_grad, g_qkv, g_gu, g_down, g_out = layer(n_dp, seg_lens, freq, piece, x, cot, qkv_w, out_w, gu_w, down_w)
        g_qkv, g_gu, g_down, g_out = (g.astype(f32) for g in (g_qkv, g_gu, g_down, g_out))
    else:
        wqkv = lax.all_gather(qkv_w.astype(bf16), "dp", axis=1, tiled=True)
        gain_full = lax.all_gather(gain_low, "dp", axis=1, tiled=True).astype(f32)
        wo = lax.all_gather(out_w.astype(bf16), "dp", axis=0, tiled=True)
        wgu = lax.all_gather(gu_w.astype(bf16), "dp", axis=1, tiled=True)
        wd = lax.all_gather(down_w.astype(bf16), "dp", axis=0, tiled=True)
        gain8 = jnp.pad(gain_full, ((0, 6), (0, 0)))
        qT, kT, vT, oT, lse, cos, sin, segc, segr = attn_fwd(seg_lens, x, gain8, freq, wqkv)
        output, dmid, dob, dobT, dwo, dwgu, dwd = mlp(x, oT.T, oT, cot, wo, wgu, wd, gain8)
        input_grad, dwqkv = attn_bwd(x, gain8, wqkv, dmid, qT, kT, vT, dob, dobT, lse, cos, sin, segc, segr)

        def owned(grad, axis):
            part = lax.psum_scatter(grad, "dp", scatter_dimension=axis, tiled=True)
            return lax.psum(part.astype(f32), "rep")

        g_down = owned(dwd, 0)
        g_gu = owned(dwgu, 1)
        g_out = owned(dwo, 0)
        g_qkv = owned(dwqkv, 1)
    gain_f = gain_low.astype(f32)
    g_gain = jnp.stack([
        jnp.sum(g_qkv * qkv_w.astype(bf16).astype(f32), axis=(0, 2)) / gain_f[0],
        jnp.sum(g_gu * gu_w.astype(bf16).astype(f32), axis=(0, 2)) / gain_f[1],
    ])
    qkv_res = adam_step(qkv_w, g_qkv, qkv_m, qkv_v, matrix_rate, weight_decay)
    out_res = adam_step(out_w, g_out, out_m, out_v, matrix_rate, weight_decay)
    gu_res = adam_step(gu_w, g_gu, gu_m, gu_v, matrix_rate, weight_decay)
    down_res = adam_step(down_w, g_down, down_m, down_v, matrix_rate, weight_decay)
    gain_res = adam_step(gains, g_gain, gain_m, gain_v, gain_rate, 0.0)
    return (output.reshape(tokens.shape), input_grad.reshape(tokens.shape)) + qkv_res + out_res + gu_res + down_res + gain_res


def solution(mesh):
    rows, cols, vec = P(("dp", "rep"), None, None), P(None, "dp", None), P("dp", None)
    small = P(None, "dp")
    return jax.shard_map(
        per_device,
        mesh=mesh,
        in_specs=(rows, P(("dp", "rep"), None), rows, cols, vec, cols, vec, small,
                  cols, cols, vec, vec, cols, cols, vec, vec, small, small),
        out_specs=(rows, rows) + (cols,) * 3 + (vec,) * 3 + (cols,) * 3 + (vec,) * 3 + (small,) * 3,
        check_vma=False,
    )
```

```python
import functools
import math

import jax
import jax.numpy as jnp
from jax import lax
from jax.experimental import pallas as pl
from jax.experimental.pallas import tpu as pltpu
from jax.sharding import PartitionSpec as P

bf16, f32 = jnp.bfloat16, jnp.float32
STEP = 10
beta_one, beta_two, adam_eps = 0.9, 0.95, 1e-08
weight_decay, matrix_rate, gain_rate = 0.05, 0.1, 0.3
EPS = 1e-5
def nn(a,b): return lax.dot_general(a,b,(((1,),(0,)),((),())),preferred_element_type=f32)
def nt(a,b): return lax.dot_general(a,b,(((1,),(1,)),((),())),preferred_element_type=f32)
def tn(a,b): return lax.dot_general(a,b,(((0,),(0,)),((),())),preferred_element_type=f32)

def mlp_kernel(T, x_ref, ob_ref, obT_ref, cot_ref, wo_ref, wgu_ref, wd_ref, gain_ref,
               out_ref, dmid_ref, dob_ref, dobT_ref, dwo_ref, dwgu_ref, dwd_ref,
               h2_s, h2T_s, dfb_s, dh2_s, r_s, hid_s, dg_s, du_s):
    f = pl.program_id(0); nf = pl.num_programs(0)
    S = x_ref.shape[0]; nt_ = S // T
    gain = gain_ref[1:2, :]
    @pl.when(f == 0)
    def _():
        @pl.loop(0, nt_)
        def _(i):
            t = pl.ds(pl.multiple_of(i*T, T), T)
            mid = x_ref[t, :].astype(f32) + nn(ob_ref[t, :], wo_ref[...])
            out_ref[t, :] = mid
            dmid_ref[t, :] = mid
            r = lax.rsqrt(jnp.mean(mid*mid, axis=-1, keepdims=True) + EPS)
            r_s[t, :] = jnp.broadcast_to(r, (T, 128))
            h2 = ((mid*r)*gain).astype(bf16)
            h2_s[t, :] = h2
            h2T_s[:, t] = h2.T
            dfb_s[t, :] = cot_ref[t, :].astype(bf16)
            dh2_s[t, :] = jnp.zeros_like(mid)
    @pl.loop(0, nt_)
    def _(i):
        t = pl.ds(pl.multiple_of(i*T, T), T)
        h2 = h2_s[t, :]; dfb = dfb_s[t, :]
        g = nn(h2, wgu_ref[0]); u = nn(h2, wgu_ref[1])
        dh = nt(dfb, wd_ref[...])
        sig = 0.5*jnp.tanh(0.5*g)+0.5
        silu = g*sig
        hid = (silu*u).astype(bf16)
        dg = (dh*u*(sig*(1.0+g*(1.0-sig)))).astype(bf16)
        du = (dh*silu).astype(bf16)
        hid_s[t, :] = hid; dg_s[t, :] = dg; du_s[t, :] = du
        out_ref[t, :] += nn(hid, wd_ref[...])
        dh2_s[t, :] += nt(dg, wgu_ref[0]) + nt(du, wgu_ref[1])
    dwd_ref[...] = tn(hid_s[...], dfb_s[...]).astype(bf16)
    dwgu_ref[0] = nn(h2T_s[...], dg_s[...]).astype(bf16)
    dwgu_ref[1] = nn(h2T_s[...], du_s[...]).astype(bf16)
    @pl.when(f == nf-1)
    def _():
        @pl.loop(0, nt_)
        def _(i):
            t = pl.ds(pl.multiple_of(i*T, T), T)
            mid = dmid_ref[t, :]; r = r_s[t, 0:1]
            xh = mid*r; dh = dh2_s[t, :]; w = dh*gain
            back = r*(w - xh*jnp.mean(w*xh, axis=-1, keepdims=True))
            dmid = cot_ref[t, :] + back
            dmid_ref[t, :] = dmid
            dab = dmid.astype(bf16)
            h2_s[t, :] = dab
            dob_ref[t, :] = nt(dab, wo_ref[...]).astype(bf16)
            dobT_ref[:, t] = nt(wo_ref[...], dab).astype(bf16)
        dwo_ref[...] = nn(obT_ref[...], h2_s[...]).astype(bf16)

def mlp(x, ob, obT, cot, wo, wgu, wd, gains, FC=512, T=256):
    S, D = x.shape; FF = wd.shape[0]
    full = lambda *s: pl.BlockSpec(s, lambda f: (0,)*len(s), pipeline_mode=pl.Buffered(1))
    return pl.pallas_call(
        functools.partial(mlp_kernel, T), grid=(FF//FC,),
        in_specs=[full(S,D), full(S,D), full(D,S), full(S,D), full(D,D),
                  pl.BlockSpec((2,D,FC), lambda f:(0,0,f)), pl.BlockSpec((FC,D), lambda f:(f,0)), full(8,D)],
        out_specs=[full(S,D), full(S,D), full(S,D), full(D,S), full(D,D),
                  pl.BlockSpec((2,D,FC), lambda f:(0,0,f)), pl.BlockSpec((FC,D), lambda f:(f,0))],
        out_shape=[jax.ShapeDtypeStruct((S,D),f32), jax.ShapeDtypeStruct((S,D),f32), jax.ShapeDtypeStruct((S,D),bf16),
                   jax.ShapeDtypeStruct((D,S),bf16), jax.ShapeDtypeStruct((D,D),bf16),
                   jax.ShapeDtypeStruct((2,D,FF),bf16), jax.ShapeDtypeStruct((FF,D),bf16)],
        scratch_shapes=[pltpu.VMEM((S,D),bf16), pltpu.VMEM((D,S),bf16), pltpu.VMEM((S,D),bf16), pltpu.VMEM((S,D),f32),
                        pltpu.VMEM((S,128),f32), pltpu.VMEM((S,FC),bf16), pltpu.VMEM((S,FC),bf16), pltpu.VMEM((S,FC),bf16)],
        compiler_params=pltpu.CompilerParams(vmem_limit_bytes=62*2**20),
        name="mlp",
    )(x, ob, obT, cot, wo, wgu, wd, gains)

H, HD = 12, 64
NEG = -1e30
VM = pl.BlockSpec(memory_space=pltpu.VMEM)
def tnt(a,b): return lax.dot_general(a,b,(((0,),(1,)),((),())),preferred_element_type=f32)

def seg_rows(lens_ref, S):
    slot = lax.broadcasted_iota(jnp.int32, (8, S), 1)
    seg = jnp.zeros((8, S), jnp.int32); start = jnp.zeros((8, S), jnp.int32)
    end = jnp.int32(0)
    for s in range(lens_ref.shape[1]-1):
        end = end + lens_ref[0, s]
        past = (slot >= end).astype(jnp.int32)
        seg += past
        start += past * lens_ref[0, s]
    return seg, slot - start


MESH = pl.DeviceIdType.MESH

def flip(v, b):
    return v + b - 2*b*lax.rem(lax.div(v, b), 2)

def places():
    d = lax.axis_index("dp"); z = lax.axis_index("rep")
    sib, xn, yn = flip(d, 1), flip(d, 2), flip(d, 4)
    xy = flip(xn, 4)
    return d, z, sib, xn, yn, xy

def greet(devs):
    bar = pltpu.get_barrier_semaphore()
    for dev in devs:
        pl.semaphore_signal(bar, inc=1, device_id=dev, device_id_type=MESH)
    pl.semaphore_wait(bar, len(devs))

class Gather:
    N = 15
    def __init__(self, ref, view, send, recv, g):
        self.ref, self.view, self.send, self.recv, self.g = ref, view, send, recv, g
        d, z, sib, xn, yn, xy = places()
        zn = flip(z, 1)
        S, X, Y, Z = (sib, z), (xn, z), (yn, z), (d, zn)
        self.moves = [(d, "all", S), (d, "zb", X), (d, "zb", Y),
                      (xn, "zb", S), (xn, "z", Y), (xn, "z", Z),
                      (yn, "zb", S), (yn, "b", X), (yn, "z", Z),
                      (xy, "z", S), (xy, "z", Z), (xy, "b", S),
                      (xn, "o", S), (yn, "o", S), (xy, "o", S)]
        self.after = {1: (3, 4, 5), 2: (6, 7, 8), 4: (9, 10), 7: (11,), 5: (12,), 8: (13,), 10: (14,)}
    def copy(self, k):
        d, part, dev = self.moves[k]
        v = self.view(self.ref, d, part)
        return pltpu.make_async_remote_copy(src_ref=v, dst_ref=v, send_sem=self.send.at[self.g, k], recv_sem=self.recv.at[self.g, k],
                                            device_id=dev, device_id_type=MESH)
    def begin(self):
        for k in (1, 2, 0): self.copy(k).start()
    def got(self, *ks):
        for k in ks:
            self.copy(k).wait_recv()
            for j in self.after.get(k, ()): self.copy(j).start()
    def first(self): self.got(1, 2)
    def second(self): self.got(4, 7, 5, 8)
    def third(self): self.got(10)
    def sibling(self): self.got(0, 3, 6, 9, 11, 12, 13, 14)
    def sent(self):
        for k in range(self.N): self.copy(k).wait_send()

def cut(rows):
    return rows // 3 // 16 * 16


ANY = pl.BlockSpec(memory_space=pl.ANY)
SM = pl.BlockSpec(memory_space=pltpu.SMEM)
B = 256

def spread_gain(pieces, D):
    n, wide = pieces.shape[0], D // pieces.shape[0]
    lane = lax.broadcasted_iota(jnp.int32, (8, 128), 1)
    total = jnp.zeros((8, D), f32)
    for i in range(n):
        row = jnp.concatenate([jnp.where(lane < wide, pieces[i], 0.0), jnp.zeros((8, D - 128), f32)], axis=1)
        total += row if i == 0 else pltpu.roll(row, i*wide, 1)
    return total

def forward_attention(lens_ref, x_ref, freq_ref, gain_of, weights_in, w_ref, qT_s, kT_s, vT_s, oT_s, lse_s, cos_s, sin_s, segc_s, segr_s, bias_s, hook):
    S, D = x_ref.shape
    n = S // B
    seg, place = seg_rows(lens_ref, S)
    ang = jnp.broadcast_to(place[0:1, :].astype(f32), (HD//2, S)) * freq_ref[:, 0:1]
    cos_s[...] = jnp.cos(ang); sin_s[...] = jnp.sin(ang)
    segf = jnp.broadcast_to(seg[0:1, :].astype(f32), (128, S))
    segr_s[...] = segf[0:8]
    segc_s[...] = segf.T
    weights_in()
    gain = gain_of()
    @pl.loop(0, n)
    def _(i):
        t = pl.ds(pl.multiple_of(i*B, B), B)
        xf = x_ref[t, :].astype(f32)
        r = lax.rsqrt(jnp.mean(xf*xf, axis=-1, keepdims=True) + EPS)
        h1 = ((xf*r)*gain).astype(bf16)
        c = cos_s[:, t]; s = sin_s[:, t]
        for w, dst, sc in ((0, qT_s, 0.125), (1, kT_s, 1.0)):
            y = tnt(w_ref[w], h1)
            for h in range(H):
                a = y[h*HD:h*HD+32]; b = y[h*HD+32:h*HD+64]
                dst[h*HD:h*HD+32, t] = ((a*c - b*s)*sc).astype(bf16)
                dst[h*HD+32:h*HD+64, t] = ((b*c + a*s)*sc).astype(bf16)
        vT_s[:, t] = tnt(w_ref[2], h1).astype(bf16)
    hook("proj")
    for i in range(n):
        k0 = max(0, i-2)*B; nk = i*B + B - k0
        q0 = i*B
        kid = lax.broadcasted_iota(jnp.int32, (nk, B), 0) + k0
        qid = lax.broadcasted_iota(jnp.int32, (nk, B), 1) + q0
        ok = (segc_s[k0:k0+nk, 0:1] == segr_s[0:1, q0:q0+B]) & (kid <= qid)
        bias_s[0:nk, :] = jnp.where(ok, 0.0, NEG)
        @pl.loop(0, H//2)
        def _(p):
            for e in range(2):
                rows = pl.ds(pl.multiple_of(p*128 + e*64, 64), 64)
                s = tn(kT_s[rows, k0:k0+nk], qT_s[rows, q0:q0+B]) + bias_s[0:nk, :]
                m = jnp.max(s, axis=0, keepdims=True)
                ex = jnp.exp(s - m)
                l = jnp.sum(ex, axis=0, keepdims=True)
                o = nn(vT_s[rows, k0:k0+nk], ex.astype(bf16)) * (1.0/l)
                oT_s[rows, q0:q0+B] = o.astype(bf16)
                lse_s[pl.ds(p*2+e, 1), q0:q0+B] = m + jnp.log(l)
        hook(i)

def local_body(lens_ref, x_ref, freq_ref, gain_ref, w_ref, qT_ref, kT_ref, vT_ref, oT_ref, lse_ref, cos_ref, sin_ref, segc_ref, segr_ref, bias_s):
    forward_attention(lens_ref, x_ref, freq_ref, lambda: gain_ref[0:1, :], lambda: None, w_ref, qT_ref, kT_ref, vT_ref, oT_ref,
                      lse_ref, cos_ref, sin_ref, segc_ref, segr_ref, bias_s, lambda at: None)

def attn_fwd(lens, x, gains, freq, wqkv):
    S, D = x.shape
    sh = lambda s, d: jax.ShapeDtypeStruct(s, d)
    return pl.pallas_call(local_body,
        in_specs=[SM]+[VM]*4, out_specs=[VM]*9,
        out_shape=[sh((D,S),bf16)]*4 + [sh((16,S),f32), sh((32,S),f32), sh((32,S),f32), sh((S,128),f32), sh((8,S),f32)],
        scratch_shapes=[pltpu.VMEM((768,256),f32)],
        compiler_params=pltpu.CompilerParams(vmem_limit_bytes=62*2**20), name="attend")(lens, x, freq, gains, wqkv)

GW = 256

def backward_attention(x_ref, gain_ref, w_ref, ig_s, ig_ready, ig_done, qT_ref, kT_ref, vT_ref, dob_ref, dobT_ref, lse_ref, cos_ref, sin_ref, segc_ref, segr_ref,
                       dw_s, bias_s, q_s, dqT_s, dk_s, dv_s, g_s, h1T_s, hook):
    S, D = x_ref.shape
    n = S // B
    gain = gain_ref[0:1, :]
    hook("start")
    blocks = []
    at = 0
    for i in range(n):
        k0 = max(0, i-2)*B; nk = i*B + B - k0
        q0 = i*B
        kid = lax.broadcasted_iota(jnp.int32, (nk, B), 0) + k0
        qid = lax.broadcasted_iota(jnp.int32, (nk, B), 1) + q0
        ok = (segc_ref[k0:k0+nk, 0:1] == segr_ref[0:1, q0:q0+B]) & (kid <= qid)
        bias_s[at:at+nk, :] = jnp.where(ok, 0.0, NEG)
        blocks.append((q0, k0, nk, at)); at += nk
    q_s[...] = qT_ref[...].T
    @pl.loop(0, n)
    def _(i):
        t = pl.ds(pl.multiple_of(i*B, B), B)
        xf = x_ref[t, :].astype(f32)
        r = lax.rsqrt(jnp.mean(xf*xf, axis=-1, keepdims=True) + EPS)
        h1T_s[:, t] = ((xf*r)*gain).astype(bf16).T
    hook("ready")
    lane = lax.broadcasted_iota(jnp.int32, (B, 128), 1)
    @pl.loop(0, H//2)
    def _(p):
        cols = pl.ds(pl.multiple_of(p*128, 128), 128)
        dk_s[...] = jnp.zeros_like(dk_s); dv_s[...] = jnp.zeros_like(dv_s)
        for q0, k0, nk, at in blocks:
            dv = dk = None
            for e in range(2):
                rows = pl.ds(pl.multiple_of(p*128 + e*64, 64), 64)
                mine = (lane < 64) if e == 0 else (lane >= 64)
                dobz = jnp.where(mine, dob_ref[q0:q0+B, cols], 0).astype(bf16)
                qz = jnp.where(mine, q_s[q0:q0+B, cols], 0).astype(bf16)
                s = tn(kT_ref[rows, k0:k0+nk], qT_ref[rows, q0:q0+B]) + bias_s[at:at+nk, :]
                pr = jnp.exp(s - lse_ref[pl.ds(p*2+e, 1), q0:q0+B])
                dp = tn(vT_ref[rows, k0:k0+nk], dobT_ref[rows, q0:q0+B])
                inner = jnp.sum(pr*dp, axis=0, keepdims=True)
                ds = (pr*(dp - inner)).astype(bf16)
                dve = nn(pr.astype(bf16), dobz)
                dke = nn(ds, qz)
                dqT_s[e*64:e*64+64, q0:q0+B] = nn(kT_ref[rows, k0:k0+nk], ds) * 0.125
                dv = dve if dv is None else dv + dve
                dk = dke if dk is None else dk + dke
            dv_s[k0:k0+nk, :] += dv
            dk_s[k0:k0+nk, :] += dk
        c = cos_ref[...]; s = sin_ref[...]
        for j, src in ((0, dqT_s[...]), (1, dk_s[...].T)):
            parts = []
            for e in range(2):
                a = src[e*HD:e*HD+32]; b = src[e*HD+32:e*HD+64]
                parts += [a*c + b*s, b*c - a*s]
            g_s[j, :, cols] = jnp.concatenate(parts, axis=0).astype(bf16).T
        g_s[2, :, cols] = dv_s[...].astype(bf16)
        @pl.when(lax.rem(p, 2) == 1)
        def _():
            g = lax.div(p, 2)
            wide = pl.ds(pl.multiple_of(g*GW, GW), GW)
            for j in range(3):
                dw_s[g, j] = nn(h1T_s[...], g_s[j, :, wide]).astype(bf16)
        for k in range(H//2):
            @pl.when(p == k)
            def _():
                hook(k)
    ig_ready()
    for i in range(n):
        t = pl.ds(i*B, B)
        xf = x_ref[t, :].astype(f32)
        r = lax.rsqrt(jnp.mean(xf*xf, axis=-1, keepdims=True) + EPS)
        xh = xf*r
        dh = nt(g_s[0, t, :], w_ref[0]) + nt(g_s[1, t, :], w_ref[1]) + nt(g_s[2, t, :], w_ref[2])
        w = dh*gain
        ig_s[t, :] += r*(w - xh*jnp.mean(w*xh, axis=-1, keepdims=True))
        ig_done(i, t)
        hook("tile%d" % i)

def scratch_bwd(S, D):
    n = S // B
    area = sum(min(i+1, 3) for i in range(n))*B
    return [pltpu.VMEM((D//GW, 3, D, GW), bf16), pltpu.VMEM((area, B), f32), pltpu.VMEM((S, D), bf16), pltpu.VMEM((128, S), f32),
            pltpu.VMEM((S, 128), f32), pltpu.VMEM((S, 128), f32), pltpu.VMEM((3, S, D), bf16), pltpu.VMEM((D, S), bf16)]

def bwd_local_body(x_ref, gain_ref, w_ref, dmid_ref, qT_ref, kT_ref, vT_ref, dob_ref, dobT_ref, lse_ref, cos_ref, sin_ref, segc_ref, segr_ref,
                   ig_ref, dw_ref, bias_s, q_s, dqT_s, dk_s, dv_s, g_s, h1T_s):
    ig_ref[...] = dmid_ref[...]
    backward_attention(x_ref, gain_ref, w_ref, ig_ref, lambda: None, lambda i, t: None, qT_ref, kT_ref, vT_ref, dob_ref, dobT_ref, lse_ref, cos_ref, sin_ref,
                       segc_ref, segr_ref, dw_ref, bias_s, q_s, dqT_s, dk_s, dv_s, g_s, h1T_s, lambda at: None)

def attn_bwd(x, gains, wqkv, dmid, qT, kT, vT, dob, dobT, lse, cos, sin, segc, segr):
    S, D = x.shape
    sh = lambda s, d: jax.ShapeDtypeStruct(s, d)
    ig, dw = pl.pallas_call(bwd_local_body,
        in_specs=[VM]*14, out_specs=[VM]*2,
        out_shape=[sh((S,D),f32), sh((D//GW,3,D,GW),bf16)],
        scratch_shapes=scratch_bwd(S, D)[1:],
        compiler_params=pltpu.CompilerParams(vmem_limit_bytes=62*2**20), name="attend_back")(x, gains, wqkv, dmid, qT, kT, vT, dob, dobT, lse, cos, sin, segc, segr)
    return ig, jnp.moveaxis(dw, 0, 2).reshape(3, D, D)


FC, MT = 512, 512

def staggered(items, first, middle, last, at=None, between=None):
    a = first(items[0]); prev = None
    for i, it in enumerate(items):
        nxt = first(items[i+1]) if i + 1 < len(items) else None
        m = middle(it, a)
        if prev is not None: last(items[i-1], prev)
        if i == at: between()
        prev, a = m, nxt
    last(items[-1], prev)

class Sum(object):
    def __init__(self, u, piece, other, rs, rx, r2, zr, out, send, recv, loc):
        self.u, self.piece, self.other, self.rs, self.rx, self.r2, self.zr, self.out = u, piece, other, rs, rx, r2, zr, out
        self.send, self.recv, self.loc = send, recv, loc
        self.d, self.z, self.sib, self.xn, self.yn, self.xy = places()
        self.rows = rs.shape[-2]; self.half = self.rows // 2
        self.inner = (self.z == 1) | (self.z == 2)
    def cut(self, ref, h):
        s = slice(0, self.half) if h == 0 else slice(self.half, self.rows)
        return ref.at[..., s, :]
    def copy(self, k, src, dst, dev):
        return pltpu.make_async_remote_copy(src_ref=src, dst_ref=dst, send_sem=self.send.at[self.u, k], recv_sem=self.recv.at[self.u, k],
                                            device_id=dev, device_id_type=MESH)
    def s_copy(self, j): return self.copy(j, self.other(j), self.rs.at[j], (self.sib, self.z))
    def x_copies(self):
        X, Y = (self.xn, self.z), (self.yn, self.z)
        return [self.copy(4, self.piece(1, 0), self.cut(self.rx.at[0], 0), X), self.copy(5, self.piece(3, 0), self.cut(self.rx.at[1], 0), X),
                self.copy(6, self.piece(2, 1), self.cut(self.rx.at[0], 1), Y), self.copy(7, self.piece(3, 1), self.cut(self.rx.at[1], 1), Y)]
    def y_copies(self):
        return [self.copy(8, self.piece(2, 0), self.cut(self.r2, 0), (self.yn, self.z)), self.copy(9, self.piece(1, 1), self.cut(self.r2, 1), (self.xn, self.z))]
    def z_copy(self, k):
        zn = (self.d, flip(self.z, 1))
        if k == 0: return self.copy(10, self.piece(0, None), self.zr.at[0], zn)
        if k == 1: return self.copy(11, self.zr.at[0], self.zr.at[1], (self.d, 3 - self.z))
        return self.copy(12, self.piece(0, None), self.zr.at[0], zn)
    def fin(self, inner): return pltpu.make_async_copy(self.piece(0, None) if inner else self.zr.at[0], self.out, self.loc)
    def add(self, dst, a, b):
        if len(dst.shape) == 2: dst[...] = a[...] + b[...]
        else:
            for i in range(dst.shape[0]): dst[i] = a[i] + b[i]
    def a(self):
        for j in (3, 1, 2, 0): self.s_copy(j).start()
    def b(self):
        xs = self.x_copies()
        for j in (3, 1, 2, 0):
            self.s_copy(j).wait_recv()
            p = self.piece(j, None)
            self.add(p, p, self.rs.at[j])
            for k in {3: (1, 3), 1: (0,), 2: (2,), 0: ()}[j]: xs[k].start()
    def c(self):
        for k in self.x_copies(): k.wait_recv()
        ys = self.y_copies()
        for j, h, k in ((2, 0, 0), (1, 1, 1)):
            p = self.piece(j, h)
            self.add(p, p, self.cut(self.rx.at[1], h))
            ys[k].start()
        p = self.piece(0, None)
        self.add(p, p, self.rx.at[0])
    def e(self):
        for k in self.y_copies(): k.wait_recv()
        p = self.piece(0, None)
        self.add(p, p, self.r2)
        @pl.when(jnp.logical_not(self.inner))
        def _(): self.z_copy(0).start()
    def f(self):
        @pl.when(self.inner)
        def _():
            self.z_copy(0).wait_recv()
            self.add(self.zr.at[0], self.zr.at[0], self.piece(0, None))
            self.z_copy(1).start()
    def g(self):
        @pl.when(self.inner)
        def _():
            self.z_copy(1).wait_recv()
            self.add(self.piece(0, None), self.zr.at[0], self.zr.at[1])
            self.z_copy(2).start()
            self.fin(True).start()
    def h(self):
        @pl.when(jnp.logical_not(self.inner))
        def _():
            self.z_copy(2).wait_recv()
            self.fin(False).start()
    def drain(self):
        for j in range(4): self.s_copy(j).wait_send()
        for k in self.x_copies() + self.y_copies(): k.wait_send()
        @pl.when(self.inner)
        def _():
            self.z_copy(1).wait_send(); self.z_copy(2).wait_send()
            self.fin(True).wait()
        @pl.when(jnp.logical_not(self.inner))
        def _():
            self.z_copy(0).wait_send()
            self.fin(False).wait()

def layer_body(n_dp, lens_ref, gain_ref, x_hbm, cot_hbm, qw_hbm, ow_hbm, gw_hbm, dw_hbm,
               out_o, ig_o, gq_o, gou_o, ggu_o, gdn_o,
               wq_s, wo_s, wgu_s, wd_s, qT_s, kT_s, vT_s, oT_s, cos_s, sin_s, segc_s, segr_s, lse_s, dlt_s, gain_s, gp_s,
               out_s, dh2_s, mid_s, acc_s, h2T_s, dfb_s, ch_s, dw2_s,
               g_rs, g_rx, g_r2, g_z, n_rs, n_rx, n_r2, n_z, o_rs, o_rx, o_r2, o_z, q_rs, q_rx, q_r2, q_z,
               ag_send, ag_recv, gn_send, gn_recv, rs_send, rs_recv, rs_loc, loc):
    S, D = x_hbm.shape
    x_s, h1T_s, h1T_late = dfb_s, h2T_s, oT_s
    nf = wd_s.shape[0]
    FF = nf*FC
    n, ng = S//B, len(HEADS_IN)
    rq, rd = D//n_dp, FF//n_dp
    sub = rd//nf
    d, z, sib, xn, yn, xy = places()
    owners = [d, xn, yn, xy]
    others = [lax.rem(d + j, n_dp) for j in range(1, n_dp)]
    gp_s[...] = jnp.zeros_like(gp_s)
    bar = pltpu.get_barrier_semaphore()
    met = [(o, z) for o in others] + [(d, flip(z, 1)), (d, 3 - z)]
    for dev in met: pl.semaphore_signal(bar, inc=1, device_id=dev, device_id_type=MESH)

    def rows(o, r): return pl.ds(pl.multiple_of(o*r, 16), r)
    loads = {}
    def load(key, src, dst):
        c = pltpu.make_async_copy(src, dst, loc.at[len(loads)]); c.start(); loads[key] = c
    for c in range(3): load("q%d" % c, qw_hbm.at[c], out_s.at[c*rq:(c+1)*rq, :])
    load("x", x_hbm, x_s)
    load("o", ow_hbm, out_s.at[3*rq:4*rq, :])
    load("d", dw_hbm, out_s.at[4*rq:4*rq+rd, :])
    wides = [(a, min(D, FF - a)) for a in range(0, FF, D)]
    for c in range(2):
        for k, (a, w) in enumerate(wides):
            load("g%d%d" % (c, k), gw_hbm.at[c, :, a:a+w], dh2_s.at[(c*len(wides)+k)*rq:(c*len(wides)+k+1)*rq, 0:w])
    cot_base = len(loads)
    base = cot_base + 4
    HB = B//2
    def cot_copies(i): return [pltpu.make_async_copy(cot_hbm.at[(i % n)*B + k*HB:(i % n)*B + (k+1)*HB, :], acc_s.at[i % 2 * 2 + k, :, 0:D],
                                                     loc.at[cot_base + i % 2 * 2 + k]) for k in range(2)]
    def cot_start(i):
        for c in cot_copies(i): c.start()
    def cot_get(i):
        for c in cot_copies(i): c.wait()
        return jnp.concatenate([acc_s[i % 2 * 2 + k, :, 0:D] for k in range(2)], axis=0)
    cot_start(0); cot_start(1)

    def rv(r, lead, cols=None):
        a = cut(r)
        p = lax.rem(z, 2)
        def view(ref, o, part):
            off, m = {"all": (0, r), "zb": (p*a, r - a), "z": (p*(r - a), a), "b": (a, r - 2*a), "o": ((1 - p)*(r - a), a)}[part]
            s = pl.ds(pl.multiple_of(o*r + off, 16), m)
            if not lead: return ref.at[s, :]
            return ref.at[:, s, :] if cols is None else ref.at[:, s, cols]
        return view
    G = [Gather(wq_s.at[c], rv(rq, False), ag_send, ag_recv, c) for c in range(3)]
    G.append(Gather(wo_s, rv(rq, False), ag_send, ag_recv, 3))
    of_gu, of_dn = [], []
    for f in range(nf):
        of_gu.append(len(G))
        G.append(Gather(wgu_s, rv(rq, True, slice(f*FC, (f+1)*FC)), ag_send, ag_recv, len(G)))
        if f % 2 == 0:
            of_dn.append(len(G))
            G.append(Gather(wd_s.at[f:f+2], rv(sub, True), ag_send, ag_recv, len(G)))

    def unit(u, ref, r, lead, cols, bufs, out):
        def piece(j, h):
            o, m = (0, r) if h is None else (h*(r//2), r//2)
            s = pl.ds(pl.multiple_of(owners[j]*r + o, 16), m)
            return ref.at[:, s, cols] if lead else ref.at[s, :]
        def other(j):
            s = rows(flip(owners[j], 1), r)
            return ref.at[:, s, cols] if lead else ref.at[s, :]
        return Sum(u, piece, other, *bufs, out, rs_send, rs_recv, rs_loc.at[u])
    R = []
    for f in range(nf):
        cols = slice(f*FC, (f+1)*FC)
        R.append(unit(f, wgu_s, rq, True, cols, [b.at[f] for b in (g_rs, g_rx, g_r2, g_z)], ggu_o.at[:, :, cols]))
    for h in range(nf//2):
        R.append(unit(nf+h, wd_s.at[2*h:2*h+2], sub, True, slice(None), [b.at[h] for b in (n_rs, n_rx, n_r2, n_z)], gdn_o.at[2*h:2*h+2]))
    R.append(unit(nf+nf//2, wo_s, rq, False, None, (o_rs, o_rx, o_r2, o_z), gou_o))
    groups, c0 = [], 0
    for g, many in enumerate(HEADS_IN):
        w = many*HD
        r = ch_s.at[:, 0:D, g*GW:g*GW+w] if (g+1)*GW <= FC else dw2_s.at[:, :, c0-(D-GW):c0-(D-GW)+w]
        groups.append((slice(c0, c0+w), r))
        R.append(unit(nf+nf//2+1+g, r, rq, True, slice(None), [b.at[..., c0:c0+w] for b in (q_rs, q_rx, q_r2, q_z)], gq_o.at[:, :, c0:c0+w]))
        c0 += w
    done = [sum(HEADS_IN[:g+1])//2 - 1 for g in range(ng)]
    def hook(at):
        for what in PLAN.get(at, ()):
            k = int(what[1:])
            if what[0] == "B": G[k].begin()
            elif what[0] in "1234": getattr(G[k], ("first", "second", "third", "sibling")[int(what[0])-1])()
            else: getattr(R[k], what[0])()

    gp_s[pl.ds(d, 1), 0:2, 0:gain_ref.shape[1]] = gain_ref[...].astype(bf16).astype(f32)[None]
    for c in range(3):
        loads["q%d" % c].wait()
        wq_s[c, rows(d, rq), :] = out_s[c*rq:(c+1)*rq, :].astype(bf16)
        if c == 0:
            pl.semaphore_wait(bar, len(met))
            gains = [pltpu.make_async_remote_copy(src_ref=gp_s.at[d], dst_ref=gp_s.at[d], send_sem=gn_send.at[j], recv_sem=gn_recv.at[j],
                                                  device_id=(o, z), device_id_type=MESH) for j, o in enumerate(others)]
        hook("begin%d" % c)
        if c == 0:
            for k in gains: k.start()
    loads["o"].wait()
    wo_s[rows(d, rq), :] = out_s[3*rq:4*rq, :].astype(bf16)
    hook("s0")
    for k in loads:
        if k[0] == "g": loads[k].wait()
    for c in range(2):
        def at(col):
            k = col//D
            return dh2_s[(c*len(wides)+k)*rq:(c*len(wides)+k+1)*rq, col - k*D:col - k*D + sub]
        for f in range(nf):
            for o in range(0, n_dp, 2):
                two = jnp.concatenate([at(o*rd + f*sub), at((o+1)*rd + f*sub)], axis=1)
                wgu_s[c, rows(d, rq), f*FC + o*sub:f*FC + (o+2)*sub] = two.astype(bf16)
    loads["d"].wait()
    for f in range(nf): wd_s[f, rows(d, sub), :] = out_s[4*rq + f*sub:4*rq + (f+1)*sub, :].astype(bf16)
    hook("s1")

    seg, place = seg_rows(lens_ref, S)
    half = lax.broadcasted_iota(jnp.int32, (HD//2, 128), 0).astype(f32)
    freq = jnp.exp(half*(-math.log(10000.0)/(HD//2)))
    ang = jnp.broadcast_to(place[0:1, :].astype(f32), (HD//2, S)) * freq[:, 0:1]
    cos_s[...] = jnp.cos(ang); sin_s[...] = jnp.sin(ang)
    segf = jnp.broadcast_to(seg[0:1, :].astype(f32), (128, S))
    segr_s[...] = segf[0:8]
    segc_s[...] = segf.astype(bf16).T
    hook("s2")
    blocks = []
    at = {0: (0, 0), 1: (B, 0), 2: (0, B), 3: (0, 2*B)}
    for i in range(n):
        k0 = max(0, i-2)*B
        blocks.append((i*B, k0, i*B + B - k0) + at[i])
    def masks():
        for q0, k0, nk, r0, c0 in blocks:
            kid = lax.broadcasted_iota(jnp.int32, (nk, B), 0) + k0
            qid = lax.broadcasted_iota(jnp.int32, (nk, B), 1) + q0
            ok = (segc_s[k0:k0+nk, 0:1].astype(f32) == segr_s[0:1, q0:q0+B]) & (kid <= qid)
            dh2_s[r0:r0+nk, c0:c0+B] = jnp.where(ok, 0.0, NEG)
    masks()
    loads["x"].wait()
    hook("s3")
    for k in gains: k.wait_recv()
    gain_s[...] = spread_gain(gp_s[...], D)
    def normed(dst):
        @pl.loop(0, n)
        def _(i):
            t = pl.ds(pl.multiple_of(i*B, B), B)
            xf = x_s[t, :].astype(f32)
            r = lax.rsqrt(jnp.mean(xf*xf, axis=-1, keepdims=True) + EPS)
            dst[:, t] = ((xf*r)*gain_s[0:1, :]).astype(bf16).T
    normed(h1T_s)
    hook("start")
    for w, dst, sc in ((0, qT_s, 0.125), (1, kT_s, 1.0), (2, vT_s, None)):
        hook("proj%d" % w)
        for t0 in range(0, S, MT):
            t = slice(t0, t0+MT)
            y = tn(wq_s[w], h1T_s[:, t])
            if sc is None: dst[:, t] = y.astype(bf16)
            else:
                c = cos_s[:, t]; s = sin_s[:, t]
                for h in range(H):
                    a = y[h*HD:h*HD+32]; b = y[h*HD+32:h*HD+64]
                    dst[h*HD:h*HD+32, t] = ((a*c - b*s)*sc).astype(bf16)
                    dst[h*HD+32:h*HD+64, t] = ((b*c + a*s)*sc).astype(bf16)

    @pl.loop(0, H//2)
    def _(p):
        rs = [pl.ds(pl.multiple_of(p*128 + e*64, 64), 64) for e in range(2)]
        def scores(it):
            (q0, k0, nk, r0, c0), e = it
            return tn(kT_s[rs[e], k0:k0+nk], qT_s[rs[e], q0:q0+B]) + dh2_s[r0:r0+nk, c0:c0+B]
        def soft(it, s):
            m = jnp.max(s, axis=0, keepdims=True)
            ex = jnp.exp(s - m)
            return m, ex.astype(bf16), jnp.sum(ex, axis=0, keepdims=True)
        def mix(it, mel):
            (q0, k0, nk, r0, c0), e = it
            m, ex, l = mel
            oT_s[rs[e], q0:q0+B] = (nn(vT_s[rs[e], k0:k0+nk], ex) * (1.0/l)).astype(bf16)
            lse_s[pl.ds(p*2+e, 1), q0:q0+B] = m + jnp.log(l)
        staggered([(b, e) for b in blocks for e in range(2)], scores, soft, mix)
        for k in range(H//2):
            @pl.when(p == k)
            def _(): hook("a%d" % k)

    hook("mlp")
    gain2 = gain_s[1:2, :]
    for i in range(n):
        t = slice(i*B, (i+1)*B)
        mid = x_s[t, :].astype(f32) + tn(oT_s[:, t], wo_s[...])
        out_s[t, :] = mid; mid_s[t, :] = mid
        r = lax.rsqrt(jnp.mean(mid*mid, axis=-1, keepdims=True) + EPS)
        h2T_s[:, t] = ((mid*r)*gain2).astype(bf16).T
        dfb_s[t, :] = cot_get(i).astype(bf16)
        cot_start(i+2)
        dh2_s[t, :] = jnp.zeros_like(mid)
    @pl.loop(0, nf)
    def _(f):
        cols = pl.ds(pl.multiple_of(f*FC, FC), FC)
        def first(i):
            t = slice(i*MT, (i+1)*MT)
            return tn(h2T_s[:, t], wgu_s[0, :, cols]), tn(h2T_s[:, t], wgu_s[1, :, cols]), nt(dfb_s[t, :], wd_s[f])
        def middle(i, gud):
            g, u, dh = gud
            t = slice(i*MT, (i+1)*MT)
            sig = 0.5*jnp.tanh(0.5*g) + 0.5
            silu = g*sig
            hid = (silu*u).astype(bf16)
            dg = (dh*u*(sig + silu*(1.0 - sig))).astype(bf16)
            du = (dh*silu).astype(bf16)
            ch_s[0, t, :] = hid; ch_s[1, t, :] = dg; ch_s[2, t, :] = du
            if i == 0:
                for k in range(nf):
                    @pl.when(f == k)
                    def _(): hook("f%dmid" % k)
            return hid, dg, du
        def last(i, hdd):
            hid, dg, du = hdd
            t = slice(i*MT, (i+1)*MT)
            out_s[t, :] += nn(hid, wd_s[f])
            dh2_s[t, :] += nt(dg, wgu_s[0, :, cols]) + nt(du, wgu_s[1, :, cols])
        staggered(list(range(S//MT)), first, middle, last)
        for k in range(nf):
            @pl.when(f == k)
            def _():
                for g in [of_gu[k]] + ([of_dn[k//2]] if k % 2 == 0 else []): G[g].sent()
        wgu_s[0, :, cols] = nn(h2T_s[...], ch_s[1]).astype(bf16)
        wgu_s[1, :, cols] = nn(h2T_s[...], ch_s[2]).astype(bf16)
        wd_s[f] = tn(ch_s[0], dfb_s[...]).astype(bf16)
        for k in range(nf):
            @pl.when(f == k)
            def _(): hook("f%dend" % k)
    out_c = pltpu.make_async_copy(out_s, out_o, loc.at[base]); out_c.start()
    for i in range(n):
        t = slice(i*B, (i+1)*B)
        mid = mid_s[t, :]; dh = dh2_s[t, :]
        r = lax.rsqrt(jnp.mean(mid*mid, axis=-1, keepdims=True) + EPS)
        xh = mid*r; w = dh*gain2
        dmid = cot_get(i) + r*(w - xh*jnp.mean(w*xh, axis=-1, keepdims=True))
        if i + 2 < n: cot_start(i+2)
        mid_s[t, :] = dmid
        dab = dmid.astype(bf16)
        dfb_s[t, :] = dab
        h2T_s[:, t] = nt(wo_s[...], dab).astype(bf16)
        if i == 1: hook("e0")
    G[3].sent()
    wo_s[...] = nn(oT_s[...], dfb_s[...]).astype(bf16)
    x_again = pltpu.make_async_copy(x_hbm, x_s, loc.at[0]); x_again.start()
    for h in range(H):
        r = slice(h*HD, (h+1)*HD)
        dlt_s[h:h+1, :] = jnp.sum(h2T_s[r, :].astype(f32)*oT_s[r, :].astype(f32), axis=0, keepdims=True)
    masks()
    hook("e1")
    x_again.wait()
    normed(h1T_late)

    dq_s, dk_s, dv_s = (acc_s.at[j] for j in range(3))
    @pl.loop(0, H//2)
    def _(p):
        rs = [pl.ds(pl.multiple_of(p*128 + e*64, 64), 64) for e in range(2)]
        dk_s[...] = jnp.zeros_like(dk_s); dv_s[...] = jnp.zeros_like(dv_s)
        def first(it):
            (q0, k0, nk, r0, c0), e = it
            return (tn(kT_s[rs[e], k0:k0+nk], qT_s[rs[e], q0:q0+B]) + dh2_s[r0:r0+nk, c0:c0+B],
                    tn(vT_s[rs[e], k0:k0+nk], h2T_s[rs[e], q0:q0+B]))
        def middle(it, sd):
            (q0, k0, nk, r0, c0), e = it
            s, dp = sd
            pr = jnp.exp(s - lse_s[pl.ds(p*2+e, 1), q0:q0+B])
            return pr.astype(bf16), (pr*(dp - dlt_s[pl.ds(p*2+e, 1), q0:q0+B])).astype(bf16)
        def last(it, pd):
            (q0, k0, nk, r0, c0), e = it
            pr, ds = pd
            r = slice(e*HD, (e+1)*HD)
            dv_s[r, k0:k0+nk] += nt(h2T_s[rs[e], q0:q0+B], pr)
            dk_s[r, k0:k0+nk] += nt(qT_s[rs[e], q0:q0+B], ds)
            dq_s[r, q0:q0+B] = nn(kT_s[rs[e], k0:k0+nk], ds) * 0.125
        def half():
            for k in range(H//2):
                @pl.when(p == k)
                def _(): hook("c%da" % k)
        staggered([(b, e) for b in blocks for e in range(2)], first, middle, last, 5, half)
        c = cos_s[...]; s = sin_s[...]
        for src, dst in ((dq_s, qT_s), (dk_s, kT_s)):
            for e in range(2):
                a = src[e*HD:e*HD+32, :]; b = src[e*HD+32:(e+1)*HD, :]
                dst[pl.ds(pl.multiple_of(p*128 + e*64, 32), 32), :] = (a*c + b*s).astype(bf16)
                dst[pl.ds(pl.multiple_of(p*128 + e*64 + 32, 32), 32), :] = (b*c - a*s).astype(bf16)
        vT_s[pl.ds(pl.multiple_of(p*128, 128), 128), :] = dv_s[...].astype(bf16)
        for k in range(H//2):
            @pl.when(p == k)
            def _():
                if k in done:
                    cols, r = groups[done.index(k)]
                    for j, src in enumerate((qT_s, kT_s, vT_s)):
                        r[j] = nt(h1T_late[...], src[cols, :]).astype(bf16)
                hook("c%d" % k)
    def ig_copy(i): return pltpu.make_async_copy(mid_s.at[i*B:(i+1)*B, :], ig_o.at[i*B:(i+1)*B, :], loc.at[base + 1 + i])
    gain1 = gain_s[0:1, :]
    for i in range(n):
        t = slice(i*B, (i+1)*B)
        xf = x_s[t, :].astype(f32)
        r = lax.rsqrt(jnp.mean(xf*xf, axis=-1, keepdims=True) + EPS)
        xh = xf*r
        dh = tnt(qT_s[:, t], wq_s[0]) + tnt(kT_s[:, t], wq_s[1]) + tnt(vT_s[:, t], wq_s[2])
        w = dh*gain1
        mid_s[t, :] += r*(w - xh*jnp.mean(w*xh, axis=-1, keepdims=True))
        ig_copy(i).start()
        hook("t%d" % i)
    hook("end")
    for g in range(3): G[g].sent()
    for k in gains: k.wait_send()
    for u in R: u.drain()
    out_c.wait()
    for i in range(n): ig_copy(i).wait()

HEADS_IN = (4, 4, 2, 2)
PLAN = {
    "begin0": ("B0",),
    "begin1": ("B1",),
    "begin2": ("B2",),
    "s2": ("10",),
    "s3": ("11", "B3"),
    "start": ("20", "12", "B4"),
    "proj0": ("21", "30", "40", "13", "B5"),
    "proj1": ("22", "31", "41"),
    "proj2": ("23", "14", "B6", "32", "42"),
    "a0": ("33", "15", "B7", "24", "43"),
    "a1": ("16", "B8"),
    "a2": ("25",),
    "a3": ("34", "17", "B9"),
    "a4": ("44", "26", "18", "35"),
    "a5": ("45", "27"),
    "f0mid": ("36", "37", "28", "19", "46", "47"),
    "f0end": ("a0", "38", "29"),
    "f1mid": ("48", "39", "b0", "49"),
    "f1end": ("a1", "a4", "c0"),
    "f2mid": ("b1", "b4", "e0"),
    "f2end": ("a2", "c1"),
    "f3mid": ("f0", "c4", "b2"),
    "f3end": ("a3", "a5", "g0", "e1", "e4"),
    "e0": ("c2", "b3", "b5"),
    "e1": ("a6", "h0", "f1", "e2"),
    "c0a": ("f4", "c3", "b6"),
    "c0": ("g1", "f2"),
    "c1a": ("c5", "e3"),
    "c1": ("a7", "g4"),
    "c2a": ("h1", "c6", "b7", "g2", "f3", "e5"),
    "c3a": ("h4", "e6"),
    "c3": ("a8", "g3", "f5", "c7"),
    "c4a": ("h2", "f6", "b8"),
    "c4": ("a9", "e7"),
    "c5a": ("g5", "c8", "b9", "h3", "f7", "g6"),
    "c5": ("a10",),
    "t0": ("e8", "b10", "c9"),
    "t1": ("g7", "f8"),
    "t2": ("h5", "c10", "e9", "f9"),
    "end": ("h6", "e10", "h7", "f10", "g8", "g9", "g10", "h8", "h9", "h10"),
}


def layer(n_dp, lens, gains, x, cot, qw, ow, gw, dw):
    S, D = x.shape
    FF = gw.shape[2]
    sh = lambda s, d: jax.ShapeDtypeStruct(s, d)
    b = lambda *s: pltpu.VMEM(s, bf16)
    w = lambda *s: pltpu.VMEM(s, f32)
    rq, rd, nf, ng = D//n_dp, FF//n_dp, FF//FC, len(HEADS_IN)
    ag, rs = 4 + nf + nf//2, nf + nf//2 + 1 + ng
    dma = pltpu.SemaphoreType.DMA
    def bufs(*lead_piece, many=None):
        m = () if many is None else (many,)
        return [b(*m, 4, *lead_piece), b(*m, 2, *lead_piece), b(*m, *lead_piece), b(*m, 2, *lead_piece)]
    return pl.pallas_call(functools.partial(layer_body, n_dp),
        in_specs=[SM, VM] + [ANY]*6, out_specs=[ANY]*6,
        out_shape=[sh((S,D),f32), sh((S,D),f32), sh((3,rq,D),bf16), sh((rq,D),bf16), sh((2,rq,FF),bf16), sh((nf,rd//nf,D),bf16)],
        scratch_shapes=[b(3,D,D), b(D,D), b(2,D,FF), b(nf,FC,D), b(D,S), b(D,S), b(D,S), b(D,S),
                        w(HD//2,S), w(HD//2,S), b(S,128), w(8,S), w(16,S), w(16,S), w(8,D), w(n_dp,8,128),
                        w(S,D), w(S,D), w(S,D), w(4,128,S), b(D,S), b(S,D), b(3,S,FC), b(3,D,GW)]
            + bufs(2,rq,FC,many=nf) + bufs(2,rd//nf,D,many=nf//2) + bufs(rq,D) + bufs(3,rq,D)
            + [dma((ag,15)), dma((ag,15)), dma((n_dp-1,)), dma((n_dp-1,)), dma((rs,13)), dma((rs,13)), dma((rs,)), dma((24,))],
        compiler_params=pltpu.CompilerParams(collective_id=0, has_side_effects=True, vmem_limit_bytes=63*2**20),
        cost_estimate=pl.CostEstimate(flops=55*10**9, bytes_accessed=40*10**6, transcendentals=20*10**6),
        name="layer")(lens, gains, x, cot, qw, ow, gw, dw)

def can_fuse(n_dp, n_rep, S, D, FF, *rows):
    return n_dp == 8 and n_rep == 4 and S == 4*B and D % GW == 0 and FF == 4*FC and FC == n_dp*64 and sum(HEADS_IN) == H and all(r % 32 == 0 for r in rows)


def adam_body(sub, qg, og, gg, dg, qw, ow, gw, dw, nw, qm, om, gm, dm, nm, qv, ov, gv, dv, nv,
              qm_o, om_o, gm_o, dm_o, nm_o, qv_o, ov_o, gv_o, dv_o, nv_o, qw_o, ow_o, gw_o, dw_o, nw_o, acc_s, gg_s):
    i = pl.program_id(0)
    R = ow.shape[0]
    FF = gg.shape[2]
    nf = dg.shape[0]
    n_dp = FF//(nf*sub)
    for c in range(2):
        for o in range(n_dp):
            for f in range(0, nf, 2):
                a = f*n_dp*sub + o*sub
                b = a + n_dp*sub
                gg_s[c, :, (o*nf + f)*sub:(o*nf + f + 2)*sub] = jnp.concatenate([gg[c, :, a:a+sub], gg[c, :, b:b+sub]], axis=1).astype(f32)
    for g, w_ref, m_ref, v_ref, mo, vo, wo in ((qg[...].astype(f32), qw, qm, qv, qm_o, qv_o, qw_o), (og[...].astype(f32), ow, om, ov, om_o, ov_o, ow_o),
                                              (gg_s[...], gw, gm, gv, gm_o, gv_o, gw_o), (dg[...].astype(f32).reshape(dw.shape), dw, dm, dv, dm_o, dv_o, dw_o)):
        mo[...], vo[...], wo[...] = adam_step(w_ref[...], g, m_ref[...], v_ref[...], matrix_rate, weight_decay)
    rows = pl.ds(pl.multiple_of(i*R, 8), R)
    for k, (g_ref, w_ref) in enumerate(((qg, qw), (gg_s, gw))):
        s = jnp.sum(g_ref[...].astype(f32) * w_ref[...].astype(bf16).astype(f32), axis=0)
        acc_s[k, rows, :] = jnp.broadcast_to(jnp.sum(s, axis=1, keepdims=True), (R, 128))
    @pl.when(i == pl.num_programs(0)-1)
    def _():
        g = jnp.concatenate([acc_s[k].T[0:1, :] for k in range(2)], axis=0) / nw[...].astype(bf16).astype(f32)
        nm_o[...], nv_o[...], nw_o[...] = adam_step(nw[...], g, nm[...], nv[...], gain_rate, 0.0)

def adam_all(grads, weights, moments, seconds, steps):
    q, o, g, d = grads
    rq, D = o.shape
    def spec(a):
        if a.ndim == 3 and a.shape[1] == rq: return pl.BlockSpec((a.shape[0], rq//steps, a.shape[2]), lambda i: (0, i, 0))
        if a.shape[0] == rq: return pl.BlockSpec((rq//steps, D), lambda i: (i, 0))
        if a.ndim == 3: return pl.BlockSpec(a.shape[:2] + (D//steps,), lambda i: (0, 0, i))
        return pl.BlockSpec((a.shape[0], D//steps), lambda i: (0, i))
    small = pl.BlockSpec(weights[4].shape, lambda i: (0, 0))
    four = [spec(a) for a in weights[:4]]
    sh = [jax.ShapeDtypeStruct(w.shape, f32) for w in weights]
    return pl.pallas_call(functools.partial(adam_body, d.shape[1]), grid=(steps,),
        in_specs=[spec(a) for a in grads] + (four + [small])*3, out_specs=(four + [small])*3, out_shape=sh*3,
        scratch_shapes=[pltpu.VMEM((2, rq, 128), f32), pltpu.VMEM((2, rq//steps, g.shape[2]), f32)],
        compiler_params=pltpu.CompilerParams(vmem_limit_bytes=63*2**20), name="adamw")(*grads, *weights, *moments, *seconds)

def adam_step(weight, grad_sum, moment, second, rate, decay):
    moment_new = beta_one * moment + (1.0 - beta_one) * grad_sum
    second_new = beta_two * second + (1.0 - beta_two) * grad_sum * grad_sum
    moment_hat = moment_new / (1.0 - beta_one**STEP)
    second_hat = second_new / (1.0 - beta_two**STEP)
    weight_new = weight - rate * (moment_hat / (jnp.sqrt(second_hat) + adam_eps) + decay * weight)
    return (moment_new, second_new, weight_new)


def per_device(tokens, seg_lens, cotangent, qkv_w, out_w, gu_w, down_w, gains,
               qkv_m, qkv_v, out_m, out_v, gu_m, gu_v, down_m, down_v, gain_m, gain_v):
    _, S, D = tokens.shape
    x = tokens.reshape(S, D)
    cot = cotangent.reshape(S, D)
    gain_low = gains.astype(bf16)
    n_dp, n_rep = lax.axis_size("dp"), lax.axis_size("rep")
    if can_fuse(n_dp, n_rep, S, D, gu_w.shape[2], qkv_w.shape[1], out_w.shape[0], gu_w.shape[1], down_w.shape[0]):
        output, input_grad, *grads = layer(n_dp, seg_lens, gains, x, cot, qkv_w, out_w, gu_w, down_w)
        new = adam_all(grads, (qkv_w, out_w, gu_w, down_w, gains), (qkv_m, out_m, gu_m, down_m, gain_m), (qkv_v, out_v, gu_v, down_v, gain_v), qkv_w.shape[1]//16)
        states = tuple(new[5*k + a] for a in range(5) for k in range(3))
        return (output.reshape(tokens.shape), input_grad.reshape(tokens.shape)) + states
    else:
        wqkv = lax.all_gather(qkv_w.astype(bf16), "dp", axis=1, tiled=True)
        gain_full = lax.all_gather(gain_low, "dp", axis=1, tiled=True).astype(f32)
        wo = lax.all_gather(out_w.astype(bf16), "dp", axis=0, tiled=True)
        wgu = lax.all_gather(gu_w.astype(bf16), "dp", axis=1, tiled=True)
        wd = lax.all_gather(down_w.astype(bf16), "dp", axis=0, tiled=True)
        freq = 10000.0 ** (-jnp.arange(HD // 2, dtype=f32) / (HD // 2))
        freq = jnp.broadcast_to(freq[:, None], (HD // 2, 128))
        gain8 = jnp.pad(gain_full, ((0, 6), (0, 0)))
        qT, kT, vT, oT, lse, cos, sin, segc, segr = attn_fwd(seg_lens, x, gain8, freq, wqkv)
        output, dmid, dob, dobT, dwo, dwgu, dwd = mlp(x, oT.T, oT, cot, wo, wgu, wd, gain8)
        input_grad, dwqkv = attn_bwd(x, gain8, wqkv, dmid, qT, kT, vT, dob, dobT, lse, cos, sin, segc, segr)

        def owned(grad, axis):
            part = lax.psum_scatter(grad, "dp", scatter_dimension=axis, tiled=True)
            return lax.psum(part.astype(f32), "rep")

        g_down = owned(dwd, 0)
        g_gu = owned(dwgu, 1)
        g_out = owned(dwo, 0)
        g_qkv = owned(dwqkv, 1)
    gain_f = gain_low.astype(f32)
    g_gain = jnp.stack([
        jnp.sum(g_qkv * qkv_w.astype(bf16).astype(f32), axis=(0, 2)) / gain_f[0],
        jnp.sum(g_gu * gu_w.astype(bf16).astype(f32), axis=(0, 2)) / gain_f[1],
    ])
    qkv_res = adam_step(qkv_w, g_qkv, qkv_m, qkv_v, matrix_rate, weight_decay)
    out_res = adam_step(out_w, g_out, out_m, out_v, matrix_rate, weight_decay)
    gu_res = adam_step(gu_w, g_gu, gu_m, gu_v, matrix_rate, weight_decay)
    down_res = adam_step(down_w, g_down, down_m, down_v, matrix_rate, weight_decay)
    gain_res = adam_step(gains, g_gain, gain_m, gain_v, gain_rate, 0.0)
    return (output.reshape(tokens.shape), input_grad.reshape(tokens.shape)) + qkv_res + out_res + gu_res + down_res + gain_res


def solution(mesh):
    rows, cols, vec = P(("dp", "rep"), None, None), P(None, "dp", None), P("dp", None)
    small = P(None, "dp")
    return jax.shard_map(
        per_device,
        mesh=mesh,
        in_specs=(rows, P(("dp", "rep"), None), rows, cols, vec, cols, vec, small,
                  cols, cols, vec, vec, cols, cols, vec, vec, small, small),
        out_specs=(rows, rows) + (cols,) * 3 + (vec,) * 3 + (cols,) * 3 + (vec,) * 3 + (small,) * 3,
        check_vma=False,
    )
```

```python
import functools
import math

import jax
import jax.numpy as jnp
from jax import lax
from jax.experimental import pallas as pl
from jax.experimental.pallas import tpu as pltpu
from jax.sharding import PartitionSpec as P

bf16, f32 = jnp.bfloat16, jnp.float32
STEP = 10
beta_one, beta_two, adam_eps = 0.9, 0.95, 1e-08
weight_decay, matrix_rate, gain_rate = 0.05, 0.1, 0.3
EPS = 1e-5
def nn(a,b): return lax.dot_general(a,b,(((1,),(0,)),((),())),preferred_element_type=f32)
def nt(a,b): return lax.dot_general(a,b,(((1,),(1,)),((),())),preferred_element_type=f32)
def tn(a,b): return lax.dot_general(a,b,(((0,),(0,)),((),())),preferred_element_type=f32)

def mlp_kernel(T, x_ref, ob_ref, obT_ref, cot_ref, wo_ref, wgu_ref, wd_ref, gain_ref,
               out_ref, dmid_ref, dob_ref, dobT_ref, dwo_ref, dwgu_ref, dwd_ref,
               h2_s, h2T_s, dfb_s, dh2_s, r_s, hid_s, dg_s, du_s):
    f = pl.program_id(0); nf = pl.num_programs(0)
    S = x_ref.shape[0]; nt_ = S // T
    gain = gain_ref[1:2, :]
    @pl.when(f == 0)
    def _():
        @pl.loop(0, nt_)
        def _(i):
            t = pl.ds(pl.multiple_of(i*T, T), T)
            mid = x_ref[t, :].astype(f32) + nn(ob_ref[t, :], wo_ref[...])
            out_ref[t, :] = mid
            dmid_ref[t, :] = mid
            r = lax.rsqrt(jnp.mean(mid*mid, axis=-1, keepdims=True) + EPS)
            r_s[t, :] = jnp.broadcast_to(r, (T, 128))
            h2 = ((mid*r)*gain).astype(bf16)
            h2_s[t, :] = h2
            h2T_s[:, t] = h2.T
            dfb_s[t, :] = cot_ref[t, :].astype(bf16)
            dh2_s[t, :] = jnp.zeros_like(mid)
    @pl.loop(0, nt_)
    def _(i):
        t = pl.ds(pl.multiple_of(i*T, T), T)
        h2 = h2_s[t, :]; dfb = dfb_s[t, :]
        g = nn(h2, wgu_ref[0]); u = nn(h2, wgu_ref[1])
        dh = nt(dfb, wd_ref[...])
        sig = 0.5*jnp.tanh(0.5*g)+0.5
        silu = g*sig
        hid = (silu*u).astype(bf16)
        dg = (dh*u*(sig*(1.0+g*(1.0-sig)))).astype(bf16)
        du = (dh*silu).astype(bf16)
        hid_s[t, :] = hid; dg_s[t, :] = dg; du_s[t, :] = du
        out_ref[t, :] += nn(hid, wd_ref[...])
        dh2_s[t, :] += nt(dg, wgu_ref[0]) + nt(du, wgu_ref[1])
    dwd_ref[...] = tn(hid_s[...], dfb_s[...]).astype(bf16)
    dwgu_ref[0] = nn(h2T_s[...], dg_s[...]).astype(bf16)
    dwgu_ref[1] = nn(h2T_s[...], du_s[...]).astype(bf16)
    @pl.when(f == nf-1)
    def _():
        @pl.loop(0, nt_)
        def _(i):
            t = pl.ds(pl.multiple_of(i*T, T), T)
            mid = dmid_ref[t, :]; r = r_s[t, 0:1]
            xh = mid*r; dh = dh2_s[t, :]; w = dh*gain
            back = r*(w - xh*jnp.mean(w*xh, axis=-1, keepdims=True))
            dmid = cot_ref[t, :] + back
            dmid_ref[t, :] = dmid
            dab = dmid.astype(bf16)
            h2_s[t, :] = dab
            dob_ref[t, :] = nt(dab, wo_ref[...]).astype(bf16)
            dobT_ref[:, t] = nt(wo_ref[...], dab).astype(bf16)
        dwo_ref[...] = nn(obT_ref[...], h2_s[...]).astype(bf16)

def mlp(x, ob, obT, cot, wo, wgu, wd, gains, FC=512, T=256):
    S, D = x.shape; FF = wd.shape[0]
    full = lambda *s: pl.BlockSpec(s, lambda f: (0,)*len(s), pipeline_mode=pl.Buffered(1))
    return pl.pallas_call(
        functools.partial(mlp_kernel, T), grid=(FF//FC,),
        in_specs=[full(S,D), full(S,D), full(D,S), full(S,D), full(D,D),
                  pl.BlockSpec((2,D,FC), lambda f:(0,0,f)), pl.BlockSpec((FC,D), lambda f:(f,0)), full(8,D)],
        out_specs=[full(S,D), full(S,D), full(S,D), full(D,S), full(D,D),
                  pl.BlockSpec((2,D,FC), lambda f:(0,0,f)), pl.BlockSpec((FC,D), lambda f:(f,0))],
        out_shape=[jax.ShapeDtypeStruct((S,D),f32), jax.ShapeDtypeStruct((S,D),f32), jax.ShapeDtypeStruct((S,D),bf16),
                   jax.ShapeDtypeStruct((D,S),bf16), jax.ShapeDtypeStruct((D,D),bf16),
                   jax.ShapeDtypeStruct((2,D,FF),bf16), jax.ShapeDtypeStruct((FF,D),bf16)],
        scratch_shapes=[pltpu.VMEM((S,D),bf16), pltpu.VMEM((D,S),bf16), pltpu.VMEM((S,D),bf16), pltpu.VMEM((S,D),f32),
                        pltpu.VMEM((S,128),f32), pltpu.VMEM((S,FC),bf16), pltpu.VMEM((S,FC),bf16), pltpu.VMEM((S,FC),bf16)],
        compiler_params=pltpu.CompilerParams(vmem_limit_bytes=62*2**20),
        name="mlp",
    )(x, ob, obT, cot, wo, wgu, wd, gains)

H, HD = 12, 64
NEG = -1e30
VM = pl.BlockSpec(memory_space=pltpu.VMEM)
def tnt(a,b): return lax.dot_general(a,b,(((0,),(1,)),((),())),preferred_element_type=f32)

def seg_rows(lens_ref, S):
    slot = lax.broadcasted_iota(jnp.int32, (8, S), 1)
    seg = jnp.zeros((8, S), jnp.int32); start = jnp.zeros((8, S), jnp.int32)
    end = jnp.int32(0)
    for s in range(lens_ref.shape[1]-1):
        end = end + lens_ref[0, s]
        past = (slot >= end).astype(jnp.int32)
        seg += past
        start += past * lens_ref[0, s]
    return seg, slot - start


MESH = pl.DeviceIdType.MESH

def flip(v, b):
    return v + b - 2*b*lax.rem(lax.div(v, b), 2)

def cut(rows):
    return rows // 3 // 16 * 16

class Place:
    def __init__(self):
        d, z = lax.axis_index("dp"), lax.axis_index("rep")
        self.d, self.z = d, z
        self.y, self.x, self.c = lax.div(d, 4), lax.rem(lax.div(d, 2), 2), lax.rem(d, 2)
        self.S, self.X, self.Y = (flip(d, 1), z), (flip(d, 2), z), (flip(d, 4), z)
        self.Z, self.I = (d, flip(z, 1)), (d, 3 - z)
        self.inner = (z == 1) | (z == 2)

def settle(sem, view):
    pltpu.make_async_copy(view, view, sem).wait()

class Gather:
    def __init__(self, at, here, ref, send, recv, lead=None, cols=slice(None)):
        self.at, self.ref, self.send, self.recv, self.lead, self.cols = at, ref, send, recv, lead, cols
        r = ref.shape[-2]; a = cut(r)
        p = lax.rem(at.z, 2)
        self.parts = {"all": (0, r), "zb": (p*a, r - a), "z": (p*(r - a), a), "b": (a, r - 2*a)}
        self.r, self.a = r, a
        at_ = at
        self.own, self.xs, self.ys, self.xys = (at_.y, at_.x, at_.c), (at_.y, 1 - at_.x, at_.c), (1 - at_.y, at_.x, at_.c), (1 - at_.y, 1 - at_.x, at_.c)
    def view(self, who, part="all"):
        off, m = self.parts[part]
        rows = slice(None) if part == "all" else pl.ds(off if isinstance(off, int) else pl.multiple_of(off, 16), m)
        return self.ref.at[(() if self.lead is None else (self.lead,)) + tuple(who) + (rows, self.cols)]
    def put(self, who, part, dev, out, sem):
        v = self.view(who, part)
        pltpu.make_async_remote_copy(src_ref=v, dst_ref=v, send_sem=self.send.at[out], recv_sem=self.recv.at[sem], device_id=dev, device_id_type=MESH).start()
    def some(self, *idx):
        return self.ref.at[(() if self.lead is None else (self.lead,)) + idx + (self.cols,)]
    def begin(self):
        self.put(self.own, "zb", self.at.X, 1, 0); self.put(self.own, "zb", self.at.Y, 1, 0); self.put(self.own, "all", self.at.S, 0, 3)
    def first(self):
        settle(self.recv.at[0], self.some(0, 0, slice(None), slice(0, self.r - self.a)))
        self.put(self.xs, "z", self.at.Y, 2, 1); self.put(self.ys, "b", self.at.X, 2, 1)
        self.put(self.xs, "z", self.at.Z, 1, 4); self.put(self.ys, "z", self.at.Z, 1, 4)
    def second(self):
        settle(self.recv.at[1], self.some(0, 0, 0, slice(0, self.r - self.a)))
        self.put(self.xys, "z", self.at.Z, 2, 2)
        settle(self.recv.at[4], self.some(0, 0, slice(None), slice(0, self.a)))
        self.put(self.xs, "all", self.at.S, 0, 3); self.put(self.ys, "all", self.at.S, 0, 3)
    def third(self):
        settle(self.recv.at[2], self.some(0, 0, 0, slice(0, self.a)))
        self.put(self.xys, "all", self.at.S, 0, 3)
    def sibling(self):
        settle(self.recv.at[3], self.some(0, slice(None), slice(None), slice(None)))
    def sent(self):
        settle(self.send.at[0], self.some(0, slice(None), slice(None), slice(None)))
        settle(self.send.at[1], self.some(0, 0, slice(None), slice(None)))
        settle(self.send.at[2], self.some(0, 0, 0, slice(None)))

class Sum:
    def __init__(self, at, ref, lead, cols, rs, rx, r2, zr, out, send, recv, loc):
        self.at, self.ref, self.lead, self.cols, self.rs, self.rx, self.r2, self.zr, self.out = at, ref, lead, cols, rs, rx, r2, zr, out
        self.send, self.recv, self.loc = send, recv, loc
        self.r = ref.shape[-2]; self.h = self.r // 2
        self.halves = (slice(0, self.h), slice(self.h, self.r))
    def view(self, y, x, c, rows=slice(None)):
        return self.ref.at[(() if self.lead is None else (self.lead,)) + (y, x, c, rows, self.cols)]
    def put(self, src, dst, dev, sem):
        pltpu.make_async_remote_copy(src_ref=src, dst_ref=dst, send_sem=self.send.at[min(sem, 3)], recv_sem=self.recv.at[sem], device_id=dev, device_id_type=MESH).start()
    def add(self, dst, *srcs):
        if len(dst.shape) == 2:
            v = srcs[0][...]
            for s in srcs[1:]: v = v + s[...]
            dst[...] = v
        else:
            for i in range(dst.shape[0]): self.add(dst.at[i], *(s.at[i] for s in srcs))
    def sub(self, ref, *idx):
        return ref.at[(() if self.lead is None else (slice(None),)) + idx]
    def a(self):
        al = slice(None)
        self.put(self.view(al, al, 1 - self.at.c), self.rs, self.at.S, 0)
    def b(self):
        A = self.at
        settle(self.recv.at[0], self.rs)
        def got(y, x):
            p = self.view(y, x, A.c)
            self.add(p, p, self.sub(self.rs, y, x))
        got(1 - A.y, 1 - A.x); got(A.y, 1 - A.x)
        self.put(self.view(slice(None), 1 - A.x, A.c, self.halves[0]), self.rx.at[0], A.X, 1)
        got(1 - A.y, A.x)
        self.put(self.view(1 - A.y, slice(None), A.c, self.halves[1]), self.rx.at[1], A.Y, 1)
        got(A.y, A.x)
    def c(self):
        A = self.at
        settle(self.recv.at[1], self.rx)
        p = self.view(1 - A.y, A.x, A.c, self.halves[0])
        self.add(p, p, self.sub(self.rx.at[0], 1 - A.y))
        self.put(p, self.r2.at[0], A.Y, 2)
        p = self.view(A.y, 1 - A.x, A.c, self.halves[1])
        self.add(p, p, self.sub(self.rx.at[1], 1 - A.x))
        self.put(p, self.r2.at[1], A.X, 2)
        for h, w in ((0, A.y), (1, A.x)):
            p = self.view(A.y, A.x, A.c, self.halves[h])
            self.add(p, p, self.sub(self.rx.at[h], w))
    def piece(self): return self.view(self.at.y, self.at.x, self.at.c)
    def fin(self, inner): return pltpu.make_async_copy(self.piece() if inner else self.zr.at[0], self.out, self.loc)
    def e(self):
        A = self.at
        settle(self.recv.at[2], self.r2)
        for h in range(2):
            p = self.view(A.y, A.x, A.c, self.halves[h])
            self.add(p, p, self.r2.at[h])
        @pl.when(jnp.logical_not(A.inner))
        def _(): self.put(self.piece(), self.zr.at[0], A.Z, 3)
    def f(self):
        @pl.when(self.at.inner)
        def _():
            settle(self.recv.at[3], self.zr.at[0])
            self.add(self.zr.at[0], self.zr.at[0], self.piece())
            self.put(self.zr.at[0], self.zr.at[1], self.at.I, 4)
    def g(self):
        @pl.when(self.at.inner)
        def _():
            settle(self.recv.at[4], self.zr.at[1])
            self.add(self.piece(), self.zr.at[0], self.zr.at[1])
            self.put(self.piece(), self.zr.at[0], self.at.Z, 3)
            self.fin(True).start()
    def h_(self):
        @pl.when(jnp.logical_not(self.at.inner))
        def _():
            settle(self.recv.at[3], self.zr.at[0])
            self.fin(False).start()
    def drain(self):
        settle(self.send.at[0], self.rs); settle(self.send.at[1], self.rx); settle(self.send.at[2], self.r2)
        @pl.when(self.at.inner)
        def _(): settle(self.send.at[3], self.zr)
        @pl.when(jnp.logical_not(self.at.inner))
        def _(): settle(self.send.at[3], self.zr.at[0])
        self.fin(True).wait()

ANY = pl.BlockSpec(memory_space=pl.ANY)
SM = pl.BlockSpec(memory_space=pltpu.SMEM)
B = 256

def spread_gain(pieces, D):
    n, wide = pieces.shape[0], D // pieces.shape[0]
    lane = lax.broadcasted_iota(jnp.int32, (8, 128), 1)
    total = jnp.zeros((8, D), f32)
    for i in range(n):
        row = jnp.concatenate([jnp.where(lane < wide, pieces[i], 0.0), jnp.zeros((8, D - 128), f32)], axis=1)
        total += row if i == 0 else pltpu.roll(row, i*wide, 1)
    return total

def forward_attention(lens_ref, x_ref, freq_ref, gain_of, weights_in, w_ref, qT_s, kT_s, vT_s, oT_s, lse_s, cos_s, sin_s, segc_s, segr_s, bias_s, hook):
    S, D = x_ref.shape
    n = S // B
    seg, place = seg_rows(lens_ref, S)
    ang = jnp.broadcast_to(place[0:1, :].astype(f32), (HD//2, S)) * freq_ref[:, 0:1]
    cos_s[...] = jnp.cos(ang); sin_s[...] = jnp.sin(ang)
    segf = jnp.broadcast_to(seg[0:1, :].astype(f32), (128, S))
    segr_s[...] = segf[0:8]
    segc_s[...] = segf.T
    weights_in()
    gain = gain_of()
    @pl.loop(0, n)
    def _(i):
        t = pl.ds(pl.multiple_of(i*B, B), B)
        xf = x_ref[t, :].astype(f32)
        r = lax.rsqrt(jnp.mean(xf*xf, axis=-1, keepdims=True) + EPS)
        h1 = ((xf*r)*gain).astype(bf16)
        c = cos_s[:, t]; s = sin_s[:, t]
        for w, dst, sc in ((0, qT_s, 0.125), (1, kT_s, 1.0)):
            y = tnt(w_ref[w], h1)
            for h in range(H):
                a = y[h*HD:h*HD+32]; b = y[h*HD+32:h*HD+64]
                dst[h*HD:h*HD+32, t] = ((a*c - b*s)*sc).astype(bf16)
                dst[h*HD+32:h*HD+64, t] = ((b*c + a*s)*sc).astype(bf16)
        vT_s[:, t] = tnt(w_ref[2], h1).astype(bf16)
    hook("proj")
    for i in range(n):
        k0 = max(0, i-2)*B; nk = i*B + B - k0
        q0 = i*B
        kid = lax.broadcasted_iota(jnp.int32, (nk, B), 0) + k0
        qid = lax.broadcasted_iota(jnp.int32, (nk, B), 1) + q0
        ok = (segc_s[k0:k0+nk, 0:1] == segr_s[0:1, q0:q0+B]) & (kid <= qid)
        bias_s[0:nk, :] = jnp.where(ok, 0.0, NEG)
        @pl.loop(0, H//2)
        def _(p):
            for e in range(2):
                rows = pl.ds(pl.multiple_of(p*128 + e*64, 64), 64)
                s = tn(kT_s[rows, k0:k0+nk], qT_s[rows, q0:q0+B]) + bias_s[0:nk, :]
                m = jnp.max(s, axis=0, keepdims=True)
                ex = jnp.exp(s - m)
                l = jnp.sum(ex, axis=0, keepdims=True)
                o = nn(vT_s[rows, k0:k0+nk], ex.astype(bf16)) * (1.0/l)
                oT_s[rows, q0:q0+B] = o.astype(bf16)
                lse_s[pl.ds(p*2+e, 1), q0:q0+B] = m + jnp.log(l)
        hook(i)

def local_body(lens_ref, x_ref, freq_ref, gain_ref, w_ref, qT_ref, kT_ref, vT_ref, oT_ref, lse_ref, cos_ref, sin_ref, segc_ref, segr_ref, bias_s):
    forward_attention(lens_ref, x_ref, freq_ref, lambda: gain_ref[0:1, :], lambda: None, w_ref, qT_ref, kT_ref, vT_ref, oT_ref,
                      lse_ref, cos_ref, sin_ref, segc_ref, segr_ref, bias_s, lambda at: None)

def attn_fwd(lens, x, gains, freq, wqkv):
    S, D = x.shape
    sh = lambda s, d: jax.ShapeDtypeStruct(s, d)
    return pl.pallas_call(local_body,
        in_specs=[SM]+[VM]*4, out_specs=[VM]*9,
        out_shape=[sh((D,S),bf16)]*4 + [sh((16,S),f32), sh((32,S),f32), sh((32,S),f32), sh((S,128),f32), sh((8,S),f32)],
        scratch_shapes=[pltpu.VMEM((768,256),f32)],
        compiler_params=pltpu.CompilerParams(vmem_limit_bytes=62*2**20), name="attend")(lens, x, freq, gains, wqkv)

GW = 256

def backward_attention(x_ref, gain_ref, w_ref, ig_s, ig_ready, ig_done, qT_ref, kT_ref, vT_ref, dob_ref, dobT_ref, lse_ref, cos_ref, sin_ref, segc_ref, segr_ref,
                       dw_s, bias_s, q_s, dqT_s, dk_s, dv_s, g_s, h1T_s, hook):
    S, D = x_ref.shape
    n = S // B
    gain = gain_ref[0:1, :]
    hook("start")
    blocks = []
    at = 0
    for i in range(n):
        k0 = max(0, i-2)*B; nk = i*B + B - k0
        q0 = i*B
        kid = lax.broadcasted_iota(jnp.int32, (nk, B), 0) + k0
        qid = lax.broadcasted_iota(jnp.int32, (nk, B), 1) + q0
        ok = (segc_ref[k0:k0+nk, 0:1] == segr_ref[0:1, q0:q0+B]) & (kid <= qid)
        bias_s[at:at+nk, :] = jnp.where(ok, 0.0, NEG)
        blocks.append((q0, k0, nk, at)); at += nk
    q_s[...] = qT_ref[...].T
    @pl.loop(0, n)
    def _(i):
        t = pl.ds(pl.multiple_of(i*B, B), B)
        xf = x_ref[t, :].astype(f32)
        r = lax.rsqrt(jnp.mean(xf*xf, axis=-1, keepdims=True) + EPS)
        h1T_s[:, t] = ((xf*r)*gain).astype(bf16).T
    hook("ready")
    lane = lax.broadcasted_iota(jnp.int32, (B, 128), 1)
    @pl.loop(0, H//2)
    def _(p):
        cols = pl.ds(pl.multiple_of(p*128, 128), 128)
        dk_s[...] = jnp.zeros_like(dk_s); dv_s[...] = jnp.zeros_like(dv_s)
        for q0, k0, nk, at in blocks:
            dv = dk = None
            for e in range(2):
                rows = pl.ds(pl.multiple_of(p*128 + e*64, 64), 64)
                mine = (lane < 64) if e == 0 else (lane >= 64)
                dobz = jnp.where(mine, dob_ref[q0:q0+B, cols], 0).astype(bf16)
                qz = jnp.where(mine, q_s[q0:q0+B, cols], 0).astype(bf16)
                s = tn(kT_ref[rows, k0:k0+nk], qT_ref[rows, q0:q0+B]) + bias_s[at:at+nk, :]
                pr = jnp.exp(s - lse_ref[pl.ds(p*2+e, 1), q0:q0+B])
                dp = tn(vT_ref[rows, k0:k0+nk], dobT_ref[rows, q0:q0+B])
                inner = jnp.sum(pr*dp, axis=0, keepdims=True)
                ds = (pr*(dp - inner)).astype(bf16)
                dve = nn(pr.astype(bf16), dobz)
                dke = nn(ds, qz)
                dqT_s[e*64:e*64+64, q0:q0+B] = nn(kT_ref[rows, k0:k0+nk], ds) * 0.125
                dv = dve if dv is None else dv + dve
                dk = dke if dk is None else dk + dke
            dv_s[k0:k0+nk, :] += dv
            dk_s[k0:k0+nk, :] += dk
        c = cos_ref[...]; s = sin_ref[...]
        for j, src in ((0, dqT_s[...]), (1, dk_s[...].T)):
            parts = []
            for e in range(2):
                a = src[e*HD:e*HD+32]; b = src[e*HD+32:e*HD+64]
                parts += [a*c + b*s, b*c - a*s]
            g_s[j, :, cols] = jnp.concatenate(parts, axis=0).astype(bf16).T
        g_s[2, :, cols] = dv_s[...].astype(bf16)
        @pl.when(lax.rem(p, 2) == 1)
        def _():
            g = lax.div(p, 2)
            wide = pl.ds(pl.multiple_of(g*GW, GW), GW)
            for j in range(3):
                dw_s[g, j] = nn(h1T_s[...], g_s[j, :, wide]).astype(bf16)
        for k in range(H//2):
            @pl.when(p == k)
            def _():
                hook(k)
    ig_ready()
    for i in range(n):
        t = pl.ds(i*B, B)
        xf = x_ref[t, :].astype(f32)
        r = lax.rsqrt(jnp.mean(xf*xf, axis=-1, keepdims=True) + EPS)
        xh = xf*r
        dh = nt(g_s[0, t, :], w_ref[0]) + nt(g_s[1, t, :], w_ref[1]) + nt(g_s[2, t, :], w_ref[2])
        w = dh*gain
        ig_s[t, :] += r*(w - xh*jnp.mean(w*xh, axis=-1, keepdims=True))
        ig_done(i, t)
        hook("tile%d" % i)

def scratch_bwd(S, D):
    n = S // B
    area = sum(min(i+1, 3) for i in range(n))*B
    return [pltpu.VMEM((D//GW, 3, D, GW), bf16), pltpu.VMEM((area, B), f32), pltpu.VMEM((S, D), bf16), pltpu.VMEM((128, S), f32),
            pltpu.VMEM((S, 128), f32), pltpu.VMEM((S, 128), f32), pltpu.VMEM((3, S, D), bf16), pltpu.VMEM((D, S), bf16)]

def bwd_local_body(x_ref, gain_ref, w_ref, dmid_ref, qT_ref, kT_ref, vT_ref, dob_ref, dobT_ref, lse_ref, cos_ref, sin_ref, segc_ref, segr_ref,
                   ig_ref, dw_ref, bias_s, q_s, dqT_s, dk_s, dv_s, g_s, h1T_s):
    ig_ref[...] = dmid_ref[...]
    backward_attention(x_ref, gain_ref, w_ref, ig_ref, lambda: None, lambda i, t: None, qT_ref, kT_ref, vT_ref, dob_ref, dobT_ref, lse_ref, cos_ref, sin_ref,
                       segc_ref, segr_ref, dw_ref, bias_s, q_s, dqT_s, dk_s, dv_s, g_s, h1T_s, lambda at: None)

def attn_bwd(x, gains, wqkv, dmid, qT, kT, vT, dob, dobT, lse, cos, sin, segc, segr):
    S, D = x.shape
    sh = lambda s, d: jax.ShapeDtypeStruct(s, d)
    ig, dw = pl.pallas_call(bwd_local_body,
        in_specs=[VM]*14, out_specs=[VM]*2,
        out_shape=[sh((S,D),f32), sh((D//GW,3,D,GW),bf16)],
        scratch_shapes=scratch_bwd(S, D)[1:],
        compiler_params=pltpu.CompilerParams(vmem_limit_bytes=62*2**20), name="attend_back")(x, gains, wqkv, dmid, qT, kT, vT, dob, dobT, lse, cos, sin, segc, segr)
    return ig, jnp.moveaxis(dw, 0, 2).reshape(3, D, D)


FC, MT = 512, 512

def staggered(items, first, middle, last, at=None, between=None):
    a = first(items[0]); prev = None
    for i, it in enumerate(items):
        nxt = first(items[i+1]) if i + 1 < len(items) else None
        m = middle(it, a)
        if prev is not None: last(items[i-1], prev)
        if i == at: between()
        prev, a = m, nxt
    last(items[-1], prev)

def layer_body(n_dp, lens_ref, gain_ref, x_hbm, cot_hbm, qw_hbm, ow_hbm, gw_hbm, dw_hbm,
               out_o, ig_o, gq_o, gou_o, ggu_o, gdn_o,
               wq_s, wo_s, wgu_s, wd_s, qT_s, kT_s, vT_s, oT_s, cos_s, sin_s, segc_s, segr_s, lse_s, dlt_s, gain_s, gp_s,
               out_s, dh2_s, mid_s, acc_s, h2T_s, dfb_s, ch_s, dw_s,
               g_rs, g_rx, g_r2, g_z, n_rs, n_rx, n_r2, n_z, o_rs, o_rx, o_r2, o_z, q_rx, q_r2, q_z,
               ag_send, ag_recv, gn_send, gn_recv, rs_send, rs_recv, rs_loc, loc):
    S, D = x_hbm.shape
    x_s, h1T_s, h1T_late = dfb_s, h2T_s, oT_s
    nf = wd_s.shape[0]
    FF = nf*FC
    n, ng = S//B, len(HEADS_IN)
    rq, rd = D//n_dp, FF//n_dp
    sub = rd//nf
    each = [(y, x, c) for y in range(2) for x in range(2) for c in range(2)]
    def whole(v): return v.reshape(-1, v.shape[-1])
    at_ = Place()
    d, z = at_.d, at_.z
    mine = (at_.y, at_.x, at_.c)
    others = [lax.rem(d + j, n_dp) for j in range(1, n_dp)]
    gp_s[...] = jnp.zeros_like(gp_s)
    bar = pltpu.get_barrier_semaphore()
    met = [(o, z) for o in others] + [at_.Z, at_.I]
    for dev in met: pl.semaphore_signal(bar, inc=1, device_id=dev, device_id_type=MESH)

    loads = {}
    def load(key, src, dst):
        c = pltpu.make_async_copy(src, dst, loc.at[len(loads)]); c.start(); loads[key] = c
    for c in range(3): load("q%d" % c, qw_hbm.at[c], out_s.at[c*rq:(c+1)*rq, :])
    load("x", x_hbm, x_s)
    load("o", ow_hbm, out_s.at[3*rq:4*rq, :])
    load("d", dw_hbm, out_s.at[4*rq:4*rq+rd, :])
    wides = [(a, min(D, FF - a)) for a in range(0, FF, D)]
    for c in range(2):
        for k, (a, w) in enumerate(wides):
            load("g%d%d" % (c, k), gw_hbm.at[c, :, a:a+w], dh2_s.at[(c*len(wides)+k)*rq:(c*len(wides)+k+1)*rq, 0:w])
    cot_base = len(loads)
    base = cot_base + 4
    HB = B//2
    def cot_copies(i): return [pltpu.make_async_copy(cot_hbm.at[(i % n)*B + k*HB:(i % n)*B + (k+1)*HB, :], acc_s.at[i % 2 * 2 + k, :, 0:D],
                                                     loc.at[cot_base + i % 2 * 2 + k]) for k in range(2)]
    def cot_start(i):
        for c in cot_copies(i): c.start()
    def cot_get(i):
        for c in cot_copies(i): c.wait()
        return jnp.concatenate([acc_s[i % 2 * 2 + k, :, 0:D] for k in range(2)], axis=0)
    cot_start(0); cot_start(1)

    G = []
    def gather(*a): G.append(Gather(at_, mine, a[0], ag_send.at[len(G)], ag_recv.at[len(G)], *a[1:]))
    for c in range(3): gather(wq_s.at[c])
    gather(wo_s)
    of_gu, of_dn = [], []
    for f in range(nf):
        of_gu.append(len(G))
        gather(wgu_s, slice(None), slice(f*FC, (f+1)*FC))
        if f % 2 == 0:
            of_dn.append(len(G))
            gather(wd_s.at[f:f+2], slice(None))

    R = []
    def unit(ref, lead, cols, bufs, out):
        u = len(R)
        R.append(Sum(at_, ref, lead, cols, *bufs, out, rs_send.at[u], rs_recv.at[u], rs_loc.at[u]))
    al = slice(None)
    for f in range(nf):
        cols = slice(f*FC, (f+1)*FC)
        unit(wgu_s, al, cols, [b.at[f] for b in (g_rs, g_rx, g_r2, g_z)], ggu_o.at[:, :, cols])
    for h in range(nf//2):
        unit(wd_s.at[2*h:2*h+2], al, al, [b.at[h] for b in (n_rs, n_rx, n_r2, n_z)], gdn_o.at[2*h:2*h+2])
    unit(wo_s, None, al, (o_rs, o_rx, o_r2, o_z), gou_o)
    groups, c0 = [], 0
    for g, many in enumerate(HEADS_IN):
        cols = slice(c0, c0 + many*HD)
        groups.append(cols)
        up, left = c0//FC, c0 % FC
        rs = ch_s.at[:, :, :, up*rq:(up+1)*rq, left:left + many*HD]
        unit(dw_s, al, cols, [rs] + [b.at[..., cols] for b in (q_rx, q_r2, q_z)], gq_o.at[:, :, cols])
        c0 += many*HD
    done = [sum(HEADS_IN[:g+1])//2 - 1 for g in range(ng)]
    def hook(at):
        for what in PLAN.get(at, ()):
            k = int(what[1:])
            if what[0] == "B": G[k].begin()
            elif what[0] in "1234": getattr(G[k], ("first", "second", "third", "sibling")[int(what[0])-1])()
            elif what[0] == "h": R[k].h_()
            else: getattr(R[k], what[0])()

    gp_s[pl.ds(d, 1), 0:2, 0:gain_ref.shape[1]] = gain_ref[...].astype(bf16).astype(f32)[None]
    for c in range(3):
        loads["q%d" % c].wait()
        wq_s[(c,) + mine] = out_s[c*rq:(c+1)*rq, :].astype(bf16)
        if c == 0:
            pl.semaphore_wait(bar, len(met))
            gains = [pltpu.make_async_remote_copy(src_ref=gp_s.at[d], dst_ref=gp_s.at[d], send_sem=gn_send.at[j], recv_sem=gn_recv.at[j],
                                                  device_id=(o, z), device_id_type=MESH) for j, o in enumerate(others)]
        hook("begin%d" % c)
        if c == 0:
            for k in gains: k.start()
    loads["o"].wait()
    wo_s[mine] = out_s[3*rq:4*rq, :].astype(bf16)
    hook("s0")
    for k in loads:
        if k[0] == "g": loads[k].wait()
    for c in range(2):
        def at(col):
            k = col//D
            return dh2_s[(c*len(wides)+k)*rq:(c*len(wides)+k+1)*rq, col - k*D:col - k*D + sub]
        for f in range(nf):
            for o in range(0, n_dp, 2):
                two = jnp.concatenate([at(o*rd + f*sub), at((o+1)*rd + f*sub)], axis=1)
                wgu_s[(c,) + mine + (slice(None), slice(f*FC + o*sub, f*FC + (o+2)*sub))] = two.astype(bf16)
    loads["d"].wait()
    for f in range(nf): wd_s[(f,) + mine] = out_s[4*rq + f*sub:4*rq + (f+1)*sub, :].astype(bf16)
    hook("s1")

    seg, place = seg_rows(lens_ref, S)
    half = lax.broadcasted_iota(jnp.int32, (HD//2, 128), 0).astype(f32)
    freq = jnp.exp(half*(-math.log(10000.0)/(HD//2)))
    ang = jnp.broadcast_to(place[0:1, :].astype(f32), (HD//2, S)) * freq[:, 0:1]
    cos_s[...] = jnp.cos(ang); sin_s[...] = jnp.sin(ang)
    segf = jnp.broadcast_to(seg[0:1, :].astype(f32), (128, S))
    segr_s[...] = segf[0:8]
    segc_s[...] = segf.astype(bf16).T
    hook("s2")
    blocks = []
    at = {0: (0, 0), 1: (B, 0), 2: (0, B), 3: (0, 2*B)}
    for i in range(n):
        k0 = max(0, i-2)*B
        blocks.append((i*B, k0, i*B + B - k0) + at[i])
    def masks():
        for q0, k0, nk, r0, c0 in blocks:
            kid = lax.broadcasted_iota(jnp.int32, (nk, B), 0) + k0
            qid = lax.broadcasted_iota(jnp.int32, (nk, B), 1) + q0
            ok = (segc_s[k0:k0+nk, 0:1].astype(f32) == segr_s[0:1, q0:q0+B]) & (kid <= qid)
            dh2_s[r0:r0+nk, c0:c0+B] = jnp.where(ok, 0.0, NEG)
    masks()
    loads["x"].wait()
    hook("s3")
    for k in gains: k.wait_recv()
    gain_s[...] = spread_gain(gp_s[...], D)
    def normed(dst):
        @pl.loop(0, n)
        def _(i):
            t = pl.ds(pl.multiple_of(i*B, B), B)
            xf = x_s[t, :].astype(f32)
            r = lax.rsqrt(jnp.mean(xf*xf, axis=-1, keepdims=True) + EPS)
            dst[:, t] = ((xf*r)*gain_s[0:1, :]).astype(bf16).T
    normed(h1T_s)
    hook("start")
    for w, dst, sc in ((0, qT_s, 0.125), (1, kT_s, 1.0), (2, vT_s, None)):
        hook("proj%d" % w)
        for t0 in range(0, S, MT):
            t = slice(t0, t0+MT)
            y = tn(whole(wq_s[w]), h1T_s[:, t])
            if sc is None: dst[:, t] = y.astype(bf16)
            else:
                c = cos_s[:, t]; s = sin_s[:, t]
                for h in range(H):
                    a = y[h*HD:h*HD+32]; b = y[h*HD+32:h*HD+64]
                    dst[h*HD:h*HD+32, t] = ((a*c - b*s)*sc).astype(bf16)
                    dst[h*HD+32:h*HD+64, t] = ((b*c + a*s)*sc).astype(bf16)

    @pl.loop(0, H//2)
    def _(p):
        rs = [pl.ds(pl.multiple_of(p*128 + e*64, 64), 64) for e in range(2)]
        def scores(it):
            (q0, k0, nk, r0, c0), e = it
            return tn(kT_s[rs[e], k0:k0+nk], qT_s[rs[e], q0:q0+B]) + dh2_s[r0:r0+nk, c0:c0+B]
        def soft(it, s):
            m = jnp.max(s, axis=0, keepdims=True)
            ex = jnp.exp(s - m)
            return m, ex.astype(bf16), jnp.sum(ex, axis=0, keepdims=True)
        def mix(it, mel):
            (q0, k0, nk, r0, c0), e = it
            m, ex, l = mel
            oT_s[rs[e], q0:q0+B] = (nn(vT_s[rs[e], k0:k0+nk], ex) * (1.0/l)).astype(bf16)
            lse_s[pl.ds(p*2+e, 1), q0:q0+B] = m + jnp.log(l)
        staggered([(b, e) for b in blocks for e in range(2)], scores, soft, mix)
        for k in range(H//2):
            @pl.when(p == k)
            def _(): hook("a%d" % k)

    hook("mlp")
    gain2 = gain_s[1:2, :]
    for i in range(n):
        t = slice(i*B, (i+1)*B)
        mid = x_s[t, :].astype(f32) + tn(oT_s[:, t], whole(wo_s[...]))
        out_s[t, :] = mid; mid_s[t, :] = mid
        r = lax.rsqrt(jnp.mean(mid*mid, axis=-1, keepdims=True) + EPS)
        h2T_s[:, t] = ((mid*r)*gain2).astype(bf16).T
        dfb_s[t, :] = cot_get(i).astype(bf16)
        cot_start(i+2)
        dh2_s[t, :] = jnp.zeros_like(mid)
    def gu_of(k, cols): return whole(wgu_s[k, :, :, :, :, cols])
    @pl.loop(0, nf)
    def _(f):
        cols = pl.ds(pl.multiple_of(f*FC, FC), FC)
        def first(i):
            t = slice(i*MT, (i+1)*MT)
            return tn(h2T_s[:, t], gu_of(0, cols)), tn(h2T_s[:, t], gu_of(1, cols)), nt(dfb_s[t, :], whole(wd_s[f]))
        def middle(i, gud):
            g, u, dh = gud
            t = slice(i*MT, (i+1)*MT)
            sig = 0.5*jnp.tanh(0.5*g) + 0.5
            silu = g*sig
            hid = (silu*u).astype(bf16)
            dg = (dh*u*(sig + silu*(1.0 - sig))).astype(bf16)
            du = (dh*silu).astype(bf16)
            for j, v in enumerate((hid, dg, du)):
                for k in range(2): ch_s[j, i, k] = v[k*MT//2:(k+1)*MT//2]
            if i == 0:
                for k in range(nf):
                    @pl.when(f == k)
                    def _(): hook("f%dmid" % k)
            return hid, dg, du
        def last(i, hdd):
            hid, dg, du = hdd
            t = slice(i*MT, (i+1)*MT)
            out_s[t, :] += nn(hid, whole(wd_s[f]))
            dh2_s[t, :] += nt(dg, gu_of(0, cols)) + nt(du, gu_of(1, cols))
        staggered(list(range(S//MT)), first, middle, last)
        for k in range(nf):
            @pl.when(f == k)
            def _():
                for g in [of_gu[k]] + ([of_dn[k//2]] if k % 2 == 0 else []): G[g].sent()
        for k in range(2):
            v = nn(h2T_s[...], whole(ch_s[1+k])).astype(bf16)
            for o, w in enumerate(each): wgu_s[(k,) + w + (slice(None), cols)] = v[o*rq:(o+1)*rq]
        v = tn(whole(ch_s[0]), dfb_s[...]).astype(bf16)
        for o, w in enumerate(each): wd_s[(f,) + w] = v[o*sub:(o+1)*sub]
        for k in range(nf):
            @pl.when(f == k)
            def _(): hook("f%dend" % k)
    out_c = pltpu.make_async_copy(out_s, out_o, loc.at[base]); out_c.start()
    for i in range(n):
        t = slice(i*B, (i+1)*B)
        mid = mid_s[t, :]; dh = dh2_s[t, :]
        r = lax.rsqrt(jnp.mean(mid*mid, axis=-1, keepdims=True) + EPS)
        xh = mid*r; w = dh*gain2
        dmid = cot_get(i) + r*(w - xh*jnp.mean(w*xh, axis=-1, keepdims=True))
        if i + 2 < n: cot_start(i+2)
        mid_s[t, :] = dmid
        dab = dmid.astype(bf16)
        dfb_s[t, :] = dab
        h2T_s[:, t] = nt(whole(wo_s[...]), dab).astype(bf16)
        if i == 1: hook("e0")
    G[3].sent()
    v = nn(oT_s[...], dfb_s[...]).astype(bf16)
    for o, w in enumerate(each): wo_s[w] = v[o*rq:(o+1)*rq]
    x_again = pltpu.make_async_copy(x_hbm, x_s, loc.at[0]); x_again.start()
    for h in range(H):
        r = slice(h*HD, (h+1)*HD)
        dlt_s[h:h+1, :] = jnp.sum(h2T_s[r, :].astype(f32)*oT_s[r, :].astype(f32), axis=0, keepdims=True)
    masks()
    hook("e1")
    x_again.wait()
    normed(h1T_late)

    dq_s, dk_s, dv_s = (acc_s.at[j] for j in range(3))
    @pl.loop(0, H//2)
    def _(p):
        rs = [pl.ds(pl.multiple_of(p*128 + e*64, 64), 64) for e in range(2)]
        dk_s[...] = jnp.zeros_like(dk_s); dv_s[...] = jnp.zeros_like(dv_s)
        def first(it):
            (q0, k0, nk, r0, c0), e = it
            return (tn(kT_s[rs[e], k0:k0+nk], qT_s[rs[e], q0:q0+B]) + dh2_s[r0:r0+nk, c0:c0+B],
                    tn(vT_s[rs[e], k0:k0+nk], h2T_s[rs[e], q0:q0+B]))
        def middle(it, sd):
            (q0, k0, nk, r0, c0), e = it
            s, dp = sd
            pr = jnp.exp(s - lse_s[pl.ds(p*2+e, 1), q0:q0+B])
            return pr.astype(bf16), (pr*(dp - dlt_s[pl.ds(p*2+e, 1), q0:q0+B])).astype(bf16)
        def last(it, pd):
            (q0, k0, nk, r0, c0), e = it
            pr, ds = pd
            r = slice(e*HD, (e+1)*HD)
            dv_s[r, k0:k0+nk] += nt(h2T_s[rs[e], q0:q0+B], pr)
            dk_s[r, k0:k0+nk] += nt(qT_s[rs[e], q0:q0+B], ds)
            dq_s[r, q0:q0+B] = nn(kT_s[rs[e], k0:k0+nk], ds) * 0.125
        def half():
            for k in range(H//2):
                @pl.when(p == k)
                def _(): hook("c%da" % k)
        staggered([(b, e) for b in blocks for e in range(2)], first, middle, last, 5, half)
        c = cos_s[...]; s = sin_s[...]
        for src, dst in ((dq_s, qT_s), (dk_s, kT_s)):
            for e in range(2):
                a = src[e*HD:e*HD+32, :]; b = src[e*HD+32:(e+1)*HD, :]
                dst[pl.ds(pl.multiple_of(p*128 + e*64, 32), 32), :] = (a*c + b*s).astype(bf16)
                dst[pl.ds(pl.multiple_of(p*128 + e*64 + 32, 32), 32), :] = (b*c - a*s).astype(bf16)
        vT_s[pl.ds(pl.multiple_of(p*128, 128), 128), :] = dv_s[...].astype(bf16)
        for k in range(H//2):
            @pl.when(p == k)
            def _():
                if k in done:
                    cols = groups[done.index(k)]
                    for j, src in enumerate((qT_s, kT_s, vT_s)):
                        v = nt(h1T_late[...], src[cols, :]).astype(bf16)
                        for o, w in enumerate(each): dw_s[(j,) + w + (slice(None), cols)] = v[o*rq:(o+1)*rq]
                hook("c%d" % k)
    def ig_copy(i): return pltpu.make_async_copy(mid_s.at[i*B:(i+1)*B, :], ig_o.at[i*B:(i+1)*B, :], loc.at[base + 1 + i])
    gain1 = gain_s[0:1, :]
    for i in range(n):
        t = slice(i*B, (i+1)*B)
        xf = x_s[t, :].astype(f32)
        r = lax.rsqrt(jnp.mean(xf*xf, axis=-1, keepdims=True) + EPS)
        xh = xf*r
        dh = tnt(qT_s[:, t], whole(wq_s[0])) + tnt(kT_s[:, t], whole(wq_s[1])) + tnt(vT_s[:, t], whole(wq_s[2]))
        w = dh*gain1
        mid_s[t, :] += r*(w - xh*jnp.mean(w*xh, axis=-1, keepdims=True))
        ig_copy(i).start()
        hook("t%d" % i)
    hook("end")
    for g in range(3): G[g].sent()
    for k in gains: k.wait_send()
    for u in R: u.drain()
    out_c.wait()
    for i in range(n): ig_copy(i).wait()

HEADS_IN = (4, 4, 2, 2)
PLAN = {
    "begin0": ("B0",),
    "begin1": ("B1",),
    "begin2": ("B2",),
    "s2": ("10",),
    "s3": ("11", "B3"),
    "start": ("12", "B4", "20"),
    "proj0": ("21", "22", "13", "B5", "30", "31", "40"),
    "proj1": ("41", "32", "14", "B6"),
    "proj2": ("42", "23"),
    "a0": ("24", "15", "B7", "33"),
    "a1": ("43", "16", "B8"),
    "a2": ("34",),
    "a3": ("44", "25", "17", "B9"),
    "a4": ("26",),
    "a5": ("35", "18"),
    "mlp": ("45",),
    "f0mid": ("36", "27", "28", "19"),
    "f0end": ("a0", "46", "37", "38"),
    "f1mid": ("29", "b0", "47", "48"),
    "f1end": ("a1", "a4", "39"),
    "f2mid": ("c0", "b1"),
    "f2end": ("a2", "49", "e0", "b4"),
    "f3mid": ("c1", "b2"),
    "f3end": ("a3", "a5", "f0", "e1", "c4"),
    "e0": ("b3",),
    "e1": ("a6", "g0", "f1", "e4", "c2", "b5"),
    "c0a": ("c3", "b6"),
    "c0": ("h0", "g1", "f4", "e2"),
    "c1": ("a7", "c5"),
    "c2a": ("g4", "f2", "e3", "b7", "h1"),
    "c2": ("c6",),
    "c3a": ("e5",),
    "c3": ("a8", "g2", "f3"),
    "c4a": ("h4", "e6", "c7", "b8"),
    "c4": ("a9", "f5"),
    "c5a": ("g3", "f6", "e7", "b9", "h2"),
    "c5": ("a10", "c8"),
    "t0": ("g5", "f7", "c9", "b10"),
    "t1": ("e8",),
    "t2": ("h3", "g6", "e9"),
    "t3": ("f8", "c10", "g7"),
    "end": ("h5", "f9", "e10", "h6", "f10", "g8", "g9", "h7", "g10", "h8", "h9", "h10"),
}


def layer(n_dp, lens, gains, x, cot, qw, ow, gw, dw):
    S, D = x.shape
    FF = gw.shape[2]
    sh = lambda s, d: jax.ShapeDtypeStruct(s, d)
    b = lambda *s: pltpu.VMEM(s, bf16)
    w = lambda *s: pltpu.VMEM(s, f32)
    rq, rd, nf, ng = D//n_dp, FF//n_dp, FF//FC, len(HEADS_IN)
    ag, rs = 4 + nf + nf//2, nf + nf//2 + 1 + ng
    dma = pltpu.SemaphoreType.DMA
    c8 = (2, 2, 2)
    def bufs(lead, r, cols, many=()):
        return [b(*many, *lead, 2, 2, r, cols), b(*many, 2, *lead, 2, r//2, cols), b(*many, 2, *lead, r//2, cols), b(*many, 2, *lead, r, cols)]
    return pl.pallas_call(functools.partial(layer_body, n_dp),
        in_specs=[SM, VM] + [ANY]*6, out_specs=[ANY]*6,
        out_shape=[sh((S,D),f32), sh((S,D),f32), sh((3,rq,D),bf16), sh((rq,D),bf16), sh((2,rq,FF),bf16), sh((nf,rd//nf,D),bf16)],
        scratch_shapes=[b(3,*c8,rq,D), b(*c8,rq,D), b(2,*c8,rq,FF), b(nf,*c8,rd//nf,D), b(D,S), b(D,S), b(D,S), b(D,S),
                        w(HD//2,S), w(HD//2,S), b(S,128), w(8,S), w(16,S), w(16,S), w(8,D), w(n_dp,8,128),
                        w(S,D), w(S,D), w(S,D), w(4,128,S), b(D,S), b(S,D), b(3,2,S//MT,MT//2,FC), b(3,*c8,rq,D)]
            + bufs((2,), rq, FC, (nf,)) + bufs((2,), rd//nf, D, (nf//2,)) + bufs((), rq, D) + bufs((3,), rq, D)[1:]
            + [dma((ag,3)), dma((ag,5)), dma((n_dp-1,)), dma((n_dp-1,)), dma((rs,4)), dma((rs,5)), dma((rs,)), dma((24,))],
        compiler_params=pltpu.CompilerParams(collective_id=0, has_side_effects=True, vmem_limit_bytes=63*2**20),
        cost_estimate=pl.CostEstimate(flops=55*10**9, bytes_accessed=40*10**6, transcendentals=20*10**6),
        name="layer")(lens, gains, x, cot, qw, ow, gw, dw)

def can_fuse(n_dp, n_rep, S, D, FF, *rows):
    return n_dp == 8 and n_rep == 4 and S == 4*B and D % GW == 0 and FF == 4*FC and FC == n_dp*64 and sum(HEADS_IN) == H and all(r % 32 == 0 for r in rows)


def adam_body(sub, *refs):
    g_in, w_in, m_in, v_in, keep = refs[0:4], refs[4:9], refs[9:14], refs[14:19], refs[19:21]
    m_out, v_out, w_out, kept = refs[21:26], refs[26:31], refs[31:36], refs[36:38]
    bufs, acc_s, gg_s, load, store, pas, passed = refs[38:58], refs[58], refs[59], refs[60], refs[61], refs[62], refs[63:65]
    gs, ws, ms, vs = bufs[0:5], bufs[5:10], bufs[10:15], bufs[15:20]
    n_dp = w_in[2].shape[2]//(g_in[3].shape[0]*sub)
    nf = g_in[3].shape[0]
    todo = [(0, c) for c in range(3)] + [(1, None)] + [(2, c) for c in range(2)] + [(3, None), (4, None)]
    def at(ref, i): return ref if i is None else ref.at[i]
    loads = []
    for k, (a, i) in enumerate(todo):
        cs = []
        for j, (src, dst) in enumerate(((w_in, ws), (m_in, ms), (v_in, vs), (g_in, gs))):
            if j == 3 and a == 4: continue
            c = pltpu.make_async_copy(at(src[a], i), at(dst[a], i), load.at[k, j]); c.start(); cs.append(c)
        loads.append(cs)
    def halves(i, into):
        n = keep[i].shape[0]//2
        return [pltpu.make_async_copy(s.at[h*n:(h+1)*n], e.at[h*n:(h+1)*n], pas.at[into, i, h])
                for s, e in [((keep[i], passed[i]) if into == 0 else (passed[i], kept[i]))] for h in range(2)]
    for i in range(2):
        for c in halves(i, 0): c.start()
    stores = []
    for k, (a, i) in enumerate(todo):
        for c in loads[k]: c.wait()
        w = at(ws[a], i)[...]
        if a == 4:
            g = jnp.concatenate([acc_s[j].T[0:1, :] for j in range(2)], axis=0) / w.astype(bf16).astype(f32)
        elif a == 2:
            for o in range(n_dp):
                for f in range(0, nf, 2):
                    p = f*n_dp*sub + o*sub
                    q = p + n_dp*sub
                    gg_s[:, (o*nf + f)*sub:(o*nf + f + 2)*sub] = jnp.concatenate([gs[a][i, :, p:p+sub], gs[a][i, :, q:q+sub]], axis=1).astype(f32)
            g = gg_s[...]
        else:
            g = at(gs[a], i)[...].astype(f32).reshape(w.shape)
        if a in (0, 2):
            s = jnp.broadcast_to(jnp.sum(g*w.astype(bf16).astype(f32), axis=1, keepdims=True), (w.shape[0], 128))
            if i == 0: acc_s[a//2] = s
            else: acc_s[a//2] += s
        rate, decay = (gain_rate, 0.0) if a == 4 else (matrix_rate, weight_decay)
        new = adam_step(w, g, at(ms[a], i)[...], at(vs[a], i)[...], rate, decay)
        for j, (val, buf, out) in enumerate(zip(new, (ms, vs, ws), (m_out, v_out, w_out))):
            at(buf[a], i)[...] = val
            c = pltpu.make_async_copy(at(buf[a], i), at(out[a], i), store.at[k, j]); c.start(); stores.append(c)
        if k in (2, 4):
            i = (2, 4).index(k)
            for c, e in zip(halves(i, 0), halves(i, 1)):
                c.wait(); e.start()
    for c in stores + halves(0, 1) + halves(1, 1): c.wait()

def adam_all(grads, weights, moments, seconds, keep):
    q, o, g, d = grads
    rq = o.shape[0]
    sh = [jax.ShapeDtypeStruct(w.shape, f32) for w in weights]
    any_ = pl.BlockSpec(memory_space=pl.ANY)
    f = [pltpu.VMEM(w.shape, f32) for w in weights]
    dma = pltpu.SemaphoreType.DMA
    return pl.pallas_call(functools.partial(adam_body, d.shape[1]),
        in_specs=[any_]*21, out_specs=[any_]*17, out_shape=sh*3 + [jax.ShapeDtypeStruct(k.shape, k.dtype) for k in keep],
        scratch_shapes=[pltpu.VMEM(a.shape, bf16) for a in grads] + [pltpu.VMEM((8, 128), f32)] + f*3
            + [pltpu.VMEM((2, rq, 128), f32), pltpu.VMEM((rq, g.shape[2]), f32), dma((8, 4)), dma((8, 3)), dma((2, 2, 2))] + [pltpu.VMEM(k.shape, k.dtype) for k in keep],
        compiler_params=pltpu.CompilerParams(vmem_limit_bytes=63*2**20), name="adamw")(*grads, *weights, *moments, *seconds, *keep)

def adam_step(weight, grad_sum, moment, second, rate, decay):
    moment_new = beta_one * moment + (1.0 - beta_one) * grad_sum
    second_new = beta_two * second + (1.0 - beta_two) * grad_sum * grad_sum
    moment_hat = moment_new / (1.0 - beta_one**STEP)
    second_hat = second_new / (1.0 - beta_two**STEP)
    weight_new = weight - rate * (moment_hat / (jnp.sqrt(second_hat) + adam_eps) + decay * weight)
    return (moment_new, second_new, weight_new)


def per_device(tokens, seg_lens, cotangent, qkv_w, out_w, gu_w, down_w, gains,
               qkv_m, qkv_v, out_m, out_v, gu_m, gu_v, down_m, down_v, gain_m, gain_v):
    _, S, D = tokens.shape
    x = tokens.reshape(S, D)
    cot = cotangent.reshape(S, D)
    gain_low = gains.astype(bf16)
    n_dp, n_rep = lax.axis_size("dp"), lax.axis_size("rep")
    if can_fuse(n_dp, n_rep, S, D, gu_w.shape[2], qkv_w.shape[1], out_w.shape[0], gu_w.shape[1], down_w.shape[0]):
        output, input_grad, *grads = layer(n_dp, seg_lens, gains, x, cot, qkv_w, out_w, gu_w, down_w)
        new = adam_all(grads, (qkv_w, out_w, gu_w, down_w, gains), (qkv_m, out_m, gu_m, down_m, gain_m), (qkv_v, out_v, gu_v, down_v, gain_v),
                       (output, input_grad))
        states = tuple(new[5*k + a] for a in range(5) for k in range(3))
        return (new[15].reshape(tokens.shape), new[16].reshape(tokens.shape)) + states
    else:
        wqkv = lax.all_gather(qkv_w.astype(bf16), "dp", axis=1, tiled=True)
        gain_full = lax.all_gather(gain_low, "dp", axis=1, tiled=True).astype(f32)
        wo = lax.all_gather(out_w.astype(bf16), "dp", axis=0, tiled=True)
        wgu = lax.all_gather(gu_w.astype(bf16), "dp", axis=1, tiled=True)
        wd = lax.all_gather(down_w.astype(bf16), "dp", axis=0, tiled=True)
        freq = 10000.0 ** (-jnp.arange(HD // 2, dtype=f32) / (HD // 2))
        freq = jnp.broadcast_to(freq[:, None], (HD // 2, 128))
        gain8 = jnp.pad(gain_full, ((0, 6), (0, 0)))
        qT, kT, vT, oT, lse, cos, sin, segc, segr = attn_fwd(seg_lens, x, gain8, freq, wqkv)
        output, dmid, dob, dobT, dwo, dwgu, dwd = mlp(x, oT.T, oT, cot, wo, wgu, wd, gain8)
        input_grad, dwqkv = attn_bwd(x, gain8, wqkv, dmid, qT, kT, vT, dob, dobT, lse, cos, sin, segc, segr)

        def owned(grad, axis):
            part = lax.psum_scatter(grad, "dp", scatter_dimension=axis, tiled=True)
            return lax.psum(part.astype(f32), "rep")

        g_down = owned(dwd, 0)
        g_gu = owned(dwgu, 1)
        g_out = owned(dwo, 0)
        g_qkv = owned(dwqkv, 1)
    gain_f = gain_low.astype(f32)
    g_gain = jnp.stack([
        jnp.sum(g_qkv * qkv_w.astype(bf16).astype(f32), axis=(0, 2)) / gain_f[0],
        jnp.sum(g_gu * gu_w.astype(bf16).astype(f32), axis=(0, 2)) / gain_f[1],
    ])
    qkv_res = adam_step(qkv_w, g_qkv, qkv_m, qkv_v, matrix_rate, weight_decay)
    out_res = adam_step(out_w, g_out, out_m, out_v, matrix_rate, weight_decay)
    gu_res = adam_step(gu_w, g_gu, gu_m, gu_v, matrix_rate, weight_decay)
    down_res = adam_step(down_w, g_down, down_m, down_v, matrix_rate, weight_decay)
    gain_res = adam_step(gains, g_gain, gain_m, gain_v, gain_rate, 0.0)
    return (output.reshape(tokens.shape), input_grad.reshape(tokens.shape)) + qkv_res + out_res + gu_res + down_res + gain_res


def solution(mesh):
    rows, cols, vec = P(("dp", "rep"), None, None), P(None, "dp", None), P("dp", None)
    small = P(None, "dp")
    return jax.shard_map(
        per_device,
        mesh=mesh,
        in_specs=(rows, P(("dp", "rep"), None), rows, cols, vec, cols, vec, small,
                  cols, cols, vec, vec, cols, cols, vec, vec, small, small),
        out_specs=(rows, rows) + (cols,) * 3 + (vec,) * 3 + (cols,) * 3 + (vec,) * 3 + (small,) * 3,
        check_vma=False,
    )
```

```python
import functools
import math

import jax
import jax.numpy as jnp
from jax import lax
from jax.experimental import pallas as pl
from jax.experimental.pallas import tpu as pltpu
from jax.sharding import PartitionSpec as P

bf16, f32 = jnp.bfloat16, jnp.float32
STEP = 10
beta_one, beta_two, adam_eps = 0.9, 0.95, 1e-08
weight_decay, matrix_rate, gain_rate = 0.05, 0.1, 0.3
EPS = 1e-5
def nn(a,b): return lax.dot_general(a,b,(((1,),(0,)),((),())),preferred_element_type=f32)
def nt(a,b): return lax.dot_general(a,b,(((1,),(1,)),((),())),preferred_element_type=f32)
def tn(a,b): return lax.dot_general(a,b,(((0,),(0,)),((),())),preferred_element_type=f32)

def mlp_kernel(T, x_ref, ob_ref, obT_ref, cot_ref, wo_ref, wgu_ref, wd_ref, gain_ref,
               out_ref, dmid_ref, dob_ref, dobT_ref, dwo_ref, dwgu_ref, dwd_ref,
               h2_s, h2T_s, dfb_s, dh2_s, r_s, hid_s, dg_s, du_s):
    f = pl.program_id(0); nf = pl.num_programs(0)
    S = x_ref.shape[0]; nt_ = S // T
    gain = gain_ref[1:2, :]
    @pl.when(f == 0)
    def _():
        @pl.loop(0, nt_)
        def _(i):
            t = pl.ds(pl.multiple_of(i*T, T), T)
            mid = x_ref[t, :].astype(f32) + nn(ob_ref[t, :], wo_ref[...])
            out_ref[t, :] = mid
            dmid_ref[t, :] = mid
            r = lax.rsqrt(jnp.mean(mid*mid, axis=-1, keepdims=True) + EPS)
            r_s[t, :] = jnp.broadcast_to(r, (T, 128))
            h2 = ((mid*r)*gain).astype(bf16)
            h2_s[t, :] = h2
            h2T_s[:, t] = h2.T
            dfb_s[t, :] = cot_ref[t, :].astype(bf16)
            dh2_s[t, :] = jnp.zeros_like(mid)
    @pl.loop(0, nt_)
    def _(i):
        t = pl.ds(pl.multiple_of(i*T, T), T)
        h2 = h2_s[t, :]; dfb = dfb_s[t, :]
        g = nn(h2, wgu_ref[0]); u = nn(h2, wgu_ref[1])
        dh = nt(dfb, wd_ref[...])
        sig = 0.5*jnp.tanh(0.5*g)+0.5
        silu = g*sig
        hid = (silu*u).astype(bf16)
        dg = (dh*u*(sig*(1.0+g*(1.0-sig)))).astype(bf16)
        du = (dh*silu).astype(bf16)
        hid_s[t, :] = hid; dg_s[t, :] = dg; du_s[t, :] = du
        out_ref[t, :] += nn(hid, wd_ref[...])
        dh2_s[t, :] += nt(dg, wgu_ref[0]) + nt(du, wgu_ref[1])
    dwd_ref[...] = tn(hid_s[...], dfb_s[...]).astype(bf16)
    dwgu_ref[0] = nn(h2T_s[...], dg_s[...]).astype(bf16)
    dwgu_ref[1] = nn(h2T_s[...], du_s[...]).astype(bf16)
    @pl.when(f == nf-1)
    def _():
        @pl.loop(0, nt_)
        def _(i):
            t = pl.ds(pl.multiple_of(i*T, T), T)
            mid = dmid_ref[t, :]; r = r_s[t, 0:1]
            xh = mid*r; dh = dh2_s[t, :]; w = dh*gain
            back = r*(w - xh*jnp.mean(w*xh, axis=-1, keepdims=True))
            dmid = cot_ref[t, :] + back
            dmid_ref[t, :] = dmid
            dab = dmid.astype(bf16)
            h2_s[t, :] = dab
            dob_ref[t, :] = nt(dab, wo_ref[...]).astype(bf16)
            dobT_ref[:, t] = nt(wo_ref[...], dab).astype(bf16)
        dwo_ref[...] = nn(obT_ref[...], h2_s[...]).astype(bf16)

def mlp(x, ob, obT, cot, wo, wgu, wd, gains, FC=512, T=256):
    S, D = x.shape; FF = wd.shape[0]
    full = lambda *s: pl.BlockSpec(s, lambda f: (0,)*len(s), pipeline_mode=pl.Buffered(1))
    return pl.pallas_call(
        functools.partial(mlp_kernel, T), grid=(FF//FC,),
        in_specs=[full(S,D), full(S,D), full(D,S), full(S,D), full(D,D),
                  pl.BlockSpec((2,D,FC), lambda f:(0,0,f)), pl.BlockSpec((FC,D), lambda f:(f,0)), full(8,D)],
        out_specs=[full(S,D), full(S,D), full(S,D), full(D,S), full(D,D),
                  pl.BlockSpec((2,D,FC), lambda f:(0,0,f)), pl.BlockSpec((FC,D), lambda f:(f,0))],
        out_shape=[jax.ShapeDtypeStruct((S,D),f32), jax.ShapeDtypeStruct((S,D),f32), jax.ShapeDtypeStruct((S,D),bf16),
                   jax.ShapeDtypeStruct((D,S),bf16), jax.ShapeDtypeStruct((D,D),bf16),
                   jax.ShapeDtypeStruct((2,D,FF),bf16), jax.ShapeDtypeStruct((FF,D),bf16)],
        scratch_shapes=[pltpu.VMEM((S,D),bf16), pltpu.VMEM((D,S),bf16), pltpu.VMEM((S,D),bf16), pltpu.VMEM((S,D),f32),
                        pltpu.VMEM((S,128),f32), pltpu.VMEM((S,FC),bf16), pltpu.VMEM((S,FC),bf16), pltpu.VMEM((S,FC),bf16)],
        compiler_params=pltpu.CompilerParams(vmem_limit_bytes=62*2**20),
        name="mlp",
    )(x, ob, obT, cot, wo, wgu, wd, gains)

H, HD = 12, 64
NEG = -1e30
VM = pl.BlockSpec(memory_space=pltpu.VMEM)
def tnt(a,b): return lax.dot_general(a,b,(((0,),(1,)),((),())),preferred_element_type=f32)

def seg_rows(lens_ref, S):
    slot = lax.broadcasted_iota(jnp.int32, (8, S), 1)
    seg = jnp.zeros((8, S), jnp.int32); start = jnp.zeros((8, S), jnp.int32)
    end = jnp.int32(0)
    for s in range(lens_ref.shape[1]-1):
        end = end + lens_ref[0, s]
        past = (slot >= end).astype(jnp.int32)
        seg += past
        start += past * lens_ref[0, s]
    return seg, slot - start


MESH = pl.DeviceIdType.MESH

def flip(v, b):
    return v + b - 2*b*lax.rem(lax.div(v, b), 2)

def cut(rows):
    return rows // 3 // 16 * 16

class Place:
    def __init__(self):
        d, z = lax.axis_index("dp"), lax.axis_index("rep")
        self.d, self.z = d, z
        self.y, self.x, self.c = lax.div(d, 4), lax.rem(lax.div(d, 2), 2), lax.rem(d, 2)
        self.S, self.X, self.Y = (flip(d, 1), z), (flip(d, 2), z), (flip(d, 4), z)
        self.Z, self.I = (d, flip(z, 1)), (d, 3 - z)
        self.inner = (z == 1) | (z == 2)

def settle(sem, view):
    pltpu.make_async_copy(view, view, sem).wait()

class Gather:
    def __init__(self, at, here, ref, send, recv, lead=None, cols=slice(None)):
        self.at, self.ref, self.send, self.recv, self.lead, self.cols = at, ref, send, recv, lead, cols
        r = ref.shape[-2]; a = cut(r)
        p = lax.rem(at.z, 2)
        self.parts = {"all": (0, r), "zb": (p*a, r - a), "z": (p*(r - a), a), "b": (a, r - 2*a)}
        self.r, self.a = r, a
        at_ = at
        self.own, self.xs, self.ys, self.xys = (at_.y, at_.x, at_.c), (at_.y, 1 - at_.x, at_.c), (1 - at_.y, at_.x, at_.c), (1 - at_.y, 1 - at_.x, at_.c)
    def view(self, who, part="all"):
        off, m = self.parts[part]
        rows = slice(None) if part == "all" else pl.ds(off if isinstance(off, int) else pl.multiple_of(off, 16), m)
        return self.ref.at[(() if self.lead is None else (self.lead,)) + tuple(who) + (rows, self.cols)]
    def put(self, who, part, dev, out, sem):
        v = self.view(who, part)
        pltpu.make_async_remote_copy(src_ref=v, dst_ref=v, send_sem=self.send.at[out], recv_sem=self.recv.at[sem], device_id=dev, device_id_type=MESH).start()
    def some(self, *idx):
        return self.ref.at[(() if self.lead is None else (self.lead,)) + idx + (self.cols,)]
    def begin(self):
        self.put(self.own, "zb", self.at.X, 1, 0); self.put(self.own, "zb", self.at.Y, 1, 0); self.put(self.own, "all", self.at.S, 0, 3)
    def first(self):
        settle(self.recv.at[0], self.some(0, 0, slice(None), slice(0, self.r - self.a)))
        self.put(self.xs, "z", self.at.Y, 2, 1); self.put(self.ys, "b", self.at.X, 2, 1)
        self.put(self.xs, "z", self.at.Z, 1, 4); self.put(self.ys, "z", self.at.Z, 1, 4)
    def second(self):
        settle(self.recv.at[1], self.some(0, 0, 0, slice(0, self.r - self.a)))
        self.put(self.xys, "z", self.at.Z, 2, 2)
        settle(self.recv.at[4], self.some(0, 0, slice(None), slice(0, self.a)))
        self.put(self.xs, "all", self.at.S, 0, 3); self.put(self.ys, "all", self.at.S, 0, 3)
    def third(self):
        settle(self.recv.at[2], self.some(0, 0, 0, slice(0, self.a)))
        self.put(self.xys, "all", self.at.S, 0, 3)
    def sibling(self):
        settle(self.recv.at[3], self.some(0, slice(None), slice(None), slice(None)))
    def sent(self):
        settle(self.send.at[0], self.some(0, slice(None), slice(None), slice(None)))
        settle(self.send.at[1], self.some(0, 0, slice(None), slice(None)))
        settle(self.send.at[2], self.some(0, 0, 0, slice(None)))

class Sum:
    def __init__(self, at, ref, lead, cols, rs, rx, r2, zr, out, send, recv, loc):
        self.at, self.ref, self.lead, self.cols, self.rs, self.rx, self.r2, self.zr, self.out = at, ref, lead, cols, rs, rx, r2, zr, out
        self.send, self.recv, self.loc = send, recv, loc
        self.r = ref.shape[-2]; self.h = self.r // 2
        self.halves = (slice(0, self.h), slice(self.h, self.r))
    def view(self, y, x, c, rows=slice(None)):
        return self.ref.at[(() if self.lead is None else (self.lead,)) + (y, x, c, rows, self.cols)]
    def put(self, src, dst, dev, sem):
        pltpu.make_async_remote_copy(src_ref=src, dst_ref=dst, send_sem=self.send.at[min(sem, 3)], recv_sem=self.recv.at[sem], device_id=dev, device_id_type=MESH).start()
    def add(self, dst, *srcs):
        if len(dst.shape) == 2:
            v = srcs[0][...]
            for s in srcs[1:]: v = v + s[...]
            dst[...] = v
        else:
            for i in range(dst.shape[0]): self.add(dst.at[i], *(s.at[i] for s in srcs))
    def sub(self, ref, *idx):
        return ref.at[(() if self.lead is None else (slice(None),)) + idx]
    def a(self):
        al = slice(None)
        self.put(self.view(al, al, 1 - self.at.c), self.rs, self.at.S, 0)
    def b(self):
        A = self.at
        settle(self.recv.at[0], self.rs)
        def got(y, x):
            p = self.view(y, x, A.c)
            self.add(p, p, self.sub(self.rs, y, x))
        got(1 - A.y, 1 - A.x); got(A.y, 1 - A.x)
        self.put(self.view(slice(None), 1 - A.x, A.c, self.halves[0]), self.rx.at[0], A.X, 1)
        got(1 - A.y, A.x)
        self.put(self.view(1 - A.y, slice(None), A.c, self.halves[1]), self.rx.at[1], A.Y, 1)
        got(A.y, A.x)
    def c(self):
        A = self.at
        settle(self.recv.at[1], self.rx)
        p = self.view(1 - A.y, A.x, A.c, self.halves[0])
        self.add(p, p, self.sub(self.rx.at[0], 1 - A.y))
        self.put(p, self.r2.at[0], A.Y, 2)
        p = self.view(A.y, 1 - A.x, A.c, self.halves[1])
        self.add(p, p, self.sub(self.rx.at[1], 1 - A.x))
        self.put(p, self.r2.at[1], A.X, 2)
    def piece(self): return self.view(self.at.y, self.at.x, self.at.c)
    def fin(self, inner): return pltpu.make_async_copy(self.piece() if inner else self.zr.at[0], self.out, self.loc)
    def e(self):
        A = self.at
        settle(self.recv.at[2], self.r2)
        for h, w in ((0, A.y), (1, A.x)):
            p = self.view(A.y, A.x, A.c, self.halves[h])
            self.add(p, p, self.sub(self.rx.at[h], w), self.r2.at[h])
        @pl.when(jnp.logical_not(A.inner))
        def _(): self.put(self.piece(), self.zr.at[0], A.Z, 3)
    def f(self):
        @pl.when(self.at.inner)
        def _():
            settle(self.recv.at[3], self.zr.at[0])
            self.add(self.zr.at[0], self.zr.at[0], self.piece())
            self.put(self.zr.at[0], self.zr.at[1], self.at.I, 4)
    def g(self):
        @pl.when(self.at.inner)
        def _():
            settle(self.recv.at[4], self.zr.at[1])
            self.add(self.piece(), self.zr.at[0], self.zr.at[1])
            self.put(self.piece(), self.zr.at[0], self.at.Z, 3)
            self.fin(True).start()
    def h_(self):
        @pl.when(jnp.logical_not(self.at.inner))
        def _():
            settle(self.recv.at[3], self.zr.at[0])
            self.fin(False).start()
    def drain(self):
        settle(self.send.at[0], self.rs); settle(self.send.at[1], self.rx); settle(self.send.at[2], self.r2)
        @pl.when(self.at.inner)
        def _(): settle(self.send.at[3], self.zr)
        @pl.when(jnp.logical_not(self.at.inner))
        def _(): settle(self.send.at[3], self.zr.at[0])
        self.fin(True).wait()

ANY = pl.BlockSpec(memory_space=pl.ANY)
SM = pl.BlockSpec(memory_space=pltpu.SMEM)
B = 256

def spread_gain(pieces, D):
    n, wide = pieces.shape[0], D // pieces.shape[0]
    lane = lax.broadcasted_iota(jnp.int32, (8, 128), 1)
    total = jnp.zeros((8, D), f32)
    for i in range(n):
        row = jnp.concatenate([jnp.where(lane < wide, pieces[i], 0.0), jnp.zeros((8, D - 128), f32)], axis=1)
        total += row if i == 0 else pltpu.roll(row, i*wide, 1)
    return total

def forward_attention(lens_ref, x_ref, freq_ref, gain_of, weights_in, w_ref, qT_s, kT_s, vT_s, oT_s, lse_s, cos_s, sin_s, segc_s, segr_s, bias_s, hook):
    S, D = x_ref.shape
    n = S // B
    seg, place = seg_rows(lens_ref, S)
    ang = jnp.broadcast_to(place[0:1, :].astype(f32), (HD//2, S)) * freq_ref[:, 0:1]
    cos_s[...] = jnp.cos(ang); sin_s[...] = jnp.sin(ang)
    segf = jnp.broadcast_to(seg[0:1, :].astype(f32), (128, S))
    segr_s[...] = segf[0:8]
    segc_s[...] = segf.T
    weights_in()
    gain = gain_of()
    @pl.loop(0, n)
    def _(i):
        t = pl.ds(pl.multiple_of(i*B, B), B)
        xf = x_ref[t, :].astype(f32)
        r = lax.rsqrt(jnp.mean(xf*xf, axis=-1, keepdims=True) + EPS)
        h1 = ((xf*r)*gain).astype(bf16)
        c = cos_s[:, t]; s = sin_s[:, t]
        for w, dst, sc in ((0, qT_s, 0.125), (1, kT_s, 1.0)):
            y = tnt(w_ref[w], h1)
            for h in range(H):
                a = y[h*HD:h*HD+32]; b = y[h*HD+32:h*HD+64]
                dst[h*HD:h*HD+32, t] = ((a*c - b*s)*sc).astype(bf16)
                dst[h*HD+32:h*HD+64, t] = ((b*c + a*s)*sc).astype(bf16)
        vT_s[:, t] = tnt(w_ref[2], h1).astype(bf16)
    hook("proj")
    for i in range(n):
        k0 = max(0, i-2)*B; nk = i*B + B - k0
        q0 = i*B
        kid = lax.broadcasted_iota(jnp.int32, (nk, B), 0) + k0
        qid = lax.broadcasted_iota(jnp.int32, (nk, B), 1) + q0
        ok = (segc_s[k0:k0+nk, 0:1] == segr_s[0:1, q0:q0+B]) & (kid <= qid)
        bias_s[0:nk, :] = jnp.where(ok, 0.0, NEG)
        @pl.loop(0, H//2)
        def _(p):
            for e in range(2):
                rows = pl.ds(pl.multiple_of(p*128 + e*64, 64), 64)
                s = tn(kT_s[rows, k0:k0+nk], qT_s[rows, q0:q0+B]) + bias_s[0:nk, :]
                m = jnp.max(s, axis=0, keepdims=True)
                ex = jnp.exp(s - m)
                l = jnp.sum(ex, axis=0, keepdims=True)
                o = nn(vT_s[rows, k0:k0+nk], ex.astype(bf16)) * (1.0/l)
                oT_s[rows, q0:q0+B] = o.astype(bf16)
                lse_s[pl.ds(p*2+e, 1), q0:q0+B] = m + jnp.log(l)
        hook(i)

def local_body(lens_ref, x_ref, freq_ref, gain_ref, w_ref, qT_ref, kT_ref, vT_ref, oT_ref, lse_ref, cos_ref, sin_ref, segc_ref, segr_ref, bias_s):
    forward_attention(lens_ref, x_ref, freq_ref, lambda: gain_ref[0:1, :], lambda: None, w_ref, qT_ref, kT_ref, vT_ref, oT_ref,
                      lse_ref, cos_ref, sin_ref, segc_ref, segr_ref, bias_s, lambda at: None)

def attn_fwd(lens, x, gains, freq, wqkv):
    S, D = x.shape
    sh = lambda s, d: jax.ShapeDtypeStruct(s, d)
    return pl.pallas_call(local_body,
        in_specs=[SM]+[VM]*4, out_specs=[VM]*9,
        out_shape=[sh((D,S),bf16)]*4 + [sh((16,S),f32), sh((32,S),f32), sh((32,S),f32), sh((S,128),f32), sh((8,S),f32)],
        scratch_shapes=[pltpu.VMEM((768,256),f32)],
        compiler_params=pltpu.CompilerParams(vmem_limit_bytes=62*2**20), name="attend")(lens, x, freq, gains, wqkv)

GW = 256

def backward_attention(x_ref, gain_ref, w_ref, ig_s, ig_ready, ig_done, qT_ref, kT_ref, vT_ref, dob_ref, dobT_ref, lse_ref, cos_ref, sin_ref, segc_ref, segr_ref,
                       dw_s, bias_s, q_s, dqT_s, dk_s, dv_s, g_s, h1T_s, hook):
    S, D = x_ref.shape
    n = S // B
    gain = gain_ref[0:1, :]
    hook("start")
    blocks = []
    at = 0
    for i in range(n):
        k0 = max(0, i-2)*B; nk = i*B + B - k0
        q0 = i*B
        kid = lax.broadcasted_iota(jnp.int32, (nk, B), 0) + k0
        qid = lax.broadcasted_iota(jnp.int32, (nk, B), 1) + q0
        ok = (segc_ref[k0:k0+nk, 0:1] == segr_ref[0:1, q0:q0+B]) & (kid <= qid)
        bias_s[at:at+nk, :] = jnp.where(ok, 0.0, NEG)
        blocks.append((q0, k0, nk, at)); at += nk
    q_s[...] = qT_ref[...].T
    @pl.loop(0, n)
    def _(i):
        t = pl.ds(pl.multiple_of(i*B, B), B)
        xf = x_ref[t, :].astype(f32)
        r = lax.rsqrt(jnp.mean(xf*xf, axis=-1, keepdims=True) + EPS)
        h1T_s[:, t] = ((xf*r)*gain).astype(bf16).T
    hook("ready")
    lane = lax.broadcasted_iota(jnp.int32, (B, 128), 1)
    @pl.loop(0, H//2)
    def _(p):
        cols = pl.ds(pl.multiple_of(p*128, 128), 128)
        dk_s[...] = jnp.zeros_like(dk_s); dv_s[...] = jnp.zeros_like(dv_s)
        for q0, k0, nk, at in blocks:
            dv = dk = None
            for e in range(2):
                rows = pl.ds(pl.multiple_of(p*128 + e*64, 64), 64)
                mine = (lane < 64) if e == 0 else (lane >= 64)
                dobz = jnp.where(mine, dob_ref[q0:q0+B, cols], 0).astype(bf16)
                qz = jnp.where(mine, q_s[q0:q0+B, cols], 0).astype(bf16)
                s = tn(kT_ref[rows, k0:k0+nk], qT_ref[rows, q0:q0+B]) + bias_s[at:at+nk, :]
                pr = jnp.exp(s - lse_ref[pl.ds(p*2+e, 1), q0:q0+B])
                dp = tn(vT_ref[rows, k0:k0+nk], dobT_ref[rows, q0:q0+B])
                inner = jnp.sum(pr*dp, axis=0, keepdims=True)
                ds = (pr*(dp - inner)).astype(bf16)
                dve = nn(pr.astype(bf16), dobz)
                dke = nn(ds, qz)
                dqT_s[e*64:e*64+64, q0:q0+B] = nn(kT_ref[rows, k0:k0+nk], ds) * 0.125
                dv = dve if dv is None else dv + dve
                dk = dke if dk is None else dk + dke
            dv_s[k0:k0+nk, :] += dv
            dk_s[k0:k0+nk, :] += dk
        c = cos_ref[...]; s = sin_ref[...]
        for j, src in ((0, dqT_s[...]), (1, dk_s[...].T)):
            parts = []
            for e in range(2):
                a = src[e*HD:e*HD+32]; b = src[e*HD+32:e*HD+64]
                parts += [a*c + b*s, b*c - a*s]
            g_s[j, :, cols] = jnp.concatenate(parts, axis=0).astype(bf16).T
        g_s[2, :, cols] = dv_s[...].astype(bf16)
        @pl.when(lax.rem(p, 2) == 1)
        def _():
            g = lax.div(p, 2)
            wide = pl.ds(pl.multiple_of(g*GW, GW), GW)
            for j in range(3):
                dw_s[g, j] = nn(h1T_s[...], g_s[j, :, wide]).astype(bf16)
        for k in range(H//2):
            @pl.when(p == k)
            def _():
                hook(k)
    ig_ready()
    for i in range(n):
        t = pl.ds(i*B, B)
        xf = x_ref[t, :].astype(f32)
        r = lax.rsqrt(jnp.mean(xf*xf, axis=-1, keepdims=True) + EPS)
        xh = xf*r
        dh = nt(g_s[0, t, :], w_ref[0]) + nt(g_s[1, t, :], w_ref[1]) + nt(g_s[2, t, :], w_ref[2])
        w = dh*gain
        ig_s[t, :] += r*(w - xh*jnp.mean(w*xh, axis=-1, keepdims=True))
        ig_done(i, t)
        hook("tile%d" % i)

def scratch_bwd(S, D):
    n = S // B
    area = sum(min(i+1, 3) for i in range(n))*B
    return [pltpu.VMEM((D//GW, 3, D, GW), bf16), pltpu.VMEM((area, B), f32), pltpu.VMEM((S, D), bf16), pltpu.VMEM((128, S), f32),
            pltpu.VMEM((S, 128), f32), pltpu.VMEM((S, 128), f32), pltpu.VMEM((3, S, D), bf16), pltpu.VMEM((D, S), bf16)]

def bwd_local_body(x_ref, gain_ref, w_ref, dmid_ref, qT_ref, kT_ref, vT_ref, dob_ref, dobT_ref, lse_ref, cos_ref, sin_ref, segc_ref, segr_ref,
                   ig_ref, dw_ref, bias_s, q_s, dqT_s, dk_s, dv_s, g_s, h1T_s):
    ig_ref[...] = dmid_ref[...]
    backward_attention(x_ref, gain_ref, w_ref, ig_ref, lambda: None, lambda i, t: None, qT_ref, kT_ref, vT_ref, dob_ref, dobT_ref, lse_ref, cos_ref, sin_ref,
                       segc_ref, segr_ref, dw_ref, bias_s, q_s, dqT_s, dk_s, dv_s, g_s, h1T_s, lambda at: None)

def attn_bwd(x, gains, wqkv, dmid, qT, kT, vT, dob, dobT, lse, cos, sin, segc, segr):
    S, D = x.shape
    sh = lambda s, d: jax.ShapeDtypeStruct(s, d)
    ig, dw = pl.pallas_call(bwd_local_body,
        in_specs=[VM]*14, out_specs=[VM]*2,
        out_shape=[sh((S,D),f32), sh((D//GW,3,D,GW),bf16)],
        scratch_shapes=scratch_bwd(S, D)[1:],
        compiler_params=pltpu.CompilerParams(vmem_limit_bytes=62*2**20), name="attend_back")(x, gains, wqkv, dmid, qT, kT, vT, dob, dobT, lse, cos, sin, segc, segr)
    return ig, jnp.moveaxis(dw, 0, 2).reshape(3, D, D)


FC, MT = 512, 512

def staggered(items, first, middle, last, at=None, between=None):
    a = first(items[0]); prev = None
    for i, it in enumerate(items):
        nxt = first(items[i+1]) if i + 1 < len(items) else None
        m = middle(it, a)
        if prev is not None: last(items[i-1], prev)
        if i == at: between()
        prev, a = m, nxt
    last(items[-1], prev)

def layer_body(n_dp, lens_ref, gain_ref, x_hbm, cot_hbm, qw_hbm, ow_hbm, gw_hbm, dw_hbm,
               out_o, ig_o, gq_o, gou_o, ggu_o, gdn_o, mask_o, h1_o,
               wq_s, wo_s, wgu_s, wd_s, qT_s, kT_s, vT_s, oT_s, cos_s, sin_s, segc_s, segr_s, lse_s, dlt_s, gain_s, gp_s,
               out_s, dh2_s, mid_s, acc_s, h2T_s, dfb_s, ch_s, dw_s,
               g_rs, g_rx, g_r2, g_z, n_rs, n_rx, n_r2, n_z, o_rs, o_rx, o_r2, o_z, q_rx, q_r2, q_z,
               ag_send, ag_recv, gn_send, gn_recv, rs_send, rs_recv, rs_loc, loc):
    S, D = x_hbm.shape
    x_s, h1T_s, h1T_late = dfb_s, h2T_s, oT_s
    nf = wd_s.shape[0]
    FF = nf*FC
    n, ng = S//B, len(HEADS_IN)
    rq, rd = D//n_dp, FF//n_dp
    sub = rd//nf
    each = [(y, x, c) for y in range(2) for x in range(2) for c in range(2)]
    def whole(v): return v.reshape(-1, v.shape[-1])
    at_ = Place()
    d, z = at_.d, at_.z
    mine = (at_.y, at_.x, at_.c)
    others = [lax.rem(d + j, n_dp) for j in range(1, n_dp)]
    gp_s[...] = jnp.zeros_like(gp_s)
    bar = pltpu.get_barrier_semaphore()
    met = [(o, z) for o in others] + [at_.Z, at_.I]
    for dev in met: pl.semaphore_signal(bar, inc=1, device_id=dev, device_id_type=MESH)

    loads = {}
    def load(key, src, dst):
        c = pltpu.make_async_copy(src, dst, loc.at[len(loads)]); c.start(); loads[key] = c
    for c in range(3): load("q%d" % c, qw_hbm.at[c], out_s.at[c*rq:(c+1)*rq, :])
    load("x", x_hbm, x_s)
    load("o", ow_hbm, out_s.at[3*rq:4*rq, :])
    load("d", dw_hbm, out_s.at[4*rq:4*rq+rd, :])
    wides = [(a, min(D, FF - a)) for a in range(0, FF, D)]
    for c in range(2):
        for k, (a, w) in enumerate(wides):
            load("g%d%d" % (c, k), gw_hbm.at[c, :, a:a+w], dh2_s.at[(c*len(wides)+k)*rq:(c*len(wides)+k+1)*rq, 0:w])
    cot_base = len(loads)
    base = cot_base + 4
    HB = B//2
    def cot_copies(i): return [pltpu.make_async_copy(cot_hbm.at[(i % n)*B + k*HB:(i % n)*B + (k+1)*HB, :], acc_s.at[i % 2 * 2 + k, :, 0:D],
                                                     loc.at[cot_base + i % 2 * 2 + k]) for k in range(2)]
    def cot_start(i):
        for c in cot_copies(i): c.start()
    def cot_get(i):
        for c in cot_copies(i): c.wait()
        return jnp.concatenate([acc_s[i % 2 * 2 + k, :, 0:D] for k in range(2)], axis=0)
    cot_start(0); cot_start(1)

    G = []
    def gather(*a): G.append(Gather(at_, mine, a[0], ag_send.at[len(G)], ag_recv.at[len(G)], *a[1:]))
    for g in range(D//GW): gather(wq_s, slice(None), slice(g*GW, (g+1)*GW))
    gather(wo_s)
    of_gu, of_dn = [], []
    for f in range(nf):
        of_gu.append(len(G))
        gather(wgu_s, slice(None), slice(f*FC, (f+1)*FC))
        if f % 2 == 0:
            of_dn.append(len(G))
            gather(wd_s.at[f:f+2], slice(None))

    R = []
    def unit(ref, lead, cols, bufs, out):
        u = len(R)
        R.append(Sum(at_, ref, lead, cols, *bufs, out, rs_send.at[u], rs_recv.at[u], rs_loc.at[u]))
    al = slice(None)
    for f in range(nf):
        cols = slice(f*FC, (f+1)*FC)
        unit(wgu_s, al, cols, [b.at[f] for b in (g_rs, g_rx, g_r2, g_z)], ggu_o.at[:, :, cols])
    for h in range(nf//2):
        unit(wd_s.at[2*h:2*h+2], al, al, [b.at[h] for b in (n_rs, n_rx, n_r2, n_z)], gdn_o.at[2*h:2*h+2])
    unit(wo_s, None, al, (o_rs, o_rx, o_r2, o_z), gou_o)
    groups, c0 = [], 0
    for g, many in enumerate(HEADS_IN):
        cols = slice(c0, c0 + many*HD)
        groups.append(cols)
        up, left = c0//FC, c0 % FC
        rs = ch_s.at[:, :, :, up*rq:(up+1)*rq, left:left + many*HD]
        unit(dw_s, al, cols, [rs] + [b.at[..., cols] for b in (q_rx, q_r2, q_z)], gq_o.at[:, :, cols])
        c0 += many*HD
    done = [sum(HEADS_IN[:g+1])//2 - 1 for g in range(ng)]
    def hook(at):
        for what in PLAN.get(at, ()):
            k = int(what[1:])
            if what[0] == "B": G[k].begin()
            elif what[0] in "1234": getattr(G[k], ("first", "second", "third", "sibling")[int(what[0])-1])()
            elif what[0] == "h": R[k].h_()
            else: getattr(R[k], what[0])()

    gp_s[pl.ds(d, 1), 0:2, 0:gain_ref.shape[1]] = gain_ref[...].astype(bf16).astype(f32)[None]
    gains = [pltpu.make_async_remote_copy(src_ref=gp_s.at[d], dst_ref=gp_s.at[d], send_sem=gn_send.at[j], recv_sem=gn_recv.at[j],
                                          device_id=(o, z), device_id_type=MESH) for j, o in enumerate(others)]
    for c in range(3): loads["q%d" % c].wait()
    for g in range(D//GW):
        cols = slice(g*GW, (g+1)*GW)
        for c in range(3): wq_s[(c,) + mine + (slice(None), cols)] = out_s[c*rq:(c+1)*rq, cols].astype(bf16)
        if g == 0: pl.semaphore_wait(bar, len(met))
        hook("begin%d" % g)
        if g == 0:
            for k in gains: k.start()
    loads["o"].wait()
    wo_s[mine] = out_s[3*rq:4*rq, :].astype(bf16)
    hook("s0")
    for k in loads:
        if k[0] == "g": loads[k].wait()
    for c in range(2):
        def at(col):
            k = col//D
            return dh2_s[(c*len(wides)+k)*rq:(c*len(wides)+k+1)*rq, col - k*D:col - k*D + sub]
        for f in range(nf):
            for o in range(0, n_dp, 2):
                two = jnp.concatenate([at(o*rd + f*sub), at((o+1)*rd + f*sub)], axis=1)
                wgu_s[(c,) + mine + (slice(None), slice(f*FC + o*sub, f*FC + (o+2)*sub))] = two.astype(bf16)
        if c == 0: hook("s0b")
    loads["d"].wait()
    for f in range(nf): wd_s[(f,) + mine] = out_s[4*rq + f*sub:4*rq + (f+1)*sub, :].astype(bf16)
    hook("s1")

    seg, place = seg_rows(lens_ref, S)
    half = lax.broadcasted_iota(jnp.int32, (HD//2, 128), 0).astype(f32)
    freq = jnp.exp(half*(-math.log(10000.0)/(HD//2)))
    ang = jnp.broadcast_to(place[0:1, :].astype(f32), (HD//2, S)) * freq[:, 0:1]
    cos_s[...] = jnp.cos(ang)
    hook("s1b")
    sin_s[...] = jnp.sin(ang)
    segf = jnp.broadcast_to(seg[0:1, :].astype(f32), (128, S))
    segr_s[...] = segf[0:8]
    segc_s[...] = segf.astype(bf16).T
    hook("s2")
    blocks = []
    at = {0: (0, 0), 1: (B, 0), 2: (0, B), 3: (0, 2*B)}
    for i in range(n):
        k0 = max(0, i-2)*B
        blocks.append((i*B, k0, i*B + B - k0) + at[i])
    def masks(between):
        for q0, k0, nk, r0, c0 in blocks:
            if q0 == 3*B: between()
            kid = lax.broadcasted_iota(jnp.int32, (nk, B), 0) + k0
            qid = lax.broadcasted_iota(jnp.int32, (nk, B), 1) + q0
            ok = (segc_s[k0:k0+nk, 0:1].astype(f32) == segr_s[0:1, q0:q0+B]) & (kid <= qid)
            dh2_s[r0:r0+nk, c0:c0+B] = jnp.where(ok, 0.0, NEG)
    masks(lambda: hook("s2b"))
    top = slice(0, 3*B)
    def trip(k, src, dst): return pltpu.make_async_copy(src, dst, loc.at[base + 5 + k])
    mask_out, mask_in = trip(0, dh2_s.at[top], mask_o.at[top]), trip(1, mask_o.at[top], dh2_s.at[top])
    h1_out, h1_in = trip(2, h1T_s, h1_o), trip(3, h1_o, h1T_late)
    mask_out.start()
    loads["x"].wait()
    hook("s3")
    for k in gains: k.wait_recv()
    gain_s[...] = spread_gain(gp_s[...], D)
    def normed(dst, between):
        for i in range(n):
            t = slice(i*B, (i+1)*B)
            xf = x_s[t, :].astype(f32)
            r = lax.rsqrt(jnp.mean(xf*xf, axis=-1, keepdims=True) + EPS)
            dst[:, t] = ((xf*r)*gain_s[0:1, :]).astype(bf16).T
            if i == 1: between()
    normed(h1T_s, lambda: hook("s4"))
    h1_out.start()
    hook("start")
    many = GW//HD
    @pl.loop(0, D//GW)
    def _(g):
        for k in range(D//GW):
            @pl.when(g == k)
            def _(): hook("p%d" % k)
        cols = pl.ds(pl.multiple_of(g*GW, GW), GW)
        for w, dst, sc in ((0, qT_s, 0.125), (1, kT_s, 1.0), (2, vT_s, None)):
            for t0 in range(0, S, MT):
                t = slice(t0, t0+MT)
                y = tn(whole(wq_s[w, :, :, :, :, cols]), h1T_s[:, t])
                if sc is None: dst[cols, t] = y.astype(bf16)
                else:
                    c = cos_s[:, t]; s = sin_s[:, t]
                    for h in range(many):
                        a = y[h*HD:h*HD+32]; b = y[h*HD+32:h*HD+64]
                        dst[pl.ds(pl.multiple_of(g*GW + h*HD, 32), 32), t] = ((a*c - b*s)*sc).astype(bf16)
                        dst[pl.ds(pl.multiple_of(g*GW + h*HD + 32, 32), 32), t] = ((b*c + a*s)*sc).astype(bf16)
        @pl.loop(0, many//2)
        def _(half):
            p = g*(many//2) + half
            rs = [pl.ds(pl.multiple_of(p*128 + e*64, 64), 64) for e in range(2)]
            def scores(it):
                (q0, k0, nk, r0, c0), e = it
                return tn(kT_s[rs[e], k0:k0+nk], qT_s[rs[e], q0:q0+B]) + dh2_s[r0:r0+nk, c0:c0+B]
            def soft(it, s):
                m = jnp.max(s, axis=0, keepdims=True)
                ex = jnp.exp(s - m)
                return m, ex.astype(bf16), jnp.sum(ex, axis=0, keepdims=True)
            def mix(it, mel):
                (q0, k0, nk, r0, c0), e = it
                m, ex, l = mel
                oT_s[rs[e], q0:q0+B] = (nn(vT_s[rs[e], k0:k0+nk], ex) * (1.0/l)).astype(bf16)
                lse_s[pl.ds(p*2+e, 1), q0:q0+B] = m + jnp.log(l)
            staggered([(b, e) for b in blocks for e in range(2)], scores, soft, mix)
            for k in range(H//2):
                @pl.when(p == k)
                def _(): hook("a%d" % k)

    hook("mlp")
    mask_out.wait(); h1_out.wait()
    gain2 = gain_s[1:2, :]
    for i in range(n):
        t = slice(i*B, (i+1)*B)
        mid = x_s[t, :].astype(f32) + tn(oT_s[:, t], whole(wo_s[...]))
        out_s[t, :] = mid; mid_s[t, :] = mid
        r = lax.rsqrt(jnp.mean(mid*mid, axis=-1, keepdims=True) + EPS)
        h2T_s[:, t] = ((mid*r)*gain2).astype(bf16).T
        dfb_s[t, :] = cot_get(i).astype(bf16)
        cot_start(i+2)
        dh2_s[t, :] = jnp.zeros_like(mid)
    def gu_of(k, cols): return whole(wgu_s[k, :, :, :, :, cols])
    @pl.loop(0, nf)
    def _(f):
        cols = pl.ds(pl.multiple_of(f*FC, FC), FC)
        def first(i):
            t = slice(i*MT, (i+1)*MT)
            return tn(h2T_s[:, t], gu_of(0, cols)), tn(h2T_s[:, t], gu_of(1, cols)), nt(dfb_s[t, :], whole(wd_s[f]))
        def middle(i, gud):
            g, u, dh = gud
            t = slice(i*MT, (i+1)*MT)
            sig = 0.5*jnp.tanh(0.5*g) + 0.5
            silu = g*sig
            hid = (silu*u).astype(bf16)
            dg = (dh*u*(sig + silu*(1.0 - sig))).astype(bf16)
            du = (dh*silu).astype(bf16)
            for j, v in enumerate((hid, dg, du)):
                for k in range(2): ch_s[j, i, k] = v[k*MT//2:(k+1)*MT//2]
            if i == 0:
                for k in range(nf):
                    @pl.when(f == k)
                    def _(): hook("f%dmid" % k)
            return hid, dg, du
        def last(i, hdd):
            hid, dg, du = hdd
            t = slice(i*MT, (i+1)*MT)
            dh2_s[t, :] += nt(dg, gu_of(0, cols)) + nt(du, gu_of(1, cols))
        staggered(list(range(S//MT)), first, middle, last)
        for k in range(nf):
            @pl.when(f == k)
            def _():
                G[of_gu[k]].sent()
                if k % 2 == 0: G[of_dn[k//2]].sent()
        for k in range(2):
            v = nn(h2T_s[...], whole(ch_s[1+k])).astype(bf16)
            for o, w in enumerate(each): wgu_s[(k,) + w + (slice(None), cols)] = v[o*rq:(o+1)*rq]
        for k in range(nf):
            @pl.when(f == k)
            def _(): hook("f%dgu" % k)
        for i in range(S//MT):
            t = slice(i*MT, (i+1)*MT)
            out_s[t, :] += nn(whole(ch_s[0, i]), whole(wd_s[f]))
        v = tn(whole(ch_s[0]), dfb_s[...]).astype(bf16)
        for o, w in enumerate(each): wd_s[(f,) + w] = v[o*sub:(o+1)*sub]
        for k in range(nf):
            @pl.when(f == k)
            def _(): hook("f%dend" % k)
    out_c = pltpu.make_async_copy(out_s, out_o, loc.at[base]); out_c.start()
    for i in range(n):
        t = slice(i*B, (i+1)*B)
        mid = mid_s[t, :]; dh = dh2_s[t, :]
        r = lax.rsqrt(jnp.mean(mid*mid, axis=-1, keepdims=True) + EPS)
        xh = mid*r; w = dh*gain2
        dmid = cot_get(i) + r*(w - xh*jnp.mean(w*xh, axis=-1, keepdims=True))
        if i + 2 < n: cot_start(i+2)
        mid_s[t, :] = dmid
        dab = dmid.astype(bf16)
        dfb_s[t, :] = dab
        h2T_s[:, t] = nt(whole(wo_s[...]), dab).astype(bf16)
        if i == 1: hook("e0")
    mask_in.start()
    G[3].sent()
    v = nn(oT_s[...], dfb_s[...]).astype(bf16)
    for o, w in enumerate(each): wo_s[w] = v[o*rq:(o+1)*rq]
    x_again = pltpu.make_async_copy(x_hbm, x_s, loc.at[0]); x_again.start()
    for h in range(H):
        r = slice(h*HD, (h+1)*HD)
        dlt_s[h:h+1, :] = jnp.sum(h2T_s[r, :].astype(f32)*oT_s[r, :].astype(f32), axis=0, keepdims=True)
    h1_in.start()
    hook("e1")
    mask_in.wait()

    dq_s, dk_s, dv_s = (acc_s.at[j] for j in range(3))
    @pl.loop(0, H//2)
    def _(p):
        rs = [pl.ds(pl.multiple_of(p*128 + e*64, 64), 64) for e in range(2)]
        dk_s[...] = jnp.zeros_like(dk_s); dv_s[...] = jnp.zeros_like(dv_s)
        def first(it):
            (q0, k0, nk, r0, c0), e = it
            return (tn(kT_s[rs[e], k0:k0+nk], qT_s[rs[e], q0:q0+B]) + dh2_s[r0:r0+nk, c0:c0+B],
                    tn(vT_s[rs[e], k0:k0+nk], h2T_s[rs[e], q0:q0+B]))
        def middle(it, sd):
            (q0, k0, nk, r0, c0), e = it
            s, dp = sd
            pr = jnp.exp(s - lse_s[pl.ds(p*2+e, 1), q0:q0+B])
            return pr.astype(bf16), (pr*(dp - dlt_s[pl.ds(p*2+e, 1), q0:q0+B])).astype(bf16)
        def last(it, pd):
            (q0, k0, nk, r0, c0), e = it
            pr, ds = pd
            r = slice(e*HD, (e+1)*HD)
            dv_s[r, k0:k0+nk] += nt(h2T_s[rs[e], q0:q0+B], pr)
            dk_s[r, k0:k0+nk] += nt(qT_s[rs[e], q0:q0+B], ds)
            dq_s[r, q0:q0+B] = nn(kT_s[rs[e], k0:k0+nk], ds) * 0.125
        def half():
            for k in range(H//2):
                @pl.when(p == k)
                def _(): hook("c%da" % k)
        staggered([(b, e) for b in blocks for e in range(2)], first, middle, last, 5, half)
        c = cos_s[...]; s = sin_s[...]
        for src, dst in ((dq_s, qT_s), (dk_s, kT_s)):
            for e in range(2):
                a = src[e*HD:e*HD+32, :]; b = src[e*HD+32:(e+1)*HD, :]
                dst[pl.ds(pl.multiple_of(p*128 + e*64, 32), 32), :] = (a*c + b*s).astype(bf16)
                dst[pl.ds(pl.multiple_of(p*128 + e*64 + 32, 32), 32), :] = (b*c - a*s).astype(bf16)
        vT_s[pl.ds(pl.multiple_of(p*128, 128), 128), :] = dv_s[...].astype(bf16)
        for k in range(H//2):
            @pl.when(p == k)
            def _():
                if k in done:
                    if k == done[0]: h1_in.wait()
                    cols = groups[done.index(k)]
                    for j, src in enumerate((qT_s, kT_s, vT_s)):
                        v = nt(h1T_late[...], src[cols, :]).astype(bf16)
                        for o, w in enumerate(each): dw_s[(j,) + w + (slice(None), cols)] = v[o*rq:(o+1)*rq]
                hook("c%d" % k)
    def ig_copy(i): return pltpu.make_async_copy(mid_s.at[i*B:(i+1)*B, :], ig_o.at[i*B:(i+1)*B, :], loc.at[base + 1 + i])
    gain1 = gain_s[0:1, :]
    x_again.wait()
    for i in range(n):
        t = slice(i*B, (i+1)*B)
        xf = x_s[t, :].astype(f32)
        r = lax.rsqrt(jnp.mean(xf*xf, axis=-1, keepdims=True) + EPS)
        xh = xf*r
        dh = tnt(qT_s[:, t], whole(wq_s[0])) + tnt(kT_s[:, t], whole(wq_s[1])) + tnt(vT_s[:, t], whole(wq_s[2]))
        w = dh*gain1
        mid_s[t, :] += r*(w - xh*jnp.mean(w*xh, axis=-1, keepdims=True))
        ig_copy(i).start()
        hook("t%d" % i)
    hook("end")
    for g in range(3): G[g].sent()
    for k in gains: k.wait_send()
    for u in R: u.drain()
    out_c.wait()
    for i in range(n): ig_copy(i).wait()

HEADS_IN = (4, 4, 2, 2)
PLAN = {
    "begin0": ("B0",),
    "s2": ("10", "B1", "B2"),
    "start": ("20",),
    "p0": ("11", "B3", "30", "12", "B4", "40"),
    "a0": ("21", "22", "13", "B5"),
    "a1": ("14", "B6", "31"),
    "p1": ("32", "41"),
    "a2": ("42", "23", "15", "B7"),
    "a3": ("24",),
    "a4": ("33", "25", "16", "B8"),
    "a5": ("43", "34", "17", "B9"),
    "mlp": ("35", "44", "45"),
    "f0mid": ("26", "27", "18", "19"),
    "f0gu": ("a0", "36"),
    "f0end": ("37", "46", "b0", "47"),
    "f1mid": ("28",),
    "f1gu": ("a1", "38", "29", "c0"),
    "f1end": ("a4", "b1", "48"),
    "f2mid": ("39", "e0", "b4"),
    "f2gu": ("a2", "49", "c1"),
    "f3mid": ("f0", "c4", "b2"),
    "f3gu": ("a3", "e1", "e4"),
    "f3end": ("a5", "g0", "b3"),
    "e0": ("c2", "b5"),
    "e1": ("a6", "f1"),
    "c0a": ("h0", "f4", "c3", "b6", "e2"),
    "c1a": ("g1", "c5"),
    "c1": ("a7", "f2", "e3"),
    "c2a": ("g4", "b7"),
    "c2": ("h1", "c6"),
    "c3a": ("g2", "f3", "e5"),
    "c3": ("a8", "c7", "h4"),
    "c4a": ("e6", "b8"),
    "c4": ("a9", "g3", "f5", "e7", "h2"),
    "c5a": ("f6", "b9"),
    "c5": ("a10", "c8"),
    "t0": ("g5", "f7", "c9", "b10"),
    "t1": ("h3", "e8"),
    "t2": ("g6", "e9"),
    "t3": ("c10",),
    "end": ("f8", "g7", "h5", "f9", "e10", "h6", "f10", "g8", "h7", "g9", "g10", "h8", "h9", "h10"),
}

def layer(n_dp, lens, gains, x, cot, qw, ow, gw, dw):
    S, D = x.shape
    FF = gw.shape[2]
    sh = lambda s, d: jax.ShapeDtypeStruct(s, d)
    b = lambda *s: pltpu.VMEM(s, bf16)
    w = lambda *s: pltpu.VMEM(s, f32)
    rq, rd, nf, ng = D//n_dp, FF//n_dp, FF//FC, len(HEADS_IN)
    ag, rs = 4 + nf + nf//2, nf + nf//2 + 1 + ng
    dma = pltpu.SemaphoreType.DMA
    c8 = (2, 2, 2)
    def bufs(lead, r, cols, many=()):
        return [b(*many, *lead, 2, 2, r, cols), b(*many, 2, *lead, 2, r//2, cols), b(*many, 2, *lead, r//2, cols), b(*many, 2, *lead, r, cols)]
    return pl.pallas_call(functools.partial(layer_body, n_dp),
        in_specs=[SM, VM] + [ANY]*6, out_specs=[ANY]*8,
        out_shape=[sh((S,D),f32), sh((S,D),f32), sh((3,rq,D),bf16), sh((rq,D),bf16), sh((2,rq,FF),bf16), sh((nf,rd//nf,D),bf16), sh((S,D),f32), sh((D,S),bf16)],
        scratch_shapes=[b(3,*c8,rq,D), b(*c8,rq,D), b(2,*c8,rq,FF), b(nf,*c8,rd//nf,D), b(D,S), b(D,S), b(D,S), b(D,S),
                        w(HD//2,S), w(HD//2,S), b(S,128), w(8,S), w(16,S), w(16,S), w(8,D), w(n_dp,8,128),
                        w(S,D), w(S,D), w(S,D), w(4,128,S), b(D,S), b(S,D), b(3,2,S//MT,MT//2,FC), b(3,*c8,rq,D)]
            + bufs((2,), rq, FC, (nf,)) + bufs((2,), rd//nf, D, (nf//2,)) + bufs((), rq, D) + bufs((3,), rq, D)[1:]
            + [dma((ag,3)), dma((ag,5)), dma((n_dp-1,)), dma((n_dp-1,)), dma((rs,4)), dma((rs,5)), dma((rs,)), dma((26,))],
        compiler_params=pltpu.CompilerParams(collective_id=0, has_side_effects=True, vmem_limit_bytes=63*2**20),
        cost_estimate=pl.CostEstimate(flops=55*10**9, bytes_accessed=40*10**6, transcendentals=20*10**6),
        name="layer")(lens, gains, x, cot, qw, ow, gw, dw)

def can_fuse(n_dp, n_rep, S, D, FF, *rows):
    return n_dp == 8 and n_rep == 4 and S == 4*B and D % GW == 0 and FF == 4*FC and FC == n_dp*64 and sum(HEADS_IN) == H and all(r % 32 == 0 for r in rows)


def adam_body(sub, *refs):
    g_in, w_in, m_in, v_in, keep = refs[0:4], refs[4:9], refs[9:14], refs[14:19], refs[19:21]
    m_out, v_out, w_out, kept = refs[21:26], refs[26:31], refs[31:36], refs[36:38]
    bufs, acc_s, gg_s, load, store, pas, passed = refs[38:58], refs[58], refs[59], refs[60], refs[61], refs[62], refs[63:65]
    gs, ws, ms, vs = bufs[0:5], bufs[5:10], bufs[10:15], bufs[15:20]
    n_dp = w_in[2].shape[2]//(g_in[3].shape[0]*sub)
    nf = g_in[3].shape[0]
    todo = [(0, c) for c in range(3)] + [(1, None)] + [(2, c) for c in range(2)] + [(3, None), (4, None)]
    def at(ref, i): return ref if i is None else ref.at[i]
    loads = []
    for k, (a, i) in enumerate(todo):
        cs = []
        for j, (src, dst) in enumerate(((w_in, ws), (m_in, ms), (v_in, vs), (g_in, gs))):
            if j == 3 and a == 4: continue
            c = pltpu.make_async_copy(at(src[a], i), at(dst[a], i), load.at[k, j]); c.start(); cs.append(c)
        loads.append(cs)
    def halves(i, into):
        n = keep[i].shape[0]//2
        return [pltpu.make_async_copy(s.at[h*n:(h+1)*n], e.at[h*n:(h+1)*n], pas.at[into, i, h])
                for s, e in [((keep[i], passed[i]) if into == 0 else (passed[i], kept[i]))] for h in range(2)]
    for i in range(2):
        for c in halves(i, 0): c.start()
    stores = []
    for k, (a, i) in enumerate(todo):
        for c in loads[k]: c.wait()
        w = at(ws[a], i)[...]
        if a == 4:
            g = jnp.concatenate([acc_s[j].T[0:1, :] for j in range(2)], axis=0) / w.astype(bf16).astype(f32)
        elif a == 2:
            for o in range(n_dp):
                for f in range(0, nf, 2):
                    p = f*n_dp*sub + o*sub
                    q = p + n_dp*sub
                    gg_s[:, (o*nf + f)*sub:(o*nf + f + 2)*sub] = jnp.concatenate([gs[a][i, :, p:p+sub], gs[a][i, :, q:q+sub]], axis=1).astype(f32)
            g = gg_s[...]
        else:
            g = at(gs[a], i)[...].astype(f32).reshape(w.shape)
        if a in (0, 2):
            s = jnp.broadcast_to(jnp.sum(g*w.astype(bf16).astype(f32), axis=1, keepdims=True), (w.shape[0], 128))
            if i == 0: acc_s[a//2] = s
            else: acc_s[a//2] += s
        rate, decay = (gain_rate, 0.0) if a == 4 else (matrix_rate, weight_decay)
        new = adam_step(w, g, at(ms[a], i)[...], at(vs[a], i)[...], rate, decay)
        for j, (val, buf, out) in enumerate(zip(new, (ms, vs, ws), (m_out, v_out, w_out))):
            at(buf[a], i)[...] = val
            c = pltpu.make_async_copy(at(buf[a], i), at(out[a], i), store.at[k, j]); c.start(); stores.append(c)
        if k in (2, 4):
            i = (2, 4).index(k)
            for c, e in zip(halves(i, 0), halves(i, 1)):
                c.wait(); e.start()
    for c in stores + halves(0, 1) + halves(1, 1): c.wait()

def adam_all(grads, weights, moments, seconds, keep):
    q, o, g, d = grads
    rq = o.shape[0]
    sh = [jax.ShapeDtypeStruct(w.shape, f32) for w in weights]
    any_ = pl.BlockSpec(memory_space=pl.ANY)
    f = [pltpu.VMEM(w.shape, f32) for w in weights]
    dma = pltpu.SemaphoreType.DMA
    return pl.pallas_call(functools.partial(adam_body, d.shape[1]),
        in_specs=[any_]*21, out_specs=[any_]*17, out_shape=sh*3 + [jax.ShapeDtypeStruct(k.shape, k.dtype) for k in keep],
        scratch_shapes=[pltpu.VMEM(a.shape, bf16) for a in grads] + [pltpu.VMEM((8, 128), f32)] + f*3
            + [pltpu.VMEM((2, rq, 128), f32), pltpu.VMEM((rq, g.shape[2]), f32), dma((8, 4)), dma((8, 3)), dma((2, 2, 2))] + [pltpu.VMEM(k.shape, k.dtype) for k in keep],
        compiler_params=pltpu.CompilerParams(vmem_limit_bytes=63*2**20), name="adamw")(*grads, *weights, *moments, *seconds, *keep)

def adam_step(weight, grad_sum, moment, second, rate, decay):
    moment_new = beta_one * moment + (1.0 - beta_one) * grad_sum
    second_new = beta_two * second + (1.0 - beta_two) * grad_sum * grad_sum
    moment_hat = moment_new / (1.0 - beta_one**STEP)
    second_hat = second_new / (1.0 - beta_two**STEP)
    weight_new = weight - rate * (moment_hat / (jnp.sqrt(second_hat) + adam_eps) + decay * weight)
    return (moment_new, second_new, weight_new)


def per_device(tokens, seg_lens, cotangent, qkv_w, out_w, gu_w, down_w, gains,
               qkv_m, qkv_v, out_m, out_v, gu_m, gu_v, down_m, down_v, gain_m, gain_v):
    _, S, D = tokens.shape
    x = tokens.reshape(S, D)
    cot = cotangent.reshape(S, D)
    gain_low = gains.astype(bf16)
    n_dp, n_rep = lax.axis_size("dp"), lax.axis_size("rep")
    if can_fuse(n_dp, n_rep, S, D, gu_w.shape[2], qkv_w.shape[1], out_w.shape[0], gu_w.shape[1], down_w.shape[0]):
        output, input_grad, *grads = layer(n_dp, seg_lens, gains, x, cot, qkv_w, out_w, gu_w, down_w)[:6]
        new = adam_all(grads, (qkv_w, out_w, gu_w, down_w, gains), (qkv_m, out_m, gu_m, down_m, gain_m), (qkv_v, out_v, gu_v, down_v, gain_v),
                       (output, input_grad))
        states = tuple(new[5*k + a] for a in range(5) for k in range(3))
        return (new[15].reshape(tokens.shape), new[16].reshape(tokens.shape)) + states
    else:
        wqkv = lax.all_gather(qkv_w.astype(bf16), "dp", axis=1, tiled=True)
        gain_full = lax.all_gather(gain_low, "dp", axis=1, tiled=True).astype(f32)
        wo = lax.all_gather(out_w.astype(bf16), "dp", axis=0, tiled=True)
        wgu = lax.all_gather(gu_w.astype(bf16), "dp", axis=1, tiled=True)
        wd = lax.all_gather(down_w.astype(bf16), "dp", axis=0, tiled=True)
        freq = 10000.0 ** (-jnp.arange(HD // 2, dtype=f32) / (HD // 2))
        freq = jnp.broadcast_to(freq[:, None], (HD // 2, 128))
        gain8 = jnp.pad(gain_full, ((0, 6), (0, 0)))
        qT, kT, vT, oT, lse, cos, sin, segc, segr = attn_fwd(seg_lens, x, gain8, freq, wqkv)
        output, dmid, dob, dobT, dwo, dwgu, dwd = mlp(x, oT.T, oT, cot, wo, wgu, wd, gain8)
        input_grad, dwqkv = attn_bwd(x, gain8, wqkv, dmid, qT, kT, vT, dob, dobT, lse, cos, sin, segc, segr)

        def owned(grad, axis):
            part = lax.psum_scatter(grad, "dp", scatter_dimension=axis, tiled=True)
            return lax.psum(part.astype(f32), "rep")

        g_down = owned(dwd, 0)
        g_gu = owned(dwgu, 1)
        g_out = owned(dwo, 0)
        g_qkv = owned(dwqkv, 1)
    gain_f = gain_low.astype(f32)
    g_gain = jnp.stack([
        jnp.sum(g_qkv * qkv_w.astype(bf16).astype(f32), axis=(0, 2)) / gain_f[0],
        jnp.sum(g_gu * gu_w.astype(bf16).astype(f32), axis=(0, 2)) / gain_f[1],
    ])
    qkv_res = adam_step(qkv_w, g_qkv, qkv_m, qkv_v, matrix_rate, weight_decay)
    out_res = adam_step(out_w, g_out, out_m, out_v, matrix_rate, weight_decay)
    gu_res = adam_step(gu_w, g_gu, gu_m, gu_v, matrix_rate, weight_decay)
    down_res = adam_step(down_w, g_down, down_m, down_v, matrix_rate, weight_decay)
    gain_res = adam_step(gains, g_gain, gain_m, gain_v, gain_rate, 0.0)
    return (output.reshape(tokens.shape), input_grad.reshape(tokens.shape)) + qkv_res + out_res + gu_res + down_res + gain_res


def solution(mesh):
    rows, cols, vec = P(("dp", "rep"), None, None), P(None, "dp", None), P("dp", None)
    small = P(None, "dp")
    return jax.shard_map(
        per_device,
        mesh=mesh,
        in_specs=(rows, P(("dp", "rep"), None), rows, cols, vec, cols, vec, small,
                  cols, cols, vec, vec, cols, cols, vec, vec, small, small),
        out_specs=(rows, rows) + (cols,) * 3 + (vec,) * 3 + (cols,) * 3 + (vec,) * 3 + (small,) * 3,
        check_vma=False,
    )
```
